128 devices in a mesh: row: 8 (over z_hi, x), col: 16 (over z_lo, y, core).
Axes of the slice: x: 4, y: 4, z: 4 (z_hi: 2, z_lo: 2; z = z_hi * 2 + z_lo), core: 2. Of those that a mesh axis runs over, the one named last changes fastest.
Arguments:
- nodes: bfloat16 [262144, 512], P(('row', 'col')), may hold values from -6 to 6
- send_list: int32 [128, 4, 4], P(('row', 'col')), may hold values from 0 to 15
- adj_index: int32 [128, 16, 4], P(('row', 'col')), may hold values from 0 to 31, as said below
- adj_weight: bfloat16 [2048, 4, 128, 128], P(('row', 'col')), may hold values from -0.25 to 0.25
- dec_send: int32 [128, 2, 4], P(('row', 'col')), may hold values from 0 to 15
- dec_index: int32 [128, 16, 3], P(('row', 'col')), may hold values from 0 to 23, as said below
- dec_weight: bfloat16 [2048, 3, 128, 128], P(('row', 'col')), may hold values from -0.3125 to 0.3125
- hidden_mask: int32 [128, 16], P(('row', 'col')), may hold values from 0 to 1, as said below
- target: bfloat16 [262144, 227], P(('row', 'col')), may hold values from -6 to 6
- w_msg: bfloat16 [512, 512], replicated, may hold values from -0.25 to 0.25
- w_update: bfloat16 [512, 512], replicated, may hold values from -0.25 to 0.25
- w_aggregate: bfloat16 [512, 512], replicated, may hold values from -0.25 to 0.25
- w_output: bfloat16 [512, 512], replicated, may hold values from -0.25 to 0.25
- w_decode: bfloat16 [512, 512], replicated, may hold values from -0.25 to 0.25
- w_head: bfloat16 [512, 227], replicated, may hold values from -0.25 to 0.25
Outputs:
- latent_grad: float32 [262144, 512], P(('row', 'col'))
- msg_grad: float32 [512, 512], replicated
- update_grad: float32 [512, 512], replicated
- aggregate_grad: float32 [512, 512], replicated
- output_grad: float32 [512, 512], replicated
- decode_grad: float32 [512, 512], replicated
- head_grad: float32 [512, 227], replicated
The draws below stay inside these ranges and needn't reach their ends.
Inputs may be any that keep to these rules, and one draw needn't show every extreme that they name: `adj_index`: slot 0 of receiver tile t is t itself and slot 1 is the halo tile 16 + t mod (16). `dec_index`: slot 0 of grid block g reads the device's own tile g mod 16. `hidden_mask`: at most 12 blocks of one device are hidden, and some device has exactly 12.
All inputs are finite; a program needn't handle non-finite values.
Results may differ from the reference program's by a relative error of at most 0.02.
Values may be sent and summed in bfloat16 or wider, within the bound.
A program may use at most 192 MiB of HBM per device.

```python
import jax
import jax.numpy as jnp
from jax import lax

D = 512
OUTC = 227
TILE = 128
NT = 16
BT = 4
K = 4
KD = 3
DB = 4
GB = 16
MASKMAX = 12
NE = 32
NR = 24
NDEV = 128
NODES = 262144
GRID = 262144
N_ROW = 8
N_COL = 16


def draw_adj_index(key, part):
    key = jax.random.fold_in(key, 11)
    rows = jnp.arange(NT, dtype=jnp.int32)
    self_slot = jnp.broadcast_to(rows[None, :, None], (NDEV, NT, 1))
    halo_slot = jnp.broadcast_to((NT + rows % (4 * BT))[None, :, None], (NDEV, NT, 1))
    others = jax.random.randint(key, (NDEV, NT, K - 2), 0, NE, dtype=jnp.int32)
    return jnp.concatenate([self_slot, halo_slot, others], axis=2).astype(jnp.int32)


def draw_dec_index(key, part):
    key = jax.random.fold_in(key, 23)
    blocks = jnp.arange(GB, dtype=jnp.int32)
    first = jnp.broadcast_to((blocks % NT)[None, :, None], (NDEV, GB, 1))
    others = jax.random.randint(key, (NDEV, GB, KD - 1), 0, NR, dtype=jnp.int32)
    return jnp.concatenate([first, others], axis=2).astype(jnp.int32)


def draw_hidden_mask(key, part):
    key = jax.random.fold_in(key, 37)
    count_key, pick_key, perm_key = jax.random.split(key, 3)
    counts = jax.random.randint(count_key, (NDEV,), MASKMAX // 4, MASKMAX + 1, dtype=jnp.int32)
    busiest = jax.random.randint(pick_key, (), 0, NDEV, dtype=jnp.int32)
    counts = jnp.where(jnp.arange(NDEV, dtype=jnp.int32) == busiest, MASKMAX, counts)
    ranks = jax.vmap(lambda one: jax.random.permutation(one, GB))(jax.random.split(perm_key, NDEV)).astype(jnp.int32)
    return (ranks < counts[:, None]).astype(jnp.int32)


def set_ends(values, key, smallest, largest):
    shape = values.shape
    spot = [jax.random.randint(jax.random.fold_in(key, axis), (), 0, shape[axis]) for axis in range(len(shape))]
    values = values.at[tuple(spot)].set(smallest)
    longest = shape.index(max(shape))
    spot[longest] = (spot[longest] + 1) % shape[longest]
    return values.at[tuple(spot)].set(largest)


def block_scale(own_key, shape, pieces, least, largest):
    level, own = 1.0, jax.random.fold_in(own_key, 6)
    for dim, shards_of in pieces:
        heights = jnp.exp(jax.random.uniform(jax.random.fold_in(own, dim), (shards_of,), jnp.float32, least / len(pieces), largest / len(pieces)))
        level = level * jnp.repeat(heights, shape[dim] // shards_of).reshape([-1 if axis == dim else 1 for axis in range(len(shape))])
    return level


def bell_draw(key, shape, width, limit, shards=(), held_as=jnp.bfloat16):
    entries = width * jax.random.normal(key, shape, jnp.float32)
    if shards:
        entries = entries * block_scale(key, shape, shards, -0.22, 0.18)
    return jnp.clip(entries, -limit, limit).astype(held_as)


def setup_inputs(seed: int = 0) -> dict:
    key_list = jax.random.split(jax.random.key(seed), 16)
    return {
        "nodes": bell_draw(key_list[0], (NODES, D), 1.0, 6.0, ((0, 128),)),
        "send_list": set_ends(jax.random.randint(key_list[1], (NDEV, 4, BT), 0, NT), jax.random.fold_in(key_list[1], 1), 0, NT - 1).astype(jnp.int32),
        "adj_index": draw_adj_index(jax.random.fold_in(key_list[15], 71), 0),
        "adj_weight": bell_draw(key_list[3], (NDEV * NT, K, TILE, TILE), (K * TILE) ** -0.5, 0.25, ((0, 128),)),
        "dec_send": set_ends(jax.random.randint(key_list[4], (NDEV, 2, DB), 0, NT), jax.random.fold_in(key_list[4], 1), 0, NT - 1).astype(jnp.int32),
        "dec_index": draw_dec_index(jax.random.fold_in(key_list[15], 71), 0),
        "dec_weight": bell_draw(key_list[6], (NDEV * GB, KD, TILE, TILE), (KD * TILE) ** -0.5, 0.3125, ((0, 128),)),
        "hidden_mask": draw_hidden_mask(jax.random.fold_in(key_list[15], 71), 0),
        "target": bell_draw(key_list[8], (GRID, OUTC), 1.0, 6.0, ((0, 128),)),
        "w_msg": bell_draw(key_list[9], (D, D), D ** -0.5, 0.25),
        "w_update": bell_draw(key_list[10], (D, D), D ** -0.5, 0.25),
        "w_aggregate": bell_draw(key_list[11], (D, D), D ** -0.5, 0.25),
        "w_output": bell_draw(key_list[12], (D, D), D ** -0.5, 0.25),
        "w_decode": bell_draw(key_list[13], (D, D), D ** -0.5, 0.25),
        "w_head": bell_draw(key_list[14], (D, OUTC), D ** -0.5, 0.25),
    }


def silu_slope(pre):
    sig = jax.nn.sigmoid(pre)
    return sig * (1.0 + pre * (1.0 - sig))


def proc_forward(local, halo, weight, index, w_msg, w_update, w_aggregate, w_output):
    extended = jnp.concatenate([local, halo], axis=0)
    ext_rows = extended.reshape(-1, D)
    msg_pre = jnp.dot(ext_rows, w_msg, preferred_element_type=jnp.float32)
    messages = jax.nn.silu(msg_pre).astype(jnp.bfloat16).reshape(-1, TILE, D)
    picked = messages[index]
    aggregated = jnp.einsum("rkij,rkjd->rid", weight.astype(jnp.float32), picked.astype(jnp.float32)).astype(jnp.bfloat16)
    flat = local.reshape(-1, D)
    agg_rows = aggregated.reshape(-1, D)
    upd_pre = jnp.dot(flat, w_update, preferred_element_type=jnp.float32) + jnp.dot(agg_rows, w_aggregate, preferred_element_type=jnp.float32)
    hidden = jax.nn.silu(upd_pre).astype(jnp.bfloat16)
    updated = (flat.astype(jnp.float32) + jnp.dot(hidden, w_output, preferred_element_type=jnp.float32)).astype(jnp.bfloat16)
    return ext_rows, msg_pre, agg_rows, upd_pre, hidden, updated


def reference(nodes, send_list, adj_index, adj_weight, dec_send, dec_index, dec_weight, hidden_mask, target, w_msg, w_update, w_aggregate, w_output, w_decode, w_head):
    nrow = N_ROW
    ncol = N_COL
    blocks5 = nodes.reshape(nrow, ncol, NT, TILE, D)
    sends = send_list.reshape(nrow, ncol, 4, BT)
    outgoing = jax.vmap(jax.vmap(lambda tiles, chosen: tiles[chosen]))(blocks5, sends)
    zero_band = jnp.zeros_like(outgoing[:1, :, 0])
    north = jnp.concatenate([zero_band, outgoing[:-1, :, 0]], axis=0)
    south = jnp.concatenate([outgoing[1:, :, 1], zero_band], axis=0)
    west = jnp.roll(outgoing[:, :, 2], 1, axis=1)
    east = jnp.roll(outgoing[:, :, 3], -1, axis=1)
    halos = jnp.concatenate([north, south, west, east], axis=2).reshape(NDEV, 4 * BT, TILE, D)
    locals_all = nodes.reshape(NDEV, NT, TILE, D)
    weights_all = adj_weight.reshape(NDEV, NT, K, TILE, TILE)

    def forward_one(item):
        local, halo, weight, index = item
        return proc_forward(local, halo, weight, index, w_msg, w_update, w_aggregate, w_output)[5]

    updated = lax.map(forward_one, (locals_all, halos, weights_all, adj_index))
    upd5 = updated.reshape(nrow, ncol, NT, TILE, D)
    dsend = dec_send.reshape(nrow, ncol, 2, DB)
    sent_tiles = jax.vmap(jax.vmap(lambda tiles, chosen: tiles[chosen]))(upd5, dsend)
    from_west = jnp.roll(sent_tiles[:, :, 1], 1, axis=1)
    from_east = jnp.roll(sent_tiles[:, :, 0], -1, axis=1)
    received = jnp.concatenate([upd5, from_west, from_east], axis=2).reshape(NDEV, NR, TILE, D)
    dweights = dec_weight.reshape(NDEV, GB, KD, TILE, TILE)
    goals = target.reshape(NDEV, GB * TILE, OUTC)

    def decode_one(carry, item):
        rtiles, dweight, dindex, mask, goal = item
        gathered = rtiles[dindex]
        latent = jnp.einsum("gkij,gkjd->gid", dweight.astype(jnp.float32), gathered.astype(jnp.float32)).astype(jnp.bfloat16)
        lat_rows = latent.reshape(-1, D)
        dec_pre = jnp.dot(lat_rows, w_decode, preferred_element_type=jnp.float32)
        decoded = jax.nn.silu(dec_pre).astype(jnp.bfloat16)
        predict = jnp.dot(decoded, w_head, preferred_element_type=jnp.float32)
        rowmask = jnp.repeat(mask.astype(jnp.float32), TILE)[:, None]
        residual = (rowmask * (predict - goal.astype(jnp.float32))).astype(jnp.bfloat16)
        head_term = jnp.dot(decoded.T, residual, preferred_element_type=jnp.float32)
        dec_slope = (jnp.dot(residual, w_head.T, preferred_element_type=jnp.float32) * silu_slope(dec_pre)).astype(jnp.bfloat16)
        decode_term = jnp.dot(lat_rows.T, dec_slope, preferred_element_type=jnp.float32)
        lat_grad = jnp.dot(dec_slope, w_decode.T, preferred_element_type=jnp.float32).astype(jnp.bfloat16).reshape(GB, TILE, D)
        spread = jnp.einsum("gkij,gid->gkjd", dweight.astype(jnp.float32), lat_grad.astype(jnp.float32))
        tile_grad = jnp.zeros((NR, TILE, D), jnp.float32).at[dindex.reshape(-1)].add(spread.reshape(-1, TILE, D))
        return (carry[0] + decode_term, carry[1] + head_term), tile_grad.astype(jnp.bfloat16)

    dec_init = (jnp.zeros((D, D), jnp.float32), jnp.zeros((D, OUTC), jnp.float32))
    (decode_sum, head_sum), tile_grads = lax.scan(decode_one, dec_init, (received, dweights, dec_index, hidden_mask, goals))
    tg = tile_grads.reshape(nrow, ncol, NR, TILE, D)
    own_part = tg[:, :, :NT].reshape(NDEV, NT, TILE, D)
    grad_west = tg[:, :, NT:NT + DB]
    grad_east = tg[:, :, NT + DB:]
    back_first = jnp.roll(grad_east, 1, axis=1)
    back_second = jnp.roll(grad_west, -1, axis=1)
    returned = jnp.stack([back_first, back_second], axis=2).reshape(NDEV, 2 * DB, TILE, D)

    def collect(own, arrived, chosen):
        return own.astype(jnp.float32).at[chosen.reshape(-1)].add(arrived.astype(jnp.float32))

    update_grads = jax.vmap(collect)(own_part, returned, dec_send)

    def backward_one(carry, item):
        local, halo, weight, index, up_grad = item
        ext_rows, msg_pre, agg_rows, upd_pre, hidden, updated_rows = proc_forward(local, halo, weight, index, w_msg, w_update, w_aggregate, w_output)
        up_rows = up_grad.reshape(-1, D)
        up_half = up_rows.astype(jnp.bfloat16)
        upd_slope = (jnp.dot(up_half, w_output.T, preferred_element_type=jnp.float32) * silu_slope(upd_pre)).astype(jnp.bfloat16)
        output_term = jnp.dot(hidden.T, up_half, preferred_element_type=jnp.float32)
        update_term = jnp.dot(local.reshape(-1, D).T, upd_slope, preferred_element_type=jnp.float32)
        aggregate_term = jnp.dot(agg_rows.T, upd_slope, preferred_element_type=jnp.float32)
        own_grad = up_rows + jnp.dot(upd_slope, w_update.T, preferred_element_type=jnp.float32)
        agg_grad = jnp.dot(upd_slope, w_aggregate.T, preferred_element_type=jnp.float32).astype(jnp.bfloat16).reshape(NT, TILE, D)
        back_spread = jnp.einsum("rkij,rid->rkjd", weight.astype(jnp.float32), agg_grad.astype(jnp.float32))
        msg_grad = jnp.zeros((NE, TILE, D), jnp.float32).at[index.reshape(-1)].add(back_spread.reshape(-1, TILE, D))
        msg_slope = (msg_grad.reshape(-1, D) * silu_slope(msg_pre)).astype(jnp.bfloat16)
        msg_term = jnp.dot(ext_rows.T, msg_slope, preferred_element_type=jnp.float32)
        ext_grad = jnp.dot(msg_slope, w_msg.T, preferred_element_type=jnp.float32).reshape(NE, TILE, D)
        local_grad = own_grad.reshape(NT, TILE, D) + ext_grad[:NT]
        halo_grad = ext_grad[NT:].astype(jnp.bfloat16)
        sums = (carry[0] + msg_term, carry[1] + update_term, carry[2] + aggregate_term, carry[3] + output_term)
        return sums, (local_grad, halo_grad)

    square = jnp.zeros((D, D), jnp.float32)
    proc_sums, (local_grads, halo_grads) = lax.scan(backward_one, (square, square, square, square), (locals_all, halos, weights_all, adj_index, update_grads))
    hg = halo_grads.reshape(nrow, ncol, 4, BT, TILE, D)
    zero_back = jnp.zeros_like(hg[:1, :, 0])
    from_south = jnp.concatenate([hg[1:, :, 0], zero_back], axis=0)
    from_north = jnp.concatenate([zero_back, hg[:-1, :, 1]], axis=0)
    from_east_g = jnp.roll(hg[:, :, 2], -1, axis=1)
    from_west_g = jnp.roll(hg[:, :, 3], 1, axis=1)
    arrived = jnp.stack([from_south, from_north, from_east_g, from_west_g], axis=2).reshape(NDEV, 4 * BT, TILE, D)

    def add_back(grad, back, chosen):
        return grad.at[chosen.reshape(-1)].add(back.astype(jnp.float32))

    latent_grad = jax.vmap(add_back)(local_grads, arrived, send_list).reshape(NODES, D)
    scale = 1.0 / NDEV
    return (latent_grad, proc_sums[0] * scale, proc_sums[1] * scale, proc_sums[2] * scale, proc_sums[3] * scale, decode_sum * scale, head_sum * scale)
```

```python
import functools

import jax
import jax.numpy as jnp
from jax import lax
from jax.experimental import pallas as pl
from jax.experimental.pallas import tpu as pltpu
from jax.sharding import PartitionSpec as P

MESH = pl.DeviceIdType.MESH
F32 = jnp.float32
BF16 = jnp.bfloat16

D = 512
OUTC = 227
TILE = 128
NT = 16
NE = 32
NR = 24
K = 4
KD = 3
SLOTS = 12
DEC_EDGES = SLOTS * KD
ADJ_EDGES = NT * K
GROUP = 4
ROWS = GROUP * TILE
CORES = 2

JOBS = (
    (0, 768, ("z", "y", "x")),
    (768, 512, ("y", "x", "z")),
    (1280, 512, ("x", "z", "y")),
    (1792, 512, ("z", "x", "y")),
    (2304, 512, ("y", "z", "x")),
)
GRAD_ROWS = 2816
GRAD_F32 = 2304
HALF = D // 2
JOB_SEMS = 17


def axes_of(rows, cols):
    if (rows, cols) == (8, 16):
        return dict(zh=2, x=4, zl=2, y=4, n=4)
    return dict(zh=1, x=2, zl=2, y=2, n=2)


def dot(a, b):
    return lax.dot_general(a, b, (((1,), (0,)), ((), ())), preferred_element_type=F32)


def dot_nt(a, b):
    return lax.dot_general(a, b, (((1,), (1,)), ((), ())), preferred_element_type=F32)


def dot_tn(a, b):
    return lax.dot_general(a, b, (((0,), (0,)), ((), ())), preferred_element_type=F32)


def sigmoid(v):
    return 0.5 * jnp.tanh(0.5 * v) + 0.5


def rows_of(ref, start, count=GROUP):
    block = ref[pl.ds(start, count)]
    return block.reshape(count * TILE, block.shape[-1])


def put_rows(ref, start, value, count=GROUP):
    ref[pl.ds(start, count)] = value.reshape(count, TILE, value.shape[-1])


def sort_plan(values, blocks=None, per=1):
    count = len(values)
    depth = -(-count // 8) * 8
    down = lax.broadcasted_iota(jnp.int32, (depth, 128), 0)
    across = lax.broadcasted_iota(jnp.int32, (depth, 128), 1)
    mine = jnp.full((depth, 128), 1000, jnp.int32)
    other = jnp.full((depth, 128), 1000, jnp.int32)
    for q, value in enumerate(values):
        mine = jnp.where(down == q, value, mine)
        other = jnp.where(across == q, value, other)
    same_before = jnp.where((other == mine) & (across < down), 1, 0)
    before = jnp.where(other < mine, 1, 0) + same_before
    rank = jnp.sum(before, axis=1, keepdims=True)
    continues = jnp.minimum(jnp.sum(same_before, axis=1, keepdims=True), 1)
    hit = jnp.where((rank == across) & (down < count), 1, 0)
    order = jnp.sum(hit * down, axis=0, keepdims=True)
    follows = jnp.sum(hit * continues, axis=0, keepdims=True)
    upto = jnp.sum(jnp.where(mine <= across, 1, 0), axis=0, keepdims=True)
    present = jnp.minimum(jnp.sum(jnp.where(mine == across, 1, 0), axis=0, keepdims=True), 1)
    group = {1: down, 3: (down * 43) >> 7, 4: down >> 2}[per]
    group_row = jnp.sum(hit * group, axis=0, keepdims=True)
    named = down
    if blocks is not None:
        for q, value in enumerate(blocks):
            named = jnp.where(down == q, value, named)
    named_row = jnp.sum(hit * named, axis=0, keepdims=True)
    return order, follows, jnp.maximum(upto - 1, 0), present, group_row, named_row


def kernel(
    sizes,
    send_ref, adj_ref, dsend_ref, didx_ref, mask_ref,
    nodes_hbm, adjw_hbm, decw_hbm, target_hbm,
    wm_hbm, wu_hbm, wa_hbm, wo_hbm, wd_hbm, wh_hbm,
    part_hbm, back_hbm, grads_hbm,
    nv, halo, adjw, decw, target, wm, wu, wa, wo, wd, wh,
    pref, msl, g2f, agg, hid, usl, redge, rgin, err, pool0, pool1, mbuf, pool4, acc,
    gbuf, cs, cr, r1, s2, r2, x4,
    plan_v, plan,
    in_sems, plan_sem, out_sem, halo_s, halo_r, edge_s, edge_r, rg_s, rg_r, hg_s, hg_r, job_s, job_r, job_l,
):
    nrow, ncol, nx, ny, nzl = sizes["rows"], sizes["cols"], sizes["x"], sizes["y"], sizes["zl"]
    nzh, n = sizes["zh"], sizes["n"]
    r = lax.axis_index("row")
    c = lax.axis_index("col")
    zh, x = lax.div(r, nx), lax.rem(r, nx)
    zl = lax.div(c, ny * CORES)
    y = lax.rem(lax.div(c, CORES), ny)
    core = lax.rem(c, CORES)
    z = zh * nzl + zl
    place = {"x": x, "y": y, "z": z}

    def peer(axis, step):
        there = lax.rem(place[axis] + step, n)
        if axis == "x":
            return (zh * nx + there, c), there
        if axis == "y":
            return (r, (zl * ny + there) * CORES + core), there
        return (lax.div(there, nzl) * nx + x, (lax.rem(there, nzl) * ny + y) * CORES + core), there

    mate = (r, c + 1 - 2 * core)
    west = (r, lax.rem(c + ncol - 1, ncol))
    east = (r, lax.rem(c + 1, ncol))
    north = (r - 1, c)
    south = (r + 1, c)
    has_north = r > 0
    has_south = r < nrow - 1

    loads = [
        pltpu.make_async_copy(src, dst, in_sems.at[i])
        for i, (src, dst) in enumerate(
            (
                (nodes_hbm, nv), (wm_hbm, wm), (wu_hbm, wu), (adjw_hbm, adjw), (wa_hbm, wa), (wo_hbm, wo),
                (decw_hbm, decw), (wd_hbm, wd), (wh_hbm, wh),
                *((target_hbm.at[:, pl.ds(g * TILE, TILE)], target.at[g]) for g in range(NT)),
            )
        )
    ]
    for load in loads:
        load.start()

    barrier = pltpu.get_barrier_semaphore()

    def greet(device):
        pl.semaphore_signal(barrier, inc=1, device_id=device, device_id_type=MESH)

    greeted = 2
    greet(west)
    greet(east)
    for axis in ("x", "y", "z"):
        for step in range(1, n):
            greet(peer(axis, step)[0])
            greeted += 1

    @pl.when(has_north)
    def _():
        greet(north)

    @pl.when(has_south)
    def _():
        greet(south)

    def send(src, dst, ssem, rsem, device):
        return pltpu.make_async_remote_copy(
            src_ref=src, dst_ref=dst, send_sem=ssem, recv_sem=rsem, device_id=device, device_id_type=MESH
        )

    loads[0].wait()
    for d in range(4):
        for b in range(4):
            pool1[d * 4 + b] = nv[send_ref[0, d, b]]
    pl.semaphore_wait(barrier, greeted + jnp.where(has_north, 1, 0) + jnp.where(has_south, 1, 0))

    halo_to = (south, north, east, west)
    halo_has = (has_south, has_north, None, None)
    from_has = (has_north, has_south, None, None)

    def when(condition, body):
        if condition is None:
            body()
        else:
            pl.when(condition)(body)

    def halo_copy(d):
        part = pl.ds(d * 4, 4)
        return send(pool1.at[part], halo.at[part], halo_s.at[d], halo_r.at[d], halo_to[d])

    for d in range(4):
        when(halo_has[d], lambda d=d: halo_copy(d).start())

    def messages(xs, at):
        pre = dot(xs, wm[...])
        s = sigmoid(pre)
        put_rows(pref, NE + at, (pre * s).astype(BF16))
        put_rows(msl, at, (s * (1.0 + pre * (1.0 - s))).astype(BF16))

    loads[1].wait()
    loads[2].wait()

    @pl.loop(0, NT // GROUP)
    def _(g):
        xs = rows_of(nv, g * GROUP)
        messages(xs, g * GROUP)
        put_rows(g2f, g * GROUP, dot(xs, wu[...]))

    def write_plan(at, rows):
        for i, row in enumerate(rows):
            plan_v[at + i : at + i + 1, :] = row

    write_plan(0, sort_plan([adj_ref[0, k, t] for t in range(NT) for k in range(K)], per=K))
    write_plan(6, sort_plan([dsend_ref[0, d, s] for d in range(2) for s in range(4)])[:4])
    write_plan(10, sort_plan([1 - mask_ref[0, g] for g in range(NT)])[:1])
    first = pltpu.make_async_copy(plan_v.at[pl.ds(0, 16)], plan.at[pl.ds(0, 16)], plan_sem.at[0])
    first.start()
    first.wait()
    hidden = [plan[10, s] for s in range(SLOTS)]
    edge_list = [(hidden[s], k) for s in range(SLOTS) for k in range(KD)]
    write_plan(16, sort_plan([didx_ref[k, 0, g] for g, k in edge_list], [g * KD + k for g, k in edge_list], KD))
    second = pltpu.make_async_copy(plan_v.at[pl.ds(16, 8)], plan.at[pl.ds(16, 8)], plan_sem.at[1])
    second.start()
    second.wait()

    for d in (3, 2, 0, 1):
        when(from_has[d], lambda d=d: halo_copy(d).wait_recv())
        if from_has[d] is not None:

            @pl.when(jnp.logical_not(from_has[d]))
            def _(d=d):
                halo[pl.ds(d * 4, 4)] = jnp.zeros((4, TILE, D), BF16)

        messages(rows_of(halo, d * 4), NT + d * 4)

    for i in (3, 4, 5):
        loads[i].wait()

    @pl.loop(0, NT // GROUP)
    def _(g):
        for i in range(GROUP):
            t = g * GROUP + i
            weights = jnp.concatenate([adjw[t * K + k] for k in range(K)], axis=1)
            picked = jnp.concatenate(
                [pref[NE + t], pref[NE + NT + t], pref[NE + adj_ref[0, 2, t]], pref[NE + adj_ref[0, 3, t]]], axis=0
            )
            agg[t] = dot(weights, picked).astype(BF16)
        upre = rows_of(g2f, g * GROUP) + dot(rows_of(agg, g * GROUP), wa[...])
        s = sigmoid(upre)
        hidden_rows = (upre * s).astype(BF16)
        put_rows(hid, g * GROUP, hidden_rows)
        put_rows(usl, g * GROUP, (s * (1.0 + upre * (1.0 - s))).astype(BF16))
        v2 = rows_of(nv, g * GROUP).astype(F32) + dot(hidden_rows, wo[...])
        put_rows(pref, g * GROUP, v2.astype(BF16))

    for d in range(4):
        when(halo_has[d], lambda d=d: halo_copy(d).wait_send())
    for d in range(2):
        for s in range(4):
            pref[NE + d * 4 + s] = pref[dsend_ref[0, d, s]]
    edges = [
        send(pref.at[pl.ds(NE, 4)], redge.at[pl.ds(4, 4)], edge_s.at[0], edge_r.at[0], west),
        send(pref.at[pl.ds(NE + 4, 4)], redge.at[pl.ds(0, 4)], edge_s.at[1], edge_r.at[1], east),
    ]
    for edge in edges:
        edge.start()
    for load in loads[6:]:
        load.wait()
    for edge in edges:
        edge.wait()
    for e in range(8):
        pref[NT + e] = redge[e]

    @pl.loop(0, SLOTS // GROUP)
    def _(g):
        goals, marks = [], []
        for i in range(GROUP):
            s = g * GROUP + i
            block = plan[10, s]
            weights = jnp.concatenate([decw[block * KD + k] for k in range(KD)], axis=1)
            picked = jnp.concatenate([pref[didx_ref[k, 0, block]] for k in range(KD)], axis=0)
            pool0[s] = dot(weights, picked).astype(BF16)
            goals.append(target[block].astype(F32))
            marks.append(jnp.full((1, TILE), mask_ref[0, block].astype(F32), F32))
        dpre = dot(rows_of(pool0, g * GROUP), wd[...])
        s = sigmoid(dpre)
        q = (dpre * s).astype(BF16)
        put_rows(pool1, g * GROUP, q)
        slope = s * (1.0 + dpre * (1.0 - s))
        residual = dot_nt(wh[...], q) - jnp.concatenate(goals, axis=1)
        residual = (jnp.concatenate(marks, axis=1) * residual).astype(BF16)
        err[:, pl.ds(pl.multiple_of(g * ROWS, ROWS), ROWS)] = residual
        dslope = (dot_tn(residual, wh[...]) * slope).astype(BF16)
        put_rows(mbuf, g * GROUP, dslope)
        put_rows(pool4, g * GROUP, dot_nt(dslope, wd[...]).astype(BF16))

    def spread(at, edges, weight, source):
        acc[...] = jnp.zeros((TILE, D), F32)

        @pl.loop(0, edges // GROUP)
        def _(h):
            total = acc[...]
            for i in range(GROUP):
                p = h * GROUP + i
                total = dot_tn(weight[plan[at + 5, p]], source[plan[at + 4, p]]) + plan[at + 1, p].astype(F32) * total
                pref[p] = total.astype(BF16)
            acc[...] = total

    def spread_of(at, tile):
        return plan[at + 3, tile].astype(F32) * pref[plan[at + 2, tile]].astype(F32)

    spread(16, DEC_EDGES, decw, pool4)
    for e in range(8):
        pref[48 + e] = spread_of(16, NT + e).astype(BF16)
    returns = [
        send(pref.at[pl.ds(48, 4)], rgin.at[pl.ds(4, 4)], rg_s.at[0], rg_r.at[0], west),
        send(pref.at[pl.ds(52, 4)], rgin.at[pl.ds(0, 4)], rg_s.at[1], rg_r.at[1], east),
    ]
    for item in returns:
        item.start()

    def job_copy(j, sem, src, dst, device):
        return send(src, dst, job_s.at[j, sem], job_r.at[j, sem], device)

    def c_copy(j):
        at, rows, _ = JOBS[j]
        return job_copy(j, 0, cs.at[pl.ds(at, rows)], cr.at[pl.ds(at, rows)], mate)

    def first_copies(j):
        at, rows, order = JOBS[j]
        quarter = rows // n
        out = []
        for step in range(1, n):
            device, there = peer(order[0], step)
            src = cs.at[pl.ds(pl.multiple_of(at + there * quarter, 16), quarter)]
            out.append(job_copy(j, step, src, r1.at[step - 1, pl.ds(at // n, quarter)], device))
        return out

    def second_copies(j):
        at, rows, order = JOBS[j]
        small = rows // (n * n)
        out = []
        for step in range(1, n):
            device, there = peer(order[1], step)
            src = s2.at[pl.ds(pl.multiple_of(at // n + there * small, 16), small)]
            out.append(job_copy(j, 3 + step, src, r2.at[step - 1, pl.ds(at // (n * n), small)], device))
        return out

    def third_copies(j):
        at, rows, order = JOBS[j]
        small = rows // (n * n)
        out = []
        for step in range(1, n):
            device, _ = peer(order[2], step)
            mine = x4.at[place[order[2]], pl.ds(at // (n * n), small)]
            out.append(job_copy(j, 6 + step, mine, mine, device))
        return out

    def small_at(j):
        at, rows, order = JOBS[j]
        quarter, small = rows // n, rows // (n * n)
        return pl.multiple_of(at + place[order[0]] * quarter + place[order[1]] * small, 16)

    def back_small(j):
        at, rows, order = JOBS[j]
        part = cr.at[pl.ds(small_at(j), rows // (n * n))]
        return [
            job_copy(j, 9 + step, part, part, peer(order[1], step)[0]) for step in range(1, n)
        ]

    def back_quarter(j):
        at, rows, order = JOBS[j]
        quarter = rows // n
        part = cr.at[pl.ds(pl.multiple_of(at + place[order[0]] * quarter, 16), quarter)]
        return [
            job_copy(j, 12 + step, part, part, peer(order[0], step)[0]) for step in range(1, n)
        ]

    def back_core(j):
        at, rows, _ = JOBS[j]
        part = pl.ds(at, rows)
        return (
            job_copy(j, 16, cr.at[part], grads_hbm.at[core, part], mate),
            pltpu.make_async_copy(cr.at[part], grads_hbm.at[core, part], job_l.at[j]),
        )

    def job_stage(j, stage_number):
        at, rows, order = JOBS[j]
        quarter, small = rows // n, rows // (n * n)
        whole = pl.ds(at, rows)
        own = pl.ds(at % GRAD_F32, rows)
        if stage_number == 0:
            low, high = gbuf[own, :HALF], gbuf[own, HALF:]
            cs[whole] = jnp.where(core == 0, high, low).astype(BF16)
            c_copy(j).start()
        elif stage_number == 1:
            c_copy(j).wait()
            low, high = gbuf[own, :HALF], gbuf[own, HALF:]
            cs[whole] = (jnp.where(core == 0, low, high) + cr[whole].astype(F32)).astype(BF16)
            for item in first_copies(j):
                item.start()
        elif stage_number == 2:
            mine = pl.ds(pl.multiple_of(at + place[order[0]] * quarter, 16), quarter)
            for item in first_copies(j):
                item.wait()
            total = cs[mine].astype(F32)
            for step in range(n - 1):
                total = total + r1[step, pl.ds(at // n, quarter)].astype(F32)
            s2[pl.ds(at // n, quarter)] = total.astype(BF16)
            for item in second_copies(j):
                item.start()
        elif stage_number == 3:
            mine = pl.ds(pl.multiple_of(at // n + place[order[1]] * small, 16), small)
            for item in second_copies(j):
                item.wait()
            total = s2[mine].astype(F32)
            for step in range(n - 1):
                total = total + r2[step, pl.ds(at // (n * n), small)].astype(F32)
            x4[place[order[2]], pl.ds(at // (n * n), small)] = total.astype(BF16)
            for item in third_copies(j):
                item.start()
        elif stage_number == 4:
            for item in third_copies(j):
                item.wait()
            total = x4[0, pl.ds(at // (n * n), small)].astype(F32)
            for other in range(1, n):
                total = total + x4[other, pl.ds(at // (n * n), small)].astype(F32)
            cr[pl.ds(small_at(j), small)] = (total * (1.0 / (nrow * ncol))).astype(BF16)
            for item in back_small(j):
                item.start()
        elif stage_number == 5:
            for item in back_small(j):
                item.wait()
            for item in back_quarter(j):
                item.start()
        elif stage_number == 6:
            for item in back_quarter(j):
                item.wait()
            for item in back_core(j):
                item.start()
        else:
            for item in back_core(j):
                item.wait()

    def gradient(at, left, right):
        for n in range(2):
            lanes = slice(n * HALF, (n + 1) * HALF)
            total = None
            for (lref, lat, count), (rref, rat) in zip(left, right):
                lhs = lref[pl.ds(lat, count)].reshape(count * TILE, D)
                rhs = rref[pl.ds(rat, count), :, lanes].reshape(count * TILE, HALF)
                term = dot_tn(lhs, rhs)
                total = term if total is None else total + term
            gbuf[pl.ds(at % GRAD_F32, D), lanes] = total

    gradient(0, [(pool0, 0, SLOTS)], [(mbuf, 0)])
    q_rows = pool1[pl.ds(0, SLOTS)].reshape(SLOTS * TILE, D)
    gbuf[512:768, :] = jnp.zeros((256, D), F32)
    gbuf[512 : 512 + OUTC, :] = dot(err[...], q_rows)
    job_stage(0, 0)

    for item in returns:
        item.wait()
    total = None
    for p in range(8):
        arrived = rgin[plan[6, p]].astype(F32)
        total = arrived if total is None else arrived + plan[7, p].astype(F32) * total
        pref[40 + p] = total.astype(BF16)

    @pl.loop(0, NT)
    def _(t):
        value = spread_of(16, t).astype(BF16).astype(F32)
        value = value + plan[9, t].astype(F32) * pref[40 + plan[8, t]].astype(F32)
        g2f[t] = value
        pool4[t] = value.astype(BF16)

    job_stage(0, 1)

    @pl.loop(0, NT // GROUP)
    def _(g):
        back = dot_nt(rows_of(pool4, g * GROUP), wo[...]) * rows_of(usl, g * GROUP).astype(F32)
        slope = back.astype(BF16)
        put_rows(pool0, g * GROUP, slope)
        put_rows(g2f, g * GROUP, rows_of(g2f, g * GROUP) + dot_nt(slope, wu[...]))
        put_rows(pool1, g * GROUP, dot_nt(slope, wa[...]).astype(BF16))

    job_stage(0, 2)
    spread(0, ADJ_EDGES, adjw, pool1)
    job_stage(0, 3)

    def message_slope(e):
        mbuf[e] = (spread_of(0, e) * msl[e].astype(F32)).astype(BF16)

    back_to = (north, south, west, east)
    back_has = (has_north, has_south, None, None)
    back_from = (has_south, has_north, None, None)

    def back_copy(d):
        part = pl.ds(d * 4, 4)
        return send(pool1.at[part], back_hbm.at[part], hg_s.at[d], hg_r.at[d], back_to[d])

    for d in range(4):

        @pl.loop(0, 4)
        def _(b, d=d):
            message_slope(NT + d * 4 + b)

        put_rows(pool1, d * 4, dot_nt(rows_of(mbuf, NT + d * 4), wm[...]).astype(BF16))
        when(back_has[d], lambda d=d: back_copy(d).start())

    job_stage(0, 4)

    @pl.loop(0, NT)
    def _(e):
        message_slope(e)

    gradient(768, [(hid, 0, NT)], [(pool4, 0)])
    job_stage(1, 0)
    gradient(1280, [(nv, 0, NT)], [(pool0, 0)])
    job_stage(2, 0)
    job_stage(1, 1)
    job_stage(0, 5)
    gradient(1792, [(agg, 0, NT)], [(pool0, 0)])
    job_stage(3, 0)
    job_stage(2, 1)
    gradient(2304, [(nv, 0, NT), (halo, 0, NT)], [(mbuf, 0), (mbuf, NT)])
    job_stage(4, 0)
    job_stage(3, 1)
    job_stage(1, 2)
    job_stage(0, 6)

    @pl.loop(0, NT // GROUP)
    def _(g):
        put_rows(g2f, g * GROUP, rows_of(g2f, g * GROUP) + dot_nt(rows_of(mbuf, g * GROUP), wm[...]))

    part_out = pltpu.make_async_copy(g2f, part_hbm, out_sem.at[0])
    part_out.start()
    job_stage(4, 1)
    for step in range(2, 8):
        if step < 7:
            job_stage(1, step + 1)
        for j in (2, 3, 4):
            job_stage(j, step)
    job_stage(0, 7)
    part_out.wait()
    for d in range(4):
        when(back_has[d], lambda d=d: back_copy(d).wait_send())
        when(back_from[d], lambda d=d: back_copy(d).wait_recv())


def finish(sizes, send_ref, part_ref, back_ref, m_ref, u_ref, a_ref, o_ref, d_ref, h_ref,
           latent_ref, msg_ref, upd_ref, agg_ref, out_ref, dec_ref, head_ref):
    r = lax.axis_index("row")
    step = pl.program_id(0)
    per = part_ref.shape[0]
    for i in range(per):
        latent_ref[i] = part_ref[i]
    for d in range(4):
        there = (r < sizes["rows"] - 1, r > 0, None, None)[d]
        for b in range(4):
            local = send_ref[0, d, b] - step * per
            hit = (local >= 0) & (local < per)
            if there is not None:
                hit = hit & there

            @pl.when(hit)
            def _(local=local, a=d * 4 + b):
                latent_ref[local] = latent_ref[local] + back_ref[a].astype(F32)

    for src, dst in ((m_ref, msg_ref), (u_ref, upd_ref), (a_ref, agg_ref), (o_ref, out_ref), (d_ref, dec_ref), (h_ref, head_ref)):
        dst[:, :HALF] = src[0].astype(F32)
        dst[:, HALF:] = src[1].astype(F32)


def on_device(
    sizes, nodes, send_list, adj_index, adj_weight, dec_send, dec_index, dec_weight, hidden_mask, target,
    w_msg, w_update, w_aggregate, w_output, w_decode, w_head,
):
    n = sizes["n"]
    tiles = lambda count, dtype=BF16: pltpu.VMEM((count, TILE, D), dtype)
    any_spec = pl.BlockSpec(memory_space=pl.ANY)
    smem = pl.BlockSpec(memory_space=pltpu.SMEM)
    scratch = [
        tiles(NT), tiles(NT),
        pltpu.VMEM((NT * K, TILE, TILE), BF16), pltpu.VMEM((NT * KD, TILE, TILE), BF16),
        pltpu.VMEM((NT, OUTC, TILE), BF16),
        *[pltpu.VMEM((D, D), BF16)] * 5, pltpu.VMEM((OUTC, D), BF16),
        tiles(2 * NE), tiles(NE), tiles(NT, F32),
        tiles(NT), tiles(NT), tiles(NT),
        tiles(8), tiles(8), pltpu.VMEM((OUTC, SLOTS * TILE), BF16),
        tiles(NT), tiles(NT), tiles(NE), tiles(NT),
        pltpu.VMEM((TILE, D), F32),
        pltpu.VMEM((GRAD_F32, D), F32),
        pltpu.VMEM((GRAD_ROWS, HALF), BF16), pltpu.VMEM((GRAD_ROWS, HALF), BF16),
        pltpu.VMEM((n - 1, GRAD_ROWS // n, HALF), BF16), pltpu.VMEM((GRAD_ROWS // n, HALF), BF16),
        pltpu.VMEM((n - 1, GRAD_ROWS // n**2, HALF), BF16), pltpu.VMEM((n, GRAD_ROWS // n**2, HALF), BF16),
        pltpu.VMEM((24, 128), jnp.int32), pltpu.SMEM((24, 128), jnp.int32),
        pltpu.SemaphoreType.DMA((9 + NT,)), pltpu.SemaphoreType.DMA((2,)), pltpu.SemaphoreType.DMA((1,)),
        *[pltpu.SemaphoreType.DMA((4,))] * 2,
        *[pltpu.SemaphoreType.DMA((2,))] * 4,
        *[pltpu.SemaphoreType.DMA((4,))] * 2,
        *[pltpu.SemaphoreType.DMA((len(JOBS), JOB_SEMS))] * 2,
        pltpu.SemaphoreType.DMA((len(JOBS),)),
    ]
    part, back, grads = pl.pallas_call(
        functools.partial(kernel, sizes),
        out_shape=(
            jax.ShapeDtypeStruct((NT, TILE, D), F32),
            jax.ShapeDtypeStruct((NT, TILE, D), BF16),
            jax.ShapeDtypeStruct((CORES, GRAD_ROWS, HALF), BF16),
        ),
        in_specs=[smem] * 5 + [any_spec] * 10,
        out_specs=(any_spec,) * 3,
        scratch_shapes=scratch,
        compiler_params=pltpu.CompilerParams(
            collective_id=0, has_side_effects=True, vmem_limit_bytes=62 * 1024 * 1024
        ),
        name="mesh_step",
    )(
        send_list, adj_index.transpose(0, 2, 1), dec_send, dec_index.transpose(2, 0, 1), hidden_mask,
        nodes.reshape(NT, TILE, D),
        adj_weight.reshape(NT * K, TILE, TILE),
        dec_weight.reshape(NT * KD, TILE, TILE),
        target.T,
        w_msg, w_update, w_aggregate, w_output, w_decode, w_head.T,
    )
    steps = 8
    block = D // steps

    def rows_spec(at, size=block):
        return pl.BlockSpec((CORES, size, HALF), lambda i, s: (0, at // size + i, 0))

    square = pl.BlockSpec((block, D), lambda i, s: (i, 0))
    f32 = lambda *shape: jax.ShapeDtypeStruct(shape, F32)
    outs = pl.pallas_call(
        functools.partial(finish, sizes),
        out_shape=(f32(NT, TILE, D), *[f32(D, D)] * 5, f32(OUTC, D)),
        grid_spec=pltpu.PrefetchScalarGridSpec(
            num_scalar_prefetch=1,
            grid=(steps,),
            in_specs=[
                pl.BlockSpec((NT // steps, TILE, D), lambda i, s: (i, 0, 0)),
                pl.BlockSpec((NT, TILE, D), lambda i, s: (0, 0, 0)),
                rows_spec(2304), rows_spec(1280), rows_spec(1792), rows_spec(768), rows_spec(0),
                rows_spec(512, HALF // steps),
            ],
            out_specs=(
                pl.BlockSpec((NT // steps, TILE, D), lambda i, s: (i, 0, 0)),
                *[square] * 5,
                pl.BlockSpec((HALF // steps, D), lambda i, s: (i, 0)),
            ),
        ),
        compiler_params=pltpu.CompilerParams(vmem_limit_bytes=60 * 1024 * 1024),
        name="finish",
    )(send_list, part, back, grads, grads, grads, grads, grads, grads)
    latent, msg, upd, agg, out, dec, head = outs
    return latent.reshape(NT * TILE, D), msg, upd, agg, out, dec, head.T


def solution(mesh):
    rows, cols = mesh.shape["row"], mesh.shape["col"]
    sizes = dict(axes_of(rows, cols), rows=rows, cols=cols)
    both = ("row", "col")
    return jax.shard_map(
        functools.partial(on_device, sizes),
        mesh=mesh,
        in_specs=(
            P(both, None),
            P(both, None, None),
            P(both, None, None),
            P(both, None, None, None),
            P(both, None, None),
            P(both, None, None),
            P(both, None, None, None),
            P(both, None),
            P(both, None),
            *[P()] * 6,
        ),
        out_specs=(P(both, None), *[P()] * 6),
        check_vma=False,
    )
```

```python
import functools

import jax
import jax.numpy as jnp
from jax import lax
from jax.experimental import pallas as pl
from jax.experimental.pallas import tpu as pltpu
from jax.sharding import PartitionSpec as P

MESH = pl.DeviceIdType.MESH
F32 = jnp.float32
BF16 = jnp.bfloat16

D = 512
OUTC = 227
TILE = 128
NT = 16
NE = 32
NR = 24
K = 4
KD = 3
SLOTS = 12
DEC_EDGES = SLOTS * KD
ADJ_EDGES = NT * K
GROUP = 4
ROWS = GROUP * TILE
CORES = 2

JOBS = (
    (0, 768, ("z", "y", "x")),
    (768, 512, ("y", "x", "z")),
    (1280, 512, ("x", "z", "y")),
    (1792, 512, ("z", "x", "y")),
    (2304, 256, ("y", "z", "x")),
    (2560, 256, ("z", "y", "x")),
)
GRAD_ROWS = 2816
GRAD_F32 = 2304
HALF = D // 2
JOB_SEMS = 17


def axes_of(rows, cols):
    if (rows, cols) == (8, 16):
        return dict(zh=2, x=4, zl=2, y=4, n=4)
    return dict(zh=1, x=2, zl=2, y=2, n=2)


def dot(a, b):
    return lax.dot_general(a, b, (((1,), (0,)), ((), ())), preferred_element_type=F32)


def dot_nt(a, b):
    return lax.dot_general(a, b, (((1,), (1,)), ((), ())), preferred_element_type=F32)


def dot_tn(a, b):
    return lax.dot_general(a, b, (((0,), (0,)), ((), ())), preferred_element_type=F32)


def sigmoid(v):
    return 0.5 * jnp.tanh(0.5 * v) + 0.5


def rows_of(ref, start, count=GROUP):
    block = ref[pl.ds(start, count)]
    return block.reshape(count * TILE, block.shape[-1])


def put_rows(ref, start, value, count=GROUP):
    ref[pl.ds(start, count)] = value.reshape(count, TILE, value.shape[-1])


def sort_plan(values, blocks=None, per=1):
    count = len(values)
    depth = -(-count // 8) * 8
    down = lax.broadcasted_iota(jnp.int32, (depth, 128), 0)
    across = lax.broadcasted_iota(jnp.int32, (depth, 128), 1)
    mine = jnp.full((depth, 128), 1000, jnp.int32)
    other = jnp.full((depth, 128), 1000, jnp.int32)
    for q, value in enumerate(values):
        mine = jnp.where(down == q, value, mine)
        other = jnp.where(across == q, value, other)
    same_before = jnp.where((other == mine) & (across < down), 1, 0)
    before = jnp.where(other < mine, 1, 0) + same_before
    rank = jnp.sum(before, axis=1, keepdims=True)
    continues = jnp.minimum(jnp.sum(same_before, axis=1, keepdims=True), 1)
    hit = jnp.where((rank == across) & (down < count), 1, 0)
    order = jnp.sum(hit * down, axis=0, keepdims=True)
    follows = jnp.sum(hit * continues, axis=0, keepdims=True)
    upto = jnp.sum(jnp.where(mine <= across, 1, 0), axis=0, keepdims=True)
    present = jnp.minimum(jnp.sum(jnp.where(mine == across, 1, 0), axis=0, keepdims=True), 1)
    group = {1: down, 3: (down * 43) >> 7, 4: down >> 2}[per]
    group_row = jnp.sum(hit * group, axis=0, keepdims=True)
    named = down
    if blocks is not None:
        for q, value in enumerate(blocks):
            named = jnp.where(down == q, value, named)
    named_row = jnp.sum(hit * named, axis=0, keepdims=True)
    return order, follows, jnp.maximum(upto - 1, 0), present, group_row, named_row


def kernel(
    sizes,
    send_ref, adj_ref, dsend_ref, didx_ref, mask_ref,
    nodes_hbm, adjw_hbm, decw_hbm, target_hbm,
    wm_hbm, wu_hbm, wa_hbm, wo_hbm, wd_hbm, wh_hbm,
    lat_hbm, grads_hbm,
    nv, halo, adjw, decw, target, wm, wu, wa, wo, wd, wh,
    pref, msl, g2f, agg, hid, usl, redge, rgin, err, pool0, pool1, mbuf, pool4, acc,
    gbuf, cs, cr, r1, s2, r2, x4,
    rel, backns, plan_v, plan,
    in_sems, plan_sem, out_sem, halo_s, halo_r, edge_s, edge_r, rg_s, rg_r, hg_s, hg_r, job_s, job_r, job_l,
    hop_s, hop_r, fwd_s, fwd_r,
):
    nrow, ncol, nx, ny, nzl = sizes["rows"], sizes["cols"], sizes["x"], sizes["y"], sizes["zl"]
    nzh, n = sizes["zh"], sizes["n"]
    r = lax.axis_index("row")
    c = lax.axis_index("col")
    zh, x = lax.div(r, nx), lax.rem(r, nx)
    zl = lax.div(c, ny * CORES)
    y = lax.rem(lax.div(c, CORES), ny)
    core = lax.rem(c, CORES)
    z = zh * nzl + zl
    place = {"x": x, "y": y, "z": z}

    def peer(axis, step):
        there = lax.rem(place[axis] + step, n)
        if axis == "x":
            return (zh * nx + there, c), there
        if axis == "y":
            return (r, (zl * ny + there) * CORES + core), there
        return (lax.div(there, nzl) * nx + x, (lax.rem(there, nzl) * ny + y) * CORES + core), there

    mate = (r, c + 1 - 2 * core)
    west = (r, lax.rem(c + ncol - 1, ncol))
    east = (r, lax.rem(c + 1, ncol))
    north = (r - 1, c)
    south = (r + 1, c)
    has_north = r > 0
    has_south = r < nrow - 1
    split = nzh == 2
    flip = ((1 - zl) * ny + y) * CORES + core
    relays = ((nx - 1, nx - 1, nx, 0), (nrow - 1, nx - 1, nx, 1), (nx, nx, nx - 1, 0), (0, nx, nx - 1, 1)) if split else ()
    to_south = has_south & (r != nx - 1) if split else has_south
    to_north = has_north & (r != nx) if split else has_north

    loads = [
        pltpu.make_async_copy(src, dst, in_sems.at[i])
        for i, (src, dst) in enumerate(
            (
                (nodes_hbm, nv), (wm_hbm, wm), (wu_hbm, wu), (adjw_hbm, adjw), (wa_hbm, wa), (wo_hbm, wo),
                (decw_hbm, decw), (wd_hbm, wd), (wh_hbm, wh),
                *((target_hbm.at[:, pl.ds(g * TILE, TILE)], target.at[g]) for g in range(NT)),
            )
        )
    ]
    for load in loads[:3]:
        load.start()

    barrier = pltpu.get_barrier_semaphore()

    def greet(device):
        pl.semaphore_signal(barrier, inc=1, device_id=device, device_id_type=MESH)

    greeted = 2
    greet(west)
    greet(east)
    for axis in ("x", "y", "z"):
        for step in range(1, n):
            greet(peer(axis, step)[0])
            greeted += 1

    @pl.when(has_north)
    def _():
        greet(north)

    @pl.when(has_south)
    def _():
        greet(south)

    extra = jnp.where(has_north, 1, 0) + jnp.where(has_south, 1, 0)
    for row, _, target_row, _ in relays:

        @pl.when(r == row)
        def _(target_row=target_row):
            greet((target_row, flip))

        @pl.when(r == target_row)
        def _(row=row):
            greet((row, flip))

        extra = extra + jnp.where(r == row, 1, 0) + jnp.where(r == target_row, 1, 0)

    def send(src, dst, ssem, rsem, device):
        return pltpu.make_async_remote_copy(
            src_ref=src, dst_ref=dst, send_sem=ssem, recv_sem=rsem, device_id=device, device_id_type=MESH
        )

    loads[0].wait()
    for d in range(4):
        for b in range(4):
            pool1[d * 4 + b] = nv[send_ref[0, d, b]]
    pl.semaphore_wait(barrier, greeted + extra)

    halo_to = (south, north, east, west)
    halo_has = (to_south, to_north, None, None)
    from_has = (to_north, to_south, None, None)
    no_from = (jnp.logical_not(has_north), jnp.logical_not(has_south))

    def when(condition, body):
        if condition is None:
            body()
        else:
            pl.when(condition)(body)

    def halo_copy(d):
        part = pl.ds(d * 4, 4)
        return send(pool1.at[part], halo.at[part], halo_s.at[d], halo_r.at[d], halo_to[d])

    def hop_copy(turn, half, i, start, row):
        return send(
            pool1.at[start + half * 2 + i], rel.at[turn * 2 + i], hop_s.at[turn, half * 2 + i], hop_r.at[turn, i], (row, flip)
        )

    def forward_copy(turn, half, i, dst, start, row):
        return send(
            rel.at[turn * 2 + i], dst.at[start + half * 2 + i], fwd_s.at[turn, i], fwd_r.at[turn, half * 2 + i], (row, flip)
        )

    def hops(turn, starts, act):
        for row, source, _, half in relays:
            start = starts[0] if source == nx - 1 else starts[1]

            @pl.when(r == source)
            def _(row=row, half=half, start=start):
                for i in range(2):
                    act(hop_copy(turn, half, i, start, row))

    def forward(turn, i, dst, starts, begin):
        for row, source, target_row, half in relays:
            start = starts[0] if source == nx - 1 else starts[1]

            @pl.when(r == row)
            def _(target_row=target_row, half=half, start=start):
                copy = forward_copy(turn, half, i, dst, start, target_row)
                if begin:
                    hop_copy(turn, half, i, 0, 0).wait_recv()
                    copy.start()
                else:
                    copy.wait_send()

    def arrivals(turn, dst, starts):
        for row, source, target_row, half in relays:
            start = starts[0] if source == nx - 1 else starts[1]

            @pl.when(r == target_row)
            def _(row=row, half=half, start=start):
                for i in range(2):
                    forward_copy(turn, half, i, dst, start, row).wait_recv()

    for d in range(4):
        when(halo_has[d], lambda d=d: halo_copy(d).start())
        if d == 1:
            hops(0, (0, 4), lambda copy: copy.start())
    for load in loads[3:]:
        load.start()

    for d in range(2):

        @pl.when(no_from[d])
        def _(d=d):
            halo[pl.ds(d * 4, 4)] = jnp.zeros((4, TILE, D), BF16)
            backns[pl.ds(4 - d * 4, 4)] = jnp.zeros((4, TILE, D), BF16)

    def messages(xs, at):
        pre = dot(xs, wm[...])
        s = sigmoid(pre)
        put_rows(pref, NE + at, (pre * s).astype(BF16))
        put_rows(msl, at, (s * (1.0 + pre * (1.0 - s))).astype(BF16))

    loads[1].wait()
    loads[2].wait()

    @pl.loop(0, NT // GROUP)
    def _(g):
        xs = rows_of(nv, g * GROUP)
        messages(xs, g * GROUP)
        put_rows(g2f, g * GROUP, dot(xs, wu[...]))

    forward(0, 0, halo, (0, 4), True)

    def write_plan(at, rows):
        for i, row in enumerate(rows):
            plan_v[at + i : at + i + 1, :] = row

    write_plan(0, sort_plan([adj_ref[0, k, t] for t in range(NT) for k in range(K)], per=K))
    write_plan(6, sort_plan([dsend_ref[0, d, s] for d in range(2) for s in range(4)])[:4])
    write_plan(10, sort_plan([1 - mask_ref[0, g] for g in range(NT)])[:1])
    write_plan(11, sort_plan([send_ref[0, d, b] for d in range(4) for b in range(4)])[:4])
    first = pltpu.make_async_copy(plan_v.at[pl.ds(0, 16)], plan.at[pl.ds(0, 16)], plan_sem.at[0])
    first.start()
    first.wait()
    hidden = [plan[10, s] for s in range(SLOTS)]
    edge_list = [(hidden[s], k) for s in range(SLOTS) for k in range(KD)]
    write_plan(16, sort_plan([didx_ref[k, 0, g] for g, k in edge_list], [g * KD + k for g, k in edge_list], KD))
    second = pltpu.make_async_copy(plan_v.at[pl.ds(16, 8)], plan.at[pl.ds(16, 8)], plan_sem.at[1])
    second.start()
    second.wait()

    forward(0, 1, halo, (0, 4), True)
    for d in (3, 2, 0, 1):
        when(from_has[d], lambda d=d: halo_copy(d).wait_recv())
        if d == 0:
            arrivals(0, halo, (0, 4))
        messages(rows_of(halo, d * 4), NT + d * 4)

    for i in (3, 4, 5):
        loads[i].wait()

    @pl.loop(0, NT // GROUP)
    def _(g):
        for i in range(GROUP):
            t = g * GROUP + i
            weights = jnp.concatenate([adjw[t * K + k] for k in range(K)], axis=1)
            picked = jnp.concatenate(
                [pref[NE + t], pref[NE + NT + t], pref[NE + adj_ref[0, 2, t]], pref[NE + adj_ref[0, 3, t]]], axis=0
            )
            agg[t] = dot(weights, picked).astype(BF16)
        upre = rows_of(g2f, g * GROUP) + dot(rows_of(agg, g * GROUP), wa[...])
        s = sigmoid(upre)
        hidden_rows = (upre * s).astype(BF16)
        put_rows(hid, g * GROUP, hidden_rows)
        put_rows(usl, g * GROUP, (s * (1.0 + upre * (1.0 - s))).astype(BF16))
        v2 = rows_of(nv, g * GROUP).astype(F32) + dot(hidden_rows, wo[...])
        put_rows(pref, g * GROUP, v2.astype(BF16))

    for d in range(4):
        when(halo_has[d], lambda d=d: halo_copy(d).wait_send())
    hops(0, (0, 4), lambda copy: copy.wait_send())
    for d in range(2):
        for s in range(4):
            pref[NE + d * 4 + s] = pref[dsend_ref[0, d, s]]
    edges = [
        send(pref.at[pl.ds(NE, 4)], redge.at[pl.ds(4, 4)], edge_s.at[0], edge_r.at[0], west),
        send(pref.at[pl.ds(NE + 4, 4)], redge.at[pl.ds(0, 4)], edge_s.at[1], edge_r.at[1], east),
    ]
    for edge in edges:
        edge.start()
    for load in loads[6:]:
        load.wait()
    for edge in edges:
        edge.wait()
    for e in range(8):
        pref[NT + e] = redge[e]

    @pl.loop(0, SLOTS // GROUP)
    def _(g):
        goals, marks = [], []
        for i in range(GROUP):
            s = g * GROUP + i
            block = plan[10, s]
            weights = jnp.concatenate([decw[block * KD + k] for k in range(KD)], axis=1)
            picked = jnp.concatenate([pref[didx_ref[k, 0, block]] for k in range(KD)], axis=0)
            pool0[s] = dot(weights, picked).astype(BF16)
            goals.append(target[block].astype(F32))
            marks.append(jnp.full((1, TILE), mask_ref[0, block].astype(F32), F32))
        dpre = dot(rows_of(pool0, g * GROUP), wd[...])
        s = sigmoid(dpre)
        q = (dpre * s).astype(BF16)
        put_rows(pool1, g * GROUP, q)
        slope = s * (1.0 + dpre * (1.0 - s))
        residual = dot_nt(wh[...], q) - jnp.concatenate(goals, axis=1)
        residual = (jnp.concatenate(marks, axis=1) * residual).astype(BF16)
        err[:, pl.ds(pl.multiple_of(g * ROWS, ROWS), ROWS)] = residual
        dslope = (dot_tn(residual, wh[...]) * slope).astype(BF16)
        put_rows(mbuf, g * GROUP, dslope)
        put_rows(pool4, g * GROUP, dot_nt(dslope, wd[...]).astype(BF16))

    def spread(at, first_edge, last_edge, weight, source):
        if first_edge == 0:
            acc[...] = jnp.zeros((TILE, D), F32)

        @pl.loop(first_edge // GROUP, last_edge // GROUP)
        def _(h):
            total = acc[...]
            for i in range(GROUP):
                p = h * GROUP + i
                total = dot_tn(weight[plan[at + 5, p]], source[plan[at + 4, p]]) + plan[at + 1, p].astype(F32) * total
                pref[p] = total.astype(BF16)
            acc[...] = total

    def spread_of(at, tile):
        return plan[at + 3, tile].astype(F32) * pref[plan[at + 2, tile]].astype(F32)

    spread(16, 0, DEC_EDGES, decw, pool4)
    for e in range(8):
        pref[48 + e] = spread_of(16, NT + e).astype(BF16)
    returns = [
        send(pref.at[pl.ds(48, 4)], rgin.at[pl.ds(4, 4)], rg_s.at[0], rg_r.at[0], west),
        send(pref.at[pl.ds(52, 4)], rgin.at[pl.ds(0, 4)], rg_s.at[1], rg_r.at[1], east),
    ]
    for item in returns:
        item.start()

    def job_copy(j, sem, src, dst, device):
        return send(src, dst, job_s.at[j, sem], job_r.at[j, sem], device)

    def c_copy(j):
        at, rows, _ = JOBS[j]
        return job_copy(j, 0, cs.at[pl.ds(at, rows)], cr.at[pl.ds(at, rows)], mate)

    def first_copies(j):
        at, rows, order = JOBS[j]
        quarter = rows // n
        out = []
        for step in range(1, n):
            device, there = peer(order[0], step)
            src = cs.at[pl.ds(pl.multiple_of(at + there * quarter, 16), quarter)]
            out.append(job_copy(j, step, src, r1.at[step - 1, pl.ds(at // n, quarter)], device))
        return out

    def second_copies(j):
        at, rows, order = JOBS[j]
        small = rows // (n * n)
        out = []
        for step in range(1, n):
            device, there = peer(order[1], step)
            src = s2.at[pl.ds(pl.multiple_of(at // n + there * small, 16), small)]
            out.append(job_copy(j, 3 + step, src, r2.at[step - 1, pl.ds(at // (n * n), small)], device))
        return out

    def third_copies(j):
        at, rows, order = JOBS[j]
        small = rows // (n * n)
        out = []
        for step in range(1, n):
            device, _ = peer(order[2], step)
            mine = x4.at[place[order[2]], pl.ds(at // (n * n), small)]
            out.append(job_copy(j, 6 + step, mine, mine, device))
        return out

    def small_at(j):
        at, rows, order = JOBS[j]
        quarter, small = rows // n, rows // (n * n)
        return pl.multiple_of(at + place[order[0]] * quarter + place[order[1]] * small, 16)

    def back_small(j):
        at, rows, order = JOBS[j]
        part = cr.at[pl.ds(small_at(j), rows // (n * n))]
        return [
            job_copy(j, 9 + step, part, part, peer(order[1], step)[0]) for step in range(1, n)
        ]

    def back_quarter(j):
        at, rows, order = JOBS[j]
        quarter = rows // n
        part = cr.at[pl.ds(pl.multiple_of(at + place[order[0]] * quarter, 16), quarter)]
        return [
            job_copy(j, 12 + step, part, part, peer(order[0], step)[0]) for step in range(1, n)
        ]

    def back_core(j):
        at, rows, _ = JOBS[j]
        part = pl.ds(at, rows)
        return (
            job_copy(j, 16, cr.at[part], grads_hbm.at[core, part], mate),
            pltpu.make_async_copy(cr.at[part], grads_hbm.at[core, part], job_l.at[j]),
        )

    def job_stage(j, stage_number):
        at, rows, order = JOBS[j]
        quarter, small = rows // n, rows // (n * n)
        whole = pl.ds(at, rows)
        own = pl.ds(at % GRAD_F32, rows)
        if stage_number == 0:
            low, high = gbuf[own, :HALF], gbuf[own, HALF:]
            cs[whole] = jnp.where(core == 0, high, low).astype(BF16)
            c_copy(j).start()
        elif stage_number == 1:
            c_copy(j).wait()
            low, high = gbuf[own, :HALF], gbuf[own, HALF:]
            cs[whole] = (jnp.where(core == 0, low, high) + cr[whole].astype(F32)).astype(BF16)
            for item in first_copies(j):
                item.start()
        elif stage_number == 2:
            mine = pl.ds(pl.multiple_of(at + place[order[0]] * quarter, 16), quarter)
            for item in first_copies(j):
                item.wait()
            total = cs[mine].astype(F32)
            for step in range(n - 1):
                total = total + r1[step, pl.ds(at // n, quarter)].astype(F32)
            s2[pl.ds(at // n, quarter)] = total.astype(BF16)
            for item in second_copies(j):
                item.start()
        elif stage_number == 3:
            mine = pl.ds(pl.multiple_of(at // n + place[order[1]] * small, 16), small)
            for item in second_copies(j):
                item.wait()
            total = s2[mine].astype(F32)
            for step in range(n - 1):
                total = total + r2[step, pl.ds(at // (n * n), small)].astype(F32)
            x4[place[order[2]], pl.ds(at // (n * n), small)] = total.astype(BF16)
            for item in third_copies(j):
                item.start()
        elif stage_number == 4:
            for item in third_copies(j):
                item.wait()
            total = x4[0, pl.ds(at // (n * n), small)].astype(F32)
            for other in range(1, n):
                total = total + x4[other, pl.ds(at // (n * n), small)].astype(F32)
            cr[pl.ds(small_at(j), small)] = (total * (1.0 / (nrow * ncol))).astype(BF16)
            for item in back_small(j):
                item.start()
        elif stage_number == 5:
            for item in back_small(j):
                item.wait()
            for item in back_quarter(j):
                item.start()
        elif stage_number == 6:
            for item in back_quarter(j):
                item.wait()
            for item in back_core(j):
                item.start()
        else:
            for item in back_core(j):
                item.wait()

    def gradient(at, left, right, halves=(0, 1)):
        for half in halves:
            lanes = slice(half * HALF, (half + 1) * HALF)
            total = None
            for (lref, lat, count), (rref, rat) in zip(left, right):
                lhs = lref[pl.ds(lat, count), :, lanes].reshape(count * TILE, HALF)
                term = dot_tn(lhs, rows_of(rref, rat, count))
                total = term if total is None else total + term
            gbuf[pl.ds(at % GRAD_F32 + half * HALF, HALF)] = total

    gradient(0, [(pool0, 0, SLOTS)], [(mbuf, 0)])
    q_rows = pool1[pl.ds(0, SLOTS)].reshape(SLOTS * TILE, D)
    gbuf[512:768, :] = jnp.zeros((256, D), F32)
    gbuf[512 : 512 + OUTC, :] = dot(err[...], q_rows)
    job_stage(0, 0)

    for item in returns:
        item.wait()
    total = None
    for p in range(8):
        arrived = rgin[plan[6, p]].astype(F32)
        total = arrived if total is None else arrived + plan[7, p].astype(F32) * total
        pref[40 + p] = total.astype(BF16)

    @pl.loop(0, NT)
    def _(t):
        value = spread_of(16, t).astype(BF16).astype(F32)
        value = value + plan[9, t].astype(F32) * pref[40 + plan[8, t]].astype(F32)
        g2f[t] = value
        pool4[t] = value.astype(BF16)

    job_stage(0, 1)
    gradient(768, [(hid, 0, NT)], [(pool4, 0)])
    job_stage(1, 0)

    @pl.loop(0, NT // GROUP)
    def _(g):
        back = dot_nt(rows_of(pool4, g * GROUP), wo[...]) * rows_of(usl, g * GROUP).astype(F32)
        slope = back.astype(BF16)
        put_rows(pool0, g * GROUP, slope)
        put_rows(g2f, g * GROUP, rows_of(g2f, g * GROUP) + dot_nt(slope, wu[...]))
        put_rows(pool1, g * GROUP, dot_nt(slope, wa[...]).astype(BF16))

    job_stage(0, 2)
    job_stage(1, 1)
    gradient(1280, [(nv, 0, NT)], [(pool0, 0)])
    job_stage(2, 0)
    gradient(1792, [(agg, 0, NT)], [(pool0, 0)])
    job_stage(3, 0)
    job_stage(2, 1)
    spread(0, 0, ADJ_EDGES // 2, adjw, pool1)
    job_stage(0, 3)
    job_stage(3, 1)
    job_stage(1, 2)
    spread(0, ADJ_EDGES // 2, ADJ_EDGES, adjw, pool1)

    def message_slope(e):
        mbuf[e] = (spread_of(0, e) * msl[e].astype(F32)).astype(BF16)

    back_to = (north, south, west, east)
    back_has = (to_north, to_south, None, None)
    back_from = (to_south, to_north, None, None)

    def back_copy(d):
        dst = (backns.at[pl.ds(0, 4)], backns.at[pl.ds(4, 4)], redge.at[pl.ds(0, 4)], redge.at[pl.ds(4, 4)])[d]
        return send(pool1.at[pl.ds(d * 4, 4)], dst, hg_s.at[d], hg_r.at[d], back_to[d])

    for d in range(4):

        @pl.loop(0, 4)
        def _(b, d=d):
            message_slope(NT + d * 4 + b)

        put_rows(pool1, d * 4, dot_nt(rows_of(mbuf, NT + d * 4), wm[...]).astype(BF16))
        when(back_has[d], lambda d=d: back_copy(d).start())
        if d == 1:
            hops(1, (4, 0), lambda copy: copy.start())

    job_stage(0, 4)
    job_stage(2, 2)

    @pl.loop(0, NT)
    def _(e):
        message_slope(e)

    job_stage(1, 3)
    job_stage(3, 2)
    left, right = [(nv, 0, NT), (halo, 0, NT)], [(mbuf, 0), (mbuf, NT)]
    gradient(2304, left, right, (0,))
    job_stage(4, 0)
    forward(1, 0, backns, (4, 0), True)
    job_stage(0, 5)
    job_stage(2, 3)
    gradient(2304, left, right, (1,))
    job_stage(5, 0)
    job_stage(4, 1)
    forward(1, 1, backns, (4, 0), True)
    job_stage(3, 3)
    job_stage(1, 4)

    @pl.loop(0, NT // GROUP)
    def _(g):
        put_rows(g2f, g * GROUP, rows_of(g2f, g * GROUP) + dot_nt(rows_of(mbuf, g * GROUP), wm[...]))

    job_stage(5, 1)
    job_stage(0, 6)
    job_stage(2, 4)
    job_stage(4, 2)
    job_stage(3, 4)
    job_stage(1, 5)
    job_stage(5, 2)
    job_stage(2, 5)
    job_stage(4, 3)
    job_stage(3, 5)
    job_stage(5, 3)
    job_stage(1, 6)
    for d in range(4):
        when(back_from[d], lambda d=d: back_copy(d).wait_recv())
    arrivals(1, backns, (4, 0))
    for e in range(8):
        pref[e] = backns[e]
        pref[8 + e] = redge[e]
    job_stage(4, 4)
    job_stage(5, 4)
    total = None
    for p in range(16):
        arrived = pref[plan[11, p]].astype(F32)
        total = arrived if total is None else arrived + plan[12, p].astype(F32) * total
        pref[16 + p] = total.astype(BF16)

    @pl.loop(0, NT)
    def _(t):
        value = g2f[t] + plan[14, t].astype(F32) * pref[16 + plan[13, t]].astype(F32)
        agg[t] = value.astype(BF16)

    lat_out = pltpu.make_async_copy(agg, lat_hbm, out_sem.at[0])
    lat_out.start()
    for stage in range(5, 7):
        for j in (4, 5):
            job_stage(j, stage)
        if stage == 5:
            job_stage(2, 6)
            job_stage(3, 6)
    for j in range(len(JOBS)):
        job_stage(j, 7)
    lat_out.wait()
    for d in range(4):
        when(back_has[d], lambda d=d: back_copy(d).wait_send())
    hops(1, (4, 0), lambda copy: copy.wait_send())
    for turn in range(2):
        for i in range(2):
            forward(turn, i, (halo, backns)[turn], (0, 4), False)


def finish(lat_ref, m_ref, u_ref, a_ref, o_ref, d_ref, h_ref,
           latent_ref, msg_ref, upd_ref, agg_ref, out_ref, dec_ref, head_ref):
    latent_ref[...] = lat_ref[...].astype(F32)
    for src, dst in (
        (m_ref, msg_ref), (u_ref, upd_ref), (a_ref, agg_ref), (o_ref, out_ref), (d_ref, dec_ref), (h_ref, head_ref),
    ):
        dst[:, :HALF] = src[0].astype(F32)
        dst[:, HALF:] = src[1].astype(F32)


def on_device(
    sizes, nodes, send_list, adj_index, adj_weight, dec_send, dec_index, dec_weight, hidden_mask, target,
    w_msg, w_update, w_aggregate, w_output, w_decode, w_head,
):
    n = sizes["n"]
    tiles = lambda count, dtype=BF16: pltpu.VMEM((count, TILE, D), dtype)
    any_spec = pl.BlockSpec(memory_space=pl.ANY)
    smem = pl.BlockSpec(memory_space=pltpu.SMEM)
    scratch = [
        tiles(NT), tiles(NT),
        pltpu.VMEM((NT * K, TILE, TILE), BF16), pltpu.VMEM((NT * KD, TILE, TILE), BF16),
        pltpu.VMEM((NT, OUTC, TILE), BF16),
        *[pltpu.VMEM((D, D), BF16)] * 5, pltpu.VMEM((OUTC, D), BF16),
        tiles(2 * NE), tiles(NE), tiles(NT, F32),
        tiles(NT), tiles(NT), tiles(NT),
        tiles(8), tiles(8), pltpu.VMEM((OUTC, SLOTS * TILE), BF16),
        tiles(NT), tiles(NT), tiles(NE), tiles(NT),
        pltpu.VMEM((TILE, D), F32),
        pltpu.VMEM((GRAD_F32, D), F32),
        pltpu.VMEM((GRAD_ROWS, HALF), BF16), pltpu.VMEM((GRAD_ROWS, HALF), BF16),
        pltpu.VMEM((n - 1, GRAD_ROWS // n, HALF), BF16), pltpu.VMEM((GRAD_ROWS // n, HALF), BF16),
        pltpu.VMEM((n - 1, GRAD_ROWS // n**2, HALF), BF16), pltpu.VMEM((n, GRAD_ROWS // n**2, HALF), BF16),
        tiles(4), tiles(8),
        pltpu.VMEM((24, 128), jnp.int32), pltpu.SMEM((24, 128), jnp.int32),
        pltpu.SemaphoreType.DMA((9 + NT,)), pltpu.SemaphoreType.DMA((2,)), pltpu.SemaphoreType.DMA((1,)),
        *[pltpu.SemaphoreType.DMA((4,))] * 2,
        *[pltpu.SemaphoreType.DMA((2,))] * 4,
        *[pltpu.SemaphoreType.DMA((4,))] * 2,
        *[pltpu.SemaphoreType.DMA((len(JOBS), JOB_SEMS))] * 2,
        pltpu.SemaphoreType.DMA((len(JOBS),)),
        pltpu.SemaphoreType.DMA((2, 4)), pltpu.SemaphoreType.DMA((2, 2)),
        pltpu.SemaphoreType.DMA((2, 2)), pltpu.SemaphoreType.DMA((2, 4)),
    ]
    lat, grads = pl.pallas_call(
        functools.partial(kernel, sizes),
        out_shape=(
            jax.ShapeDtypeStruct((NT, TILE, D), BF16),
            jax.ShapeDtypeStruct((CORES, GRAD_ROWS, HALF), BF16),
        ),
        in_specs=[smem] * 5 + [any_spec] * 10,
        out_specs=(any_spec,) * 2,
        scratch_shapes=scratch,
        compiler_params=pltpu.CompilerParams(
            collective_id=0, has_side_effects=True, vmem_limit_bytes=62 * 1024 * 1024
        ),
        name="mesh_step",
    )(
        send_list, adj_index.transpose(0, 2, 1), dec_send, dec_index.transpose(2, 0, 1), hidden_mask,
        nodes.reshape(NT, TILE, D),
        adj_weight.reshape(NT * K, TILE, TILE),
        dec_weight.reshape(NT * KD, TILE, TILE),
        target.T,
        w_msg, w_update, w_aggregate, w_output, w_decode, w_head.T,
    )
    steps = 8
    block = D // steps

    def rows_spec(at, size=block):
        return pl.BlockSpec((CORES, size, HALF), lambda i: (0, at // size + i, 0))

    latents = pl.BlockSpec((NT // steps, TILE, D), lambda i: (i, 0, 0))
    square = pl.BlockSpec((block, D), lambda i: (i, 0))
    f32 = lambda *shape: jax.ShapeDtypeStruct(shape, F32)
    outs = pl.pallas_call(
        finish,
        out_shape=(f32(NT, TILE, D), *[f32(D, D)] * 5, f32(OUTC, D)),
        grid=(steps,),
        in_specs=[latents, *(rows_spec(at) for at in (2304, 1280, 1792, 768, 0)), rows_spec(512, HALF // steps)],
        out_specs=(latents, *[square] * 5, pl.BlockSpec((HALF // steps, D), lambda i: (i, 0))),
        compiler_params=pltpu.CompilerParams(vmem_limit_bytes=60 * 1024 * 1024),
        name="finish",
    )(lat, grads, grads, grads, grads, grads, grads)
    latent, msg, upd, agg, out, dec, head = outs
    return latent.reshape(NT * TILE, D), msg, upd, agg, out, dec, head.T


def solution(mesh):
    rows, cols = mesh.shape["row"], mesh.shape["col"]
    sizes = dict(axes_of(rows, cols), rows=rows, cols=cols)
    both = ("row", "col")
    return jax.shard_map(
        functools.partial(on_device, sizes),
        mesh=mesh,
        in_specs=(
            P(both, None),
            P(both, None, None),
            P(both, None, None),
            P(both, None, None, None),
            P(both, None, None),
            P(both, None, None),
            P(both, None, None, None),
            P(both, None),
            P(both, None),
            *[P()] * 6,
        ),
        out_specs=(P(both, None), *[P()] * 6),
        check_vma=False,
    )
```

```python
import functools

import jax
import jax.numpy as jnp
from jax import lax
from jax.experimental import pallas as pl
from jax.experimental.pallas import tpu as pltpu
from jax.sharding import PartitionSpec as P

MESH = pl.DeviceIdType.MESH
F32 = jnp.float32
BF16 = jnp.bfloat16

D = 512
OUTC = 227
TILE = 128
NT = 16
NE = 32
NR = 24
K = 4
KD = 3
SLOTS = 12
DEC_EDGES = SLOTS * KD
ADJ_EDGES = NT * K
GROUP = 4
ROWS = GROUP * TILE
CORES = 2

JOBS = (
    (0, 768, ("z", "y", "x")),
    (768, 512, ("y", "x", "z")),
    (1280, 512, ("x", "z", "y")),
    (1792, 512, ("z", "x", "y")),
    (2304, 256, ("y", "z", "x")),
    (2560, 256, ("z", "y", "x")),
)
GRAD_ROWS = 2816
GRAD_F32 = 2304
HALF = D // 2
JOB_SEMS = 17


def axes_of(rows, cols):
    if (rows, cols) == (8, 16):
        return dict(zh=2, x=4, zl=2, y=4, n=4)
    return dict(zh=1, x=2, zl=2, y=2, n=2)


def dot(a, b):
    return lax.dot_general(a, b, (((1,), (0,)), ((), ())), preferred_element_type=F32)


def dot_nt(a, b):
    return lax.dot_general(a, b, (((1,), (1,)), ((), ())), preferred_element_type=F32)


def dot_tn(a, b):
    return lax.dot_general(a, b, (((0,), (0,)), ((), ())), preferred_element_type=F32)


def sigmoid(v):
    return 0.5 * jnp.tanh(0.5 * v) + 0.5


def rows_of(ref, start, count=GROUP):
    block = ref[pl.ds(start, count)]
    return block.reshape(count * TILE, block.shape[-1])


def put_rows(ref, start, value, count=GROUP):
    ref[pl.ds(start, count)] = value.reshape(count, TILE, value.shape[-1])


def outer_first(value, inner, outer):
    return jnp.where(value >= inner, value - inner, value + outer)


def sort_plan(values, blocks=None, per=1):
    count = len(values)
    depth = -(-count // 8) * 8
    down = lax.broadcasted_iota(jnp.int32, (depth, 128), 0)
    across = lax.broadcasted_iota(jnp.int32, (depth, 128), 1)
    mine = jnp.full((depth, 128), 1000, jnp.int32)
    other = jnp.full((depth, 128), 1000, jnp.int32)
    for q, value in enumerate(values):
        mine = jnp.where(down == q, value, mine)
        other = jnp.where(across == q, value, other)
    same_before = jnp.where((other == mine) & (across < down), 1, 0)
    before = jnp.where(other < mine, 1, 0) + same_before
    rank = jnp.sum(before, axis=1, keepdims=True)
    continues = jnp.minimum(jnp.sum(same_before, axis=1, keepdims=True), 1)
    hit = jnp.where((rank == across) & (down < count), 1, 0)
    order = jnp.sum(hit * down, axis=0, keepdims=True)
    follows = jnp.sum(hit * continues, axis=0, keepdims=True)
    upto = jnp.sum(jnp.where(mine <= across, 1, 0), axis=0, keepdims=True)
    present = jnp.minimum(jnp.sum(jnp.where(mine == across, 1, 0), axis=0, keepdims=True), 1)
    group = {1: down, 3: (down * 43) >> 7, 4: down >> 2}[per]
    group_row = jnp.sum(hit * group, axis=0, keepdims=True)
    named = down
    if blocks is not None:
        for q, value in enumerate(blocks):
            named = jnp.where(down == q, value, named)
    named_row = jnp.sum(hit * named, axis=0, keepdims=True)
    return order, follows, jnp.maximum(upto - 1, 0), present, group_row, named_row


def kernel(
    sizes,
    send_ref, adj_ref, dsend_ref, didx_ref, mask_ref,
    nodes_hbm, adjw_hbm, decw_hbm, target_hbm,
    wm_hbm, wu_hbm, wa_hbm, wo_hbm, wd_hbm, wh_hbm,
    lat_hbm, grads_hbm,
    nv, halo, adjw, decw, target, wm, wu, wa, wo, wd, wh,
    pref, msl, g2f, agg, hid, usl, redge, rgin, err, pool0, pool1, mbuf, pool4, acc,
    gbuf, cs, cr, r1, s2, r2, x4,
    backns, plan_v, plan,
    in_sems, plan_sem, out_sem, halo_s, halo_r, edge_s, edge_r, rg_s, rg_r, hg_s, hg_r, job_s, job_r, job_l,
):
    nrow, ncol, nx, ny, nzl = sizes["rows"], sizes["cols"], sizes["x"], sizes["y"], sizes["zl"]
    nzh, n = sizes["zh"], sizes["n"]
    r = lax.axis_index("row")
    c = lax.axis_index("col")
    zh, x = lax.div(r, nx), lax.rem(r, nx)
    zl = lax.div(c, ny * CORES)
    y = lax.rem(lax.div(c, CORES), ny)
    core = lax.rem(c, CORES)
    z = zh * nzl + zl
    place = {"x": x, "y": y, "z": z}

    def peer(axis, step):
        there = lax.rem(place[axis] + step, n)
        if axis == "x":
            return (zh * nx + there, c), there
        if axis == "y":
            return (r, (zl * ny + there) * CORES + core), there
        return (lax.div(there, nzl) * nx + x, (lax.rem(there, nzl) * ny + y) * CORES + core), there

    mate = (r, c + 1 - 2 * core)
    west = (r, lax.rem(c + ncol - 1, ncol))
    east = (r, lax.rem(c + 1, ncol))
    north = (r - 1, c)
    south = (r + 1, c)
    has_north = r > 0
    has_south = r < nrow - 1

    loads = [
        pltpu.make_async_copy(src, dst, in_sems.at[i])
        for i, (src, dst) in enumerate(
            (
                (nodes_hbm, nv), (wm_hbm, wm), (wu_hbm, wu), (adjw_hbm, adjw), (wa_hbm, wa), (wo_hbm, wo),
                (decw_hbm, decw), (wd_hbm, wd), (wh_hbm, wh),
                *((target_hbm.at[:, pl.ds(g * TILE, TILE)], target.at[g]) for g in range(NT)),
            )
        )
    ]
    for load in loads[:3]:
        load.start()

    barrier = pltpu.get_barrier_semaphore()

    def greet(device):
        pl.semaphore_signal(barrier, inc=1, device_id=device, device_id_type=MESH)

    greeted = 2
    greet(west)
    greet(east)
    for axis in ("x", "y", "z"):
        for step in range(1, n):
            greet(peer(axis, step)[0])
            greeted += 1

    @pl.when(has_north)
    def _():
        greet(north)

    @pl.when(has_south)
    def _():
        greet(south)

    extra = jnp.where(has_north, 1, 0) + jnp.where(has_south, 1, 0)

    def send(src, dst, ssem, rsem, device):
        return pltpu.make_async_remote_copy(
            src_ref=src, dst_ref=dst, send_sem=ssem, recv_sem=rsem, device_id=device, device_id_type=MESH
        )

    loads[0].wait()
    for d in range(4):
        for b in range(4):
            pool1[d * 4 + b] = nv[send_ref[0, d, b]]
    pl.semaphore_wait(barrier, greeted + extra)

    halo_to = (south, north, east, west)
    halo_has = (has_south, has_north, None, None)
    from_has = (has_north, has_south, None, None)
    no_from = (jnp.logical_not(has_north), jnp.logical_not(has_south))

    def when(condition, body):
        if condition is None:
            body()
        else:
            pl.when(condition)(body)

    def halo_copy(d):
        part = pl.ds(d * 4, 4)
        return send(pool1.at[part], halo.at[part], halo_s.at[d], halo_r.at[d], halo_to[d])

    for d in range(4):
        when(halo_has[d], lambda d=d: halo_copy(d).start())
    for load in loads[3:]:
        load.start()

    for d in range(2):

        @pl.when(no_from[d])
        def _(d=d):
            halo[pl.ds(d * 4, 4)] = jnp.zeros((4, TILE, D), BF16)
            backns[pl.ds(4 - d * 4, 4)] = jnp.zeros((4, TILE, D), BF16)

    def messages(xs, at):
        pre = dot(xs, wm[...])
        s = sigmoid(pre)
        put_rows(pref, NE + at, (pre * s).astype(BF16))
        put_rows(msl, at, (s * (1.0 + pre * (1.0 - s))).astype(BF16))

    loads[1].wait()
    loads[2].wait()

    @pl.loop(0, NT // GROUP)
    def _(g):
        xs = rows_of(nv, g * GROUP)
        messages(xs, g * GROUP)
        put_rows(g2f, g * GROUP, dot(xs, wu[...]))

    def write_plan(at, rows):
        for i, row in enumerate(rows):
            plan_v[at + i : at + i + 1, :] = row

    write_plan(0, sort_plan([outer_first(adj_ref[0, k, t], NT, NT) for t in range(NT) for k in range(K)], per=K))
    write_plan(6, sort_plan([dsend_ref[0, d, s] for d in range(2) for s in range(4)])[:4])
    write_plan(10, sort_plan([1 - mask_ref[0, g] for g in range(NT)])[:1])
    write_plan(11, sort_plan([send_ref[0, d, b] for d in range(4) for b in range(4)])[:4])
    first = pltpu.make_async_copy(plan_v.at[pl.ds(0, 16)], plan.at[pl.ds(0, 16)], plan_sem.at[0])
    first.start()
    first.wait()
    hidden = [plan[10, s] for s in range(SLOTS)]
    edge_list = [(hidden[s], k) for s in range(SLOTS) for k in range(KD)]
    write_plan(16, sort_plan([outer_first(didx_ref[k, 0, g], NT, 8) for g, k in edge_list], [g * KD + k for g, k in edge_list], KD))
    second = pltpu.make_async_copy(plan_v.at[pl.ds(16, 8)], plan.at[pl.ds(16, 8)], plan_sem.at[1])
    second.start()
    second.wait()

    for d in (3, 2, 0, 1):
        when(from_has[d], lambda d=d: halo_copy(d).wait_recv())
        messages(rows_of(halo, d * 4), NT + d * 4)

    for i in (3, 4, 5):
        loads[i].wait()

    @pl.loop(0, NT // GROUP)
    def _(g):
        for i in range(GROUP):
            t = g * GROUP + i
            weights = jnp.concatenate([adjw[t * K + k] for k in range(K)], axis=1)
            picked = jnp.concatenate(
                [pref[NE + t], pref[NE + NT + t], pref[NE + adj_ref[0, 2, t]], pref[NE + adj_ref[0, 3, t]]], axis=0
            )
            agg[t] = dot(weights, picked).astype(BF16)
        upre = rows_of(g2f, g * GROUP) + dot(rows_of(agg, g * GROUP), wa[...])
        s = sigmoid(upre)
        hidden_rows = (upre * s).astype(BF16)
        put_rows(hid, g * GROUP, hidden_rows)
        put_rows(usl, g * GROUP, (s * (1.0 + upre * (1.0 - s))).astype(BF16))
        v2 = rows_of(nv, g * GROUP).astype(F32) + dot(hidden_rows, wo[...])
        put_rows(pref, g * GROUP, v2.astype(BF16))

    for d in range(4):
        when(halo_has[d], lambda d=d: halo_copy(d).wait_send())
    for d in range(2):
        for s in range(4):
            pref[NE + d * 4 + s] = pref[dsend_ref[0, d, s]]
    edges = [
        send(pref.at[pl.ds(NE, 4)], redge.at[pl.ds(4, 4)], edge_s.at[0], edge_r.at[0], west),
        send(pref.at[pl.ds(NE + 4, 4)], redge.at[pl.ds(0, 4)], edge_s.at[1], edge_r.at[1], east),
    ]
    for edge in edges:
        edge.start()
    for load in loads[6:]:
        load.wait()
    for edge in edges:
        edge.wait()
    for e in range(8):
        pref[NT + e] = redge[e]

    @pl.loop(0, SLOTS // GROUP)
    def _(g):
        goals, marks = [], []
        for i in range(GROUP):
            s = g * GROUP + i
            block = plan[10, s]
            weights = jnp.concatenate([decw[block * KD + k] for k in range(KD)], axis=1)
            picked = jnp.concatenate([pref[didx_ref[k, 0, block]] for k in range(KD)], axis=0)
            pool0[s] = dot(weights, picked).astype(BF16)
            goals.append(target[block].astype(F32))
            marks.append(jnp.full((1, TILE), mask_ref[0, block].astype(F32), F32))
        dpre = dot(rows_of(pool0, g * GROUP), wd[...])
        s = sigmoid(dpre)
        q = (dpre * s).astype(BF16)
        put_rows(pool1, g * GROUP, q)
        slope = s * (1.0 + dpre * (1.0 - s))
        residual = dot_nt(wh[...], q) - jnp.concatenate(goals, axis=1)
        residual = (jnp.concatenate(marks, axis=1) * residual).astype(BF16)
        err[:, pl.ds(pl.multiple_of(g * ROWS, ROWS), ROWS)] = residual
        dslope = (dot_tn(residual, wh[...]) * slope).astype(BF16)
        put_rows(mbuf, g * GROUP, dslope)
        put_rows(pool4, g * GROUP, dot_nt(dslope, wd[...]).astype(BF16))

    def spread(at, first_edge, last_edge, weight, source):
        if first_edge == 0:
            acc[...] = jnp.zeros((TILE, D), F32)

        @pl.loop(first_edge // GROUP, last_edge // GROUP)
        def _(h):
            total = acc[...]
            for i in range(GROUP):
                p = h * GROUP + i
                total = dot_tn(weight[plan[at + 5, p]], source[plan[at + 4, p]]) + plan[at + 1, p].astype(F32) * total
                pref[p] = total.astype(BF16)
            acc[...] = total

    def spread_of(at, tile):
        return plan[at + 3, tile].astype(F32) * pref[plan[at + 2, tile]].astype(F32)

    spread(16, 0, SLOTS * (KD - 1), decw, pool4)
    for e in range(8):
        pref[48 + e] = spread_of(16, e).astype(BF16)
    returns = [
        send(pref.at[pl.ds(48, 4)], rgin.at[pl.ds(4, 4)], rg_s.at[0], rg_r.at[0], west),
        send(pref.at[pl.ds(52, 4)], rgin.at[pl.ds(0, 4)], rg_s.at[1], rg_r.at[1], east),
    ]
    for item in returns:
        item.start()
    spread(16, SLOTS * (KD - 1), DEC_EDGES, decw, pool4)

    def job_copy(j, sem, src, dst, device):
        return send(src, dst, job_s.at[j, sem], job_r.at[j, sem], device)

    def c_copy(j):
        at, rows, _ = JOBS[j]
        return job_copy(j, 0, cs.at[pl.ds(at, rows)], cr.at[pl.ds(at, rows)], mate)

    def first_copies(j):
        at, rows, order = JOBS[j]
        quarter = rows // n
        out = []
        for step in range(1, n):
            device, there = peer(order[0], step)
            src = cs.at[pl.ds(pl.multiple_of(at + there * quarter, 16), quarter)]
            out.append(job_copy(j, step, src, r1.at[step - 1, pl.ds(at // n, quarter)], device))
        return out

    def second_copies(j):
        at, rows, order = JOBS[j]
        small = rows // (n * n)
        out = []
        for step in range(1, n):
            device, there = peer(order[1], step)
            src = s2.at[pl.ds(pl.multiple_of(at // n + there * small, 16), small)]
            out.append(job_copy(j, 3 + step, src, r2.at[step - 1, pl.ds(at // (n * n), small)], device))
        return out

    def third_copies(j):
        at, rows, order = JOBS[j]
        small = rows // (n * n)
        out = []
        for step in range(1, n):
            device, _ = peer(order[2], step)
            mine = x4.at[place[order[2]], pl.ds(at // (n * n), small)]
            out.append(job_copy(j, 6 + step, mine, mine, device))
        return out

    def small_at(j):
        at, rows, order = JOBS[j]
        quarter, small = rows // n, rows // (n * n)
        return pl.multiple_of(at + place[order[0]] * quarter + place[order[1]] * small, 16)

    def back_small(j):
        at, rows, order = JOBS[j]
        part = cr.at[pl.ds(small_at(j), rows // (n * n))]
        return [
            job_copy(j, 9 + step, part, part, peer(order[1], step)[0]) for step in range(1, n)
        ]

    def back_quarter(j):
        at, rows, order = JOBS[j]
        quarter = rows // n
        part = cr.at[pl.ds(pl.multiple_of(at + place[order[0]] * quarter, 16), quarter)]
        return [
            job_copy(j, 12 + step, part, part, peer(order[0], step)[0]) for step in range(1, n)
        ]

    def back_core(j):
        at, rows, _ = JOBS[j]
        part = pl.ds(at, rows)
        return (
            job_copy(j, 16, cr.at[part], grads_hbm.at[core, part], mate),
            pltpu.make_async_copy(cr.at[part], grads_hbm.at[core, part], job_l.at[j]),
        )

    def job_stage(j, stage_number):
        at, rows, order = JOBS[j]
        quarter, small = rows // n, rows // (n * n)
        whole = pl.ds(at, rows)
        own = pl.ds(at % GRAD_F32, rows)
        if stage_number == 0:
            low, high = gbuf[own, :HALF], gbuf[own, HALF:]
            cs[whole] = jnp.where(core == 0, high, low).astype(BF16)
            c_copy(j).start()
        elif stage_number == 1:
            c_copy(j).wait()
            low, high = gbuf[own, :HALF], gbuf[own, HALF:]
            cs[whole] = (jnp.where(core == 0, low, high) + cr[whole].astype(F32)).astype(BF16)
            for item in first_copies(j):
                item.start()
        elif stage_number == 2:
            mine = pl.ds(pl.multiple_of(at + place[order[0]] * quarter, 16), quarter)
            for item in first_copies(j):
                item.wait()
            total = cs[mine].astype(F32)
            for step in range(n - 1):
                total = total + r1[step, pl.ds(at // n, quarter)].astype(F32)
            s2[pl.ds(at // n, quarter)] = total.astype(BF16)
            for item in second_copies(j):
                item.start()
        elif stage_number == 3:
            mine = pl.ds(pl.multiple_of(at // n + place[order[1]] * small, 16), small)
            for item in second_copies(j):
                item.wait()
            total = s2[mine].astype(F32)
            for step in range(n - 1):
                total = total + r2[step, pl.ds(at // (n * n), small)].astype(F32)
            x4[place[order[2]], pl.ds(at // (n * n), small)] = total.astype(BF16)
            for item in third_copies(j):
                item.start()
        elif stage_number == 4:
            for item in third_copies(j):
                item.wait()
            total = x4[0, pl.ds(at // (n * n), small)].astype(F32)
            for other in range(1, n):
                total = total + x4[other, pl.ds(at // (n * n), small)].astype(F32)
            cr[pl.ds(small_at(j), small)] = (total * (1.0 / (nrow * ncol))).astype(BF16)
            for item in back_small(j):
                item.start()
        elif stage_number == 5:
            for item in back_small(j):
                item.wait()
            for item in back_quarter(j):
                item.start()
        elif stage_number == 6:
            for item in back_quarter(j):
                item.wait()
            for item in back_core(j):
                item.start()
        else:
            for item in back_core(j):
                item.wait()

    def gradient(at, left, right, halves=(0, 1)):
        for half in halves:
            lanes = slice(half * HALF, (half + 1) * HALF)
            total = None
            for (lref, lat, count), (rref, rat) in zip(left, right):
                lhs = lref[pl.ds(lat, count), :, lanes].reshape(count * TILE, HALF)
                term = dot_tn(lhs, rows_of(rref, rat, count))
                total = term if total is None else total + term
            gbuf[pl.ds(at % GRAD_F32 + half * HALF, HALF)] = total

    gradient(0, [(pool0, 0, SLOTS)], [(mbuf, 0)])
    q_rows = pool1[pl.ds(0, SLOTS)].reshape(SLOTS * TILE, D)
    gbuf[512:768, :] = jnp.zeros((256, D), F32)
    gbuf[512 : 512 + OUTC, :] = dot(err[...], q_rows)
    job_stage(0, 0)

    for item in returns:
        item.wait()
    total = None
    for p in range(8):
        arrived = rgin[plan[6, p]].astype(F32)
        total = arrived if total is None else arrived + plan[7, p].astype(F32) * total
        pref[40 + p] = total.astype(BF16)

    @pl.loop(0, NT)
    def _(t):
        value = spread_of(16, 8 + t).astype(BF16).astype(F32)
        value = value + plan[9, t].astype(F32) * pref[40 + plan[8, t]].astype(F32)
        g2f[t] = value
        pool4[t] = value.astype(BF16)

    job_stage(0, 1)
    gradient(768, [(hid, 0, NT)], [(pool4, 0)])
    job_stage(1, 0)

    @pl.loop(0, NT // GROUP)
    def _(g):
        back = dot_nt(rows_of(pool4, g * GROUP), wo[...]) * rows_of(usl, g * GROUP).astype(F32)
        slope = back.astype(BF16)
        put_rows(pool0, g * GROUP, slope)
        put_rows(g2f, g * GROUP, rows_of(g2f, g * GROUP) + dot_nt(slope, wu[...]))
        put_rows(pool1, g * GROUP, dot_nt(slope, wa[...]).astype(BF16))

    job_stage(0, 2)
    job_stage(1, 1)
    gradient(1280, [(nv, 0, NT)], [(pool0, 0)])
    job_stage(2, 0)
    gradient(1792, [(agg, 0, NT)], [(pool0, 0)])
    job_stage(3, 0)
    job_stage(2, 1)
    outer_edges = NT * (K - 1)
    spread(0, 0, outer_edges // 2, adjw, pool1)
    job_stage(0, 3)
    job_stage(3, 1)
    job_stage(1, 2)
    spread(0, outer_edges // 2, outer_edges, adjw, pool1)

    def message_slope(e):
        key = lax.rem(e + NT, NE)
        mbuf[e] = (spread_of(0, key) * msl[e].astype(F32)).astype(BF16)

    back_to = (north, south, west, east)
    back_has = (has_north, has_south, None, None)
    back_from = (has_south, has_north, None, None)

    def back_copy(d):
        dst = (backns.at[pl.ds(0, 4)], backns.at[pl.ds(4, 4)], redge.at[pl.ds(0, 4)], redge.at[pl.ds(4, 4)])[d]
        return send(usl.at[pl.ds(d * 4, 4)], dst, hg_s.at[d], hg_r.at[d], back_to[d])

    for d in range(4):

        @pl.loop(0, 4)
        def _(b, d=d):
            message_slope(NT + d * 4 + b)

        put_rows(usl, d * 4, dot_nt(rows_of(mbuf, NT + d * 4), wm[...]).astype(BF16))
        when(back_has[d], lambda d=d: back_copy(d).start())

    job_stage(0, 4)
    job_stage(2, 2)
    spread(0, outer_edges, ADJ_EDGES, adjw, pool1)

    @pl.loop(0, NT)
    def _(e):
        message_slope(e)

    job_stage(1, 3)
    job_stage(3, 2)
    left, right = [(nv, 0, NT), (halo, 0, NT)], [(mbuf, 0), (mbuf, NT)]
    gradient(2304, left, right, (0,))
    job_stage(4, 0)
    job_stage(0, 5)
    job_stage(2, 3)
    gradient(2304, left, right, (1,))
    job_stage(5, 0)
    job_stage(4, 1)
    job_stage(3, 3)
    job_stage(1, 4)

    @pl.loop(0, NT // GROUP)
    def _(g):
        put_rows(g2f, g * GROUP, rows_of(g2f, g * GROUP) + dot_nt(rows_of(mbuf, g * GROUP), wm[...]))

    job_stage(5, 1)
    job_stage(0, 6)
    job_stage(2, 4)
    job_stage(4, 2)
    job_stage(3, 4)
    job_stage(1, 5)
    job_stage(5, 2)
    job_stage(2, 5)
    job_stage(4, 3)
    job_stage(3, 5)
    job_stage(5, 3)
    job_stage(1, 6)
    for d in range(4):
        when(back_from[d], lambda d=d: back_copy(d).wait_recv())
    for e in range(8):
        pref[e] = backns[e]
        pref[8 + e] = redge[e]
    job_stage(4, 4)
    job_stage(5, 4)
    total = None
    for p in range(16):
        arrived = pref[plan[11, p]].astype(F32)
        total = arrived if total is None else arrived + plan[12, p].astype(F32) * total
        pref[16 + p] = total.astype(BF16)

    @pl.loop(0, NT)
    def _(t):
        value = g2f[t] + plan[14, t].astype(F32) * pref[16 + plan[13, t]].astype(F32)
        agg[t] = value.astype(BF16)

    lat_out = pltpu.make_async_copy(agg, lat_hbm, out_sem.at[0])
    lat_out.start()
    for stage in range(5, 7):
        for j in (4, 5):
            job_stage(j, stage)
        if stage == 5:
            job_stage(2, 6)
            job_stage(3, 6)
    for j in range(len(JOBS)):
        job_stage(j, 7)
    lat_out.wait()
    for d in range(4):
        when(back_has[d], lambda d=d: back_copy(d).wait_send())


def finish(lat_ref, m_ref, u_ref, a_ref, o_ref, d_ref, h_ref,
           latent_ref, msg_ref, upd_ref, agg_ref, out_ref, dec_ref, head_ref):
    latent_ref[...] = lat_ref[...].astype(F32)
    for src, dst in (
        (m_ref, msg_ref), (u_ref, upd_ref), (a_ref, agg_ref), (o_ref, out_ref), (d_ref, dec_ref), (h_ref, head_ref),
    ):
        dst[:, :HALF] = src[0].astype(F32)
        dst[:, HALF:] = src[1].astype(F32)


def on_device(
    sizes, nodes, send_list, adj_index, adj_weight, dec_send, dec_index, dec_weight, hidden_mask, target,
    w_msg, w_update, w_aggregate, w_output, w_decode, w_head,
):
    n = sizes["n"]
    tiles = lambda count, dtype=BF16: pltpu.VMEM((count, TILE, D), dtype)
    any_spec = pl.BlockSpec(memory_space=pl.ANY)
    smem = pl.BlockSpec(memory_space=pltpu.SMEM)
    scratch = [
        tiles(NT), tiles(NT),
        pltpu.VMEM((NT * K, TILE, TILE), BF16), pltpu.VMEM((NT * KD, TILE, TILE), BF16),
        pltpu.VMEM((NT, OUTC, TILE), BF16),
        *[pltpu.VMEM((D, D), BF16)] * 5, pltpu.VMEM((OUTC, D), BF16),
        tiles(2 * NE), tiles(NE), tiles(NT, F32),
        tiles(NT), tiles(NT), tiles(NT),
        tiles(8), tiles(8), pltpu.VMEM((OUTC, SLOTS * TILE), BF16),
        tiles(NT), tiles(NT), tiles(NE), tiles(NT),
        pltpu.VMEM((TILE, D), F32),
        pltpu.VMEM((GRAD_F32, D), F32),
        pltpu.VMEM((GRAD_ROWS, HALF), BF16), pltpu.VMEM((GRAD_ROWS, HALF), BF16),
        pltpu.VMEM((n - 1, GRAD_ROWS // n, HALF), BF16), pltpu.VMEM((GRAD_ROWS // n, HALF), BF16),
        pltpu.VMEM((n - 1, GRAD_ROWS // n**2, HALF), BF16), pltpu.VMEM((n, GRAD_ROWS // n**2, HALF), BF16),
        tiles(8),
        pltpu.VMEM((24, 128), jnp.int32), pltpu.SMEM((24, 128), jnp.int32),
        pltpu.SemaphoreType.DMA((9 + NT,)), pltpu.SemaphoreType.DMA((2,)), pltpu.SemaphoreType.DMA((1,)),
        *[pltpu.SemaphoreType.DMA((4,))] * 2,
        *[pltpu.SemaphoreType.DMA((2,))] * 4,
        *[pltpu.SemaphoreType.DMA((4,))] * 2,
        *[pltpu.SemaphoreType.DMA((len(JOBS), JOB_SEMS))] * 2,
        pltpu.SemaphoreType.DMA((len(JOBS),)),
    ]
    lat, grads = pl.pallas_call(
        functools.partial(kernel, sizes),
        out_shape=(
            jax.ShapeDtypeStruct((NT, TILE, D), BF16),
            jax.ShapeDtypeStruct((CORES, GRAD_ROWS, HALF), BF16),
        ),
        in_specs=[smem] * 5 + [any_spec] * 10,
        out_specs=(any_spec,) * 2,
        scratch_shapes=scratch,
        compiler_params=pltpu.CompilerParams(
            collective_id=0, has_side_effects=True, vmem_limit_bytes=62 * 1024 * 1024
        ),
        name="mesh_step",
    )(
        send_list, adj_index.transpose(0, 2, 1), dec_send, dec_index.transpose(2, 0, 1), hidden_mask,
        nodes.reshape(NT, TILE, D),
        adj_weight.reshape(NT * K, TILE, TILE),
        dec_weight.reshape(NT * KD, TILE, TILE),
        target.T,
        w_msg, w_update, w_aggregate, w_output, w_decode, w_head.T,
    )
    steps = 8
    block = D // steps

    def rows_spec(at, size=block):
        return pl.BlockSpec((CORES, size, HALF), lambda i: (0, at // size + i, 0))

    latents = pl.BlockSpec((NT // steps, TILE, D), lambda i: (i, 0, 0))
    square = pl.BlockSpec((block, D), lambda i: (i, 0))
    f32 = lambda *shape: jax.ShapeDtypeStruct(shape, F32)
    outs = pl.pallas_call(
        finish,
        out_shape=(f32(NT, TILE, D), *[f32(D, D)] * 5, f32(OUTC, D)),
        grid=(steps,),
        in_specs=[latents, *(rows_spec(at) for at in (2304, 1280, 1792, 768, 0)), rows_spec(512, HALF // steps)],
        out_specs=(latents, *[square] * 5, pl.BlockSpec((HALF // steps, D), lambda i: (i, 0))),
        compiler_params=pltpu.CompilerParams(vmem_limit_bytes=60 * 1024 * 1024),
        name="finish",
    )(lat, grads, grads, grads, grads, grads, grads)
    latent, msg, upd, agg, out, dec, head = outs
    return latent.reshape(NT * TILE, D), msg, upd, agg, out, dec, head.T


def solution(mesh):
    rows, cols = mesh.shape["row"], mesh.shape["col"]
    sizes = dict(axes_of(rows, cols), rows=rows, cols=cols)
    both = ("row", "col")
    return jax.shard_map(
        functools.partial(on_device, sizes),
        mesh=mesh,
        in_specs=(
            P(both, None),
            P(both, None, None),
            P(both, None, None),
            P(both, None, None, None),
            P(both, None, None),
            P(both, None, None),
            P(both, None, None, None),
            P(both, None),
            P(both, None),
            *[P()] * 6,
        ),
        out_specs=(P(both, None), *[P()] * 6),
        check_vma=False,
    )
```

```python
import functools

import jax
import jax.numpy as jnp
from jax import lax
from jax.experimental import pallas as pl
from jax.experimental.pallas import tpu as pltpu
from jax.sharding import PartitionSpec as P

MESH = pl.DeviceIdType.MESH
F32 = jnp.float32
BF16 = jnp.bfloat16

D = 512
OUTC = 227
TILE = 128
NT = 16
NE = 32
NR = 24
K = 4
KD = 3
SLOTS = 12
DEC_EDGES = SLOTS * KD
ADJ_EDGES = NT * K
GROUP = 4
ROWS = GROUP * TILE
CORES = 2

JOBS = (
    (0, 768, ("z", "y", "x")),
    (768, 512, ("z", "x", "y")),
    (1280, 512, ("x", "y", "z")),
    (1792, 512, ("y", "z", "x")),
)
LAST, LAST_ROWS = 2304, 512
GRAD_ROWS = 2816
GRAD_F32 = 2304
HALF = D // 2
JOB_SEMS = 17


def axes_of(rows, cols):
    if (rows, cols) == (8, 16):
        return dict(zh=2, x=4, zl=2, y=4, n=4)
    return dict(zh=1, x=2, zl=2, y=2, n=2)


def dot(a, b):
    return lax.dot_general(a, b, (((1,), (0,)), ((), ())), preferred_element_type=F32)


def dot_nt(a, b):
    return lax.dot_general(a, b, (((1,), (1,)), ((), ())), preferred_element_type=F32)


def dot_tn(a, b):
    return lax.dot_general(a, b, (((0,), (0,)), ((), ())), preferred_element_type=F32)


def sigmoid(v):
    return 0.5 * jnp.tanh(0.5 * v) + 0.5


def rows_of(ref, start, count=GROUP):
    block = ref[pl.ds(start, count)]
    return block.reshape(count * TILE, block.shape[-1])


def put_rows(ref, start, value, count=GROUP):
    ref[pl.ds(start, count)] = value.reshape(count, TILE, value.shape[-1])


def outer_first(value, inner, outer):
    return jnp.where(value >= inner, value - inner, value + outer)


def sort_plan(values, blocks=None, per=1):
    count = len(values)
    depth = -(-count // 8) * 8
    down = lax.broadcasted_iota(jnp.int32, (depth, 128), 0)
    across = lax.broadcasted_iota(jnp.int32, (depth, 128), 1)
    mine = jnp.full((depth, 128), 1000, jnp.int32)
    other = jnp.full((depth, 128), 1000, jnp.int32)
    for q, value in enumerate(values):
        mine = jnp.where(down == q, value, mine)
        other = jnp.where(across == q, value, other)
    same_before = jnp.where((other == mine) & (across < down), 1, 0)
    before = jnp.where(other < mine, 1, 0) + same_before
    rank = jnp.sum(before, axis=1, keepdims=True)
    continues = jnp.minimum(jnp.sum(same_before, axis=1, keepdims=True), 1)
    hit = jnp.where((rank == across) & (down < count), 1, 0)
    order = jnp.sum(hit * down, axis=0, keepdims=True)
    follows = jnp.sum(hit * continues, axis=0, keepdims=True)
    upto = jnp.sum(jnp.where(mine <= across, 1, 0), axis=0, keepdims=True)
    present = jnp.minimum(jnp.sum(jnp.where(mine == across, 1, 0), axis=0, keepdims=True), 1)
    group = {1: down, 3: (down * 43) >> 7, 4: down >> 2}[per]
    group_row = jnp.sum(hit * group, axis=0, keepdims=True)
    named = down
    if blocks is not None:
        for q, value in enumerate(blocks):
            named = jnp.where(down == q, value, named)
    named_row = jnp.sum(hit * named, axis=0, keepdims=True)
    return order, follows, jnp.maximum(upto - 1, 0), present, group_row, named_row


def kernel(
    sizes,
    send_ref, adj_ref, dsend_ref, didx_ref, mask_ref,
    nodes_hbm, adjw_hbm, decw_hbm, target_hbm,
    wm_hbm, wu_hbm, wa_hbm, wo_hbm, wd_hbm, wh_hbm,
    lat_hbm, grads_hbm,
    nv, halo, adjw, decw, target, wm, wu, wa, wo, wd, wh,
    pref, msl, g2f, agg, hid, usl, redge, rgin, err, pool0, pool1, mbuf, pool4, acc,
    gbuf, cs, cr, r1, s2, r2, x4, rl,
    backns, plan_v, plan,
    in_sems, plan_sem, out_sem, halo_s, halo_r, edge_s, edge_r, rg_s, rg_r, hg_s, hg_r, job_s, job_r, job_l, last_s, last_r,
):
    nrow, ncol, nx, ny, nzl = sizes["rows"], sizes["cols"], sizes["x"], sizes["y"], sizes["zl"]
    nzh, n = sizes["zh"], sizes["n"]
    r = lax.axis_index("row")
    c = lax.axis_index("col")
    zh, x = lax.div(r, nx), lax.rem(r, nx)
    zl = lax.div(c, ny * CORES)
    y = lax.rem(lax.div(c, CORES), ny)
    core = lax.rem(c, CORES)
    z = zh * nzl + zl
    place = {"x": x, "y": y, "z": z}

    def peer(axis, step):
        there = lax.rem(place[axis] + step, n)
        if axis == "x":
            return (zh * nx + there, c), there
        if axis == "y":
            return (r, (zl * ny + there) * CORES + core), there
        return (lax.div(there, nzl) * nx + x, (lax.rem(there, nzl) * ny + y) * CORES + core), there

    def plane_peer(step):
        there = lax.rem(x * n + y + step, n * n)
        return (zh * nx + lax.div(there, n), (zl * ny + lax.rem(there, n)) * CORES + core), there

    mate = (r, c + 1 - 2 * core)
    west = (r, lax.rem(c + ncol - 1, ncol))
    east = (r, lax.rem(c + 1, ncol))
    north = (r - 1, c)
    south = (r + 1, c)
    has_north = r > 0
    has_south = r < nrow - 1

    loads = [
        pltpu.make_async_copy(src, dst, in_sems.at[i])
        for i, (src, dst) in enumerate(
            (
                (nodes_hbm, nv), (wm_hbm, wm), (wu_hbm, wu), (adjw_hbm, adjw), (wa_hbm, wa), (wo_hbm, wo),
                (decw_hbm, decw), (wd_hbm, wd), (wh_hbm, wh),
                *((target_hbm.at[:, pl.ds(g * TILE, TILE)], target.at[g]) for g in range(NT)),
            )
        )
    ]
    for load in loads[:3]:
        load.start()

    barrier = pltpu.get_barrier_semaphore()

    def greet(device):
        pl.semaphore_signal(barrier, inc=1, device_id=device, device_id_type=MESH)

    greet(west)
    greet(east)
    for step in range(1, n):
        greet(peer("z", step)[0])
    for step in range(1, n * n):
        greet(plane_peer(step)[0])
    greeted = 2 + (n - 1) + (n * n - 1)

    @pl.when(has_north)
    def _():
        greet(north)

    @pl.when(has_south)
    def _():
        greet(south)

    extra = jnp.where(has_north, 1, 0) + jnp.where(has_south, 1, 0)

    def send(src, dst, ssem, rsem, device):
        return pltpu.make_async_remote_copy(
            src_ref=src, dst_ref=dst, send_sem=ssem, recv_sem=rsem, device_id=device, device_id_type=MESH
        )

    loads[0].wait()
    for d in range(4):
        for b in range(4):
            pool1[d * 4 + b] = nv[send_ref[0, d, b]]
    pl.semaphore_wait(barrier, greeted + extra)

    halo_to = (south, north, east, west)
    halo_has = (has_south, has_north, None, None)
    from_has = (has_north, has_south, None, None)
    no_from = (jnp.logical_not(has_north), jnp.logical_not(has_south))

    def when(condition, body):
        if condition is None:
            body()
        else:
            pl.when(condition)(body)

    def halo_copy(d):
        part = pl.ds(d * 4, 4)
        return send(pool1.at[part], halo.at[part], halo_s.at[d], halo_r.at[d], halo_to[d])

    for d in range(4):
        when(halo_has[d], lambda d=d: halo_copy(d).start())
    for load in loads[3:]:
        load.start()

    for d in range(2):

        @pl.when(no_from[d])
        def _(d=d):
            halo[pl.ds(d * 4, 4)] = jnp.zeros((4, TILE, D), BF16)
            backns[pl.ds(4 - d * 4, 4)] = jnp.zeros((4, TILE, D), BF16)

    def messages(xs, at):
        pre = dot(xs, wm[...])
        s = sigmoid(pre)
        put_rows(pref, NE + at, (pre * s).astype(BF16))
        put_rows(msl, at, (s * (1.0 + pre * (1.0 - s))).astype(BF16))

    loads[1].wait()
    loads[2].wait()

    @pl.loop(0, NT // GROUP)
    def _(g):
        xs = rows_of(nv, g * GROUP)
        messages(xs, g * GROUP)
        put_rows(g2f, g * GROUP, dot(xs, wu[...]))

    def write_plan(at, rows):
        for i, row in enumerate(rows):
            plan_v[at + i : at + i + 1, :] = row

    write_plan(0, sort_plan([outer_first(adj_ref[0, k, t], NT, NT) for t in range(NT) for k in range(K)], per=K))
    write_plan(6, sort_plan([dsend_ref[0, d, s] for d in range(2) for s in range(4)])[:4])
    write_plan(10, sort_plan([1 - mask_ref[0, g] for g in range(NT)])[:1])
    write_plan(11, sort_plan([send_ref[0, d, b] for d in range(4) for b in range(4)])[:4])
    first = pltpu.make_async_copy(plan_v.at[pl.ds(0, 16)], plan.at[pl.ds(0, 16)], plan_sem.at[0])
    first.start()
    first.wait()
    hidden = [plan[10, s] for s in range(SLOTS)]
    edge_list = [(hidden[s], k) for s in range(SLOTS) for k in range(KD)]
    write_plan(16, sort_plan([outer_first(didx_ref[k, 0, g], NT, 8) for g, k in edge_list], [g * KD + k for g, k in edge_list], KD))
    second = pltpu.make_async_copy(plan_v.at[pl.ds(16, 8)], plan.at[pl.ds(16, 8)], plan_sem.at[1])
    second.start()
    second.wait()

    for d in (3, 2, 0, 1):
        when(from_has[d], lambda d=d: halo_copy(d).wait_recv())
        messages(rows_of(halo, d * 4), NT + d * 4)

    for i in (3, 4, 5):
        loads[i].wait()

    @pl.loop(0, NT // GROUP)
    def _(g):
        for i in range(GROUP):
            t = g * GROUP + i
            weights = jnp.concatenate([adjw[t * K + k] for k in range(K)], axis=1)
            picked = jnp.concatenate(
                [pref[NE + t], pref[NE + NT + t], pref[NE + adj_ref[0, 2, t]], pref[NE + adj_ref[0, 3, t]]], axis=0
            )
            agg[t] = dot(weights, picked).astype(BF16)
        upre = rows_of(g2f, g * GROUP) + dot(rows_of(agg, g * GROUP), wa[...])
        s = sigmoid(upre)
        hidden_rows = (upre * s).astype(BF16)
        put_rows(hid, g * GROUP, hidden_rows)
        put_rows(usl, g * GROUP, (s * (1.0 + upre * (1.0 - s))).astype(BF16))
        v2 = rows_of(nv, g * GROUP).astype(F32) + dot(hidden_rows, wo[...])
        put_rows(pref, g * GROUP, v2.astype(BF16))

    for d in range(4):
        when(halo_has[d], lambda d=d: halo_copy(d).wait_send())
    for d in range(2):
        for s in range(4):
            pref[NE + d * 4 + s] = pref[dsend_ref[0, d, s]]
    edges = [
        send(pref.at[pl.ds(NE, 4)], redge.at[pl.ds(4, 4)], edge_s.at[0], edge_r.at[0], west),
        send(pref.at[pl.ds(NE + 4, 4)], redge.at[pl.ds(0, 4)], edge_s.at[1], edge_r.at[1], east),
    ]
    for edge in edges:
        edge.start()
    for load in loads[6:]:
        load.wait()
    for edge in edges:
        edge.wait()
    for e in range(8):
        pref[NT + e] = redge[e]

    @pl.loop(0, SLOTS // GROUP)
    def _(g):
        goals, marks = [], []
        for i in range(GROUP):
            s = g * GROUP + i
            block = plan[10, s]
            weights = jnp.concatenate([decw[block * KD + k] for k in range(KD)], axis=1)
            picked = jnp.concatenate([pref[didx_ref[k, 0, block]] for k in range(KD)], axis=0)
            pool0[s] = dot(weights, picked).astype(BF16)
            goals.append(target[block].astype(F32))
            marks.append(jnp.full((1, TILE), mask_ref[0, block].astype(F32), F32))
        dpre = dot(rows_of(pool0, g * GROUP), wd[...])
        s = sigmoid(dpre)
        q = (dpre * s).astype(BF16)
        put_rows(pool1, g * GROUP, q)
        slope = s * (1.0 + dpre * (1.0 - s))
        residual = dot_nt(wh[...], q) - jnp.concatenate(goals, axis=1)
        residual = (jnp.concatenate(marks, axis=1) * residual).astype(BF16)
        err[:, pl.ds(pl.multiple_of(g * ROWS, ROWS), ROWS)] = residual
        dslope = (dot_tn(residual, wh[...]) * slope).astype(BF16)
        put_rows(mbuf, g * GROUP, dslope)
        put_rows(pool4, g * GROUP, dot_nt(dslope, wd[...]).astype(BF16))

    def spread(at, first_edge, last_edge, weight, source):
        if first_edge == 0:
            acc[...] = jnp.zeros((TILE, D), F32)

        @pl.loop(first_edge // GROUP, last_edge // GROUP)
        def _(h):
            total = acc[...]
            for i in range(GROUP):
                p = h * GROUP + i
                total = dot_tn(weight[plan[at + 5, p]], source[plan[at + 4, p]]) + plan[at + 1, p].astype(F32) * total
                pref[p] = total.astype(BF16)
            acc[...] = total

    def spread_of(at, tile):
        return plan[at + 3, tile].astype(F32) * pref[plan[at + 2, tile]].astype(F32)

    spread(16, 0, SLOTS * (KD - 1), decw, pool4)
    for e in range(8):
        pref[48 + e] = spread_of(16, e).astype(BF16)
    returns = [
        send(pref.at[pl.ds(48, 4)], rgin.at[pl.ds(4, 4)], rg_s.at[0], rg_r.at[0], west),
        send(pref.at[pl.ds(52, 4)], rgin.at[pl.ds(0, 4)], rg_s.at[1], rg_r.at[1], east),
    ]
    for item in returns:
        item.start()
    spread(16, SLOTS * (KD - 1), DEC_EDGES, decw, pool4)

    def job_copy(j, sem, src, dst, device):
        return send(src, dst, job_s.at[j, sem], job_r.at[j, sem], device)

    def c_copy(j):
        at, rows, _ = JOBS[j]
        return job_copy(j, 0, cs.at[pl.ds(at, rows)], cr.at[pl.ds(at, rows)], mate)

    def first_copies(j):
        at, rows, order = JOBS[j]
        quarter = rows // n
        out = []
        for step in range(1, n):
            device, there = peer(order[0], step)
            src = cs.at[pl.ds(pl.multiple_of(at + there * quarter, 16), quarter)]
            out.append(job_copy(j, step, src, r1.at[step - 1, pl.ds(at // n, quarter)], device))
        return out

    def second_copies(j):
        at, rows, order = JOBS[j]
        small = rows // (n * n)
        out = []
        for step in range(1, n):
            device, there = peer(order[1], step)
            src = s2.at[pl.ds(pl.multiple_of(at // n + there * small, 16), small)]
            out.append(job_copy(j, 3 + step, src, r2.at[step - 1, pl.ds(at // (n * n), small)], device))
        return out

    def third_copies(j):
        at, rows, order = JOBS[j]
        small = rows // (n * n)
        out = []
        for step in range(1, n):
            device, _ = peer(order[2], step)
            mine = x4.at[place[order[2]], pl.ds(at // (n * n), small)]
            out.append(job_copy(j, 6 + step, mine, mine, device))
        return out

    def small_at(j):
        at, rows, order = JOBS[j]
        quarter, small = rows // n, rows // (n * n)
        return pl.multiple_of(at + place[order[0]] * quarter + place[order[1]] * small, 16)

    def back_small(j):
        at, rows, order = JOBS[j]
        part = cr.at[pl.ds(small_at(j), rows // (n * n))]
        return [
            job_copy(j, 9 + step, part, part, peer(order[1], step)[0]) for step in range(1, n)
        ]

    def back_quarter(j):
        at, rows, order = JOBS[j]
        quarter = rows // n
        part = cr.at[pl.ds(pl.multiple_of(at + place[order[0]] * quarter, 16), quarter)]
        return [
            job_copy(j, 12 + step, part, part, peer(order[0], step)[0]) for step in range(1, n)
        ]

    def back_core(j):
        at, rows, _ = JOBS[j]
        part = pl.ds(at, rows)
        return (
            job_copy(j, 16, cr.at[part], grads_hbm.at[core, part], mate),
            pltpu.make_async_copy(cr.at[part], grads_hbm.at[core, part], job_l.at[j]),
        )

    def job_stage(j, stage_number):
        at, rows, order = JOBS[j]
        quarter, small = rows // n, rows // (n * n)
        whole = pl.ds(at, rows)
        own = pl.ds(at % GRAD_F32, rows)
        if stage_number == 0:
            low, high = gbuf[own, :HALF], gbuf[own, HALF:]
            cs[whole] = jnp.where(core == 0, high, low).astype(BF16)
            c_copy(j).start()
        elif stage_number == 1:
            c_copy(j).wait()
            low, high = gbuf[own, :HALF], gbuf[own, HALF:]
            cs[whole] = (jnp.where(core == 0, low, high) + cr[whole].astype(F32)).astype(BF16)
            for item in first_copies(j):
                item.start()
        elif stage_number == 2:
            mine = pl.ds(pl.multiple_of(at + place[order[0]] * quarter, 16), quarter)
            for item in first_copies(j):
                item.wait()
            total = cs[mine].astype(F32)
            for step in range(n - 1):
                total = total + r1[step, pl.ds(at // n, quarter)].astype(F32)
            s2[pl.ds(at // n, quarter)] = total.astype(BF16)
            for item in second_copies(j):
                item.start()
        elif stage_number == 3:
            mine = pl.ds(pl.multiple_of(at // n + place[order[1]] * small, 16), small)
            for item in second_copies(j):
                item.wait()
            total = s2[mine].astype(F32)
            for step in range(n - 1):
                total = total + r2[step, pl.ds(at // (n * n), small)].astype(F32)
            x4[place[order[2]], pl.ds(at // (n * n), small)] = total.astype(BF16)
            for item in third_copies(j):
                item.start()
        elif stage_number == 4:
            for item in third_copies(j):
                item.wait()
            total = x4[0, pl.ds(at // (n * n), small)].astype(F32)
            for other in range(1, n):
                total = total + x4[other, pl.ds(at // (n * n), small)].astype(F32)
            cr[pl.ds(small_at(j), small)] = (total * (1.0 / (nrow * ncol))).astype(BF16)
            for item in back_small(j):
                item.start()
        elif stage_number == 5:
            for item in back_small(j):
                item.wait()
            for item in back_quarter(j):
                item.start()
        elif stage_number == 6:
            for item in back_quarter(j):
                item.wait()
            for item in back_core(j):
                item.start()
        else:
            for item in back_core(j):
                item.wait()

    chunk = LAST_ROWS // (n * n)
    last_mine = pl.ds(pl.multiple_of(LAST + (x * n + y) * chunk, 16), chunk)
    last_place = pl.ds(LAST // (n * n), chunk)

    def last_copy(sem, src, dst, device):
        return send(src, dst, last_s.at[sem], last_r.at[sem], device)

    def last_core():
        return last_copy(0, cs.at[pl.ds(LAST, LAST_ROWS)], cr.at[pl.ds(LAST, LAST_ROWS)], mate)

    def last_scatter():
        out = []
        for step in range(1, n * n):
            device, there = plane_peer(step)
            src = cs.at[pl.ds(pl.multiple_of(LAST + there * chunk, 16), chunk)]
            out.append(last_copy(step, src, rl.at[step - 1], device))
        return out

    def last_exchange():
        mine = x4.at[z, last_place]
        return [last_copy(n * n + step, mine, mine, peer("z", step)[0]) for step in range(1, n)]

    def last_gather():
        part = cr.at[last_mine]
        return [last_copy(n * n + n + step, part, part, plane_peer(step)[0]) for step in range(1, n * n)]

    def last_back():
        part = pl.ds(LAST, LAST_ROWS)
        return (
            last_copy(n * n, cr.at[part], grads_hbm.at[core, part], mate),
            pltpu.make_async_copy(cr.at[part], grads_hbm.at[core, part], job_l.at[len(JOBS)]),
        )

    def last_stage(stage_number):
        whole = pl.ds(LAST, LAST_ROWS)
        if stage_number == 0:
            low, high = gbuf[:LAST_ROWS, :HALF], gbuf[:LAST_ROWS, HALF:]
            cs[whole] = jnp.where(core == 0, high, low).astype(BF16)
            last_core().start()
        elif stage_number == 1:
            last_core().wait()
            low, high = gbuf[:LAST_ROWS, :HALF], gbuf[:LAST_ROWS, HALF:]
            cs[whole] = (jnp.where(core == 0, low, high) + cr[whole].astype(F32)).astype(BF16)
            for item in last_scatter():
                item.start()
        elif stage_number == 2:
            for item in last_scatter():
                item.wait()
            total = cs[last_mine].astype(F32)
            for step in range(n * n - 1):
                total = total + rl[step].astype(F32)
            x4[z, last_place] = total.astype(BF16)
            for item in last_exchange():
                item.start()
        elif stage_number == 3:
            for item in last_exchange():
                item.wait()
            total = x4[0, last_place].astype(F32)
            for other in range(1, n):
                total = total + x4[other, last_place].astype(F32)
            cr[last_mine] = (total * (1.0 / (nrow * ncol))).astype(BF16)
            for item in last_gather():
                item.start()
        elif stage_number == 4:
            for item in last_gather():
                item.wait()
            for item in last_back():
                item.start()
        else:
            for item in last_back():
                item.wait()

    def gradient(at, left, right, halves=(0, 1)):
        for half in halves:
            lanes = slice(half * HALF, (half + 1) * HALF)
            total = None
            for (lref, lat, count), (rref, rat) in zip(left, right):
                lhs = lref[pl.ds(lat, count), :, lanes].reshape(count * TILE, HALF)
                term = dot_tn(lhs, rows_of(rref, rat, count))
                total = term if total is None else total + term
            gbuf[pl.ds(at % GRAD_F32 + half * HALF, HALF)] = total

    gradient(0, [(pool0, 0, SLOTS)], [(mbuf, 0)])
    q_rows = pool1[pl.ds(0, SLOTS)].reshape(SLOTS * TILE, D)
    gbuf[512:768, :] = jnp.zeros((256, D), F32)
    gbuf[512 : 512 + OUTC, :] = dot(err[...], q_rows)
    job_stage(0, 0)

    for item in returns:
        item.wait()
    total = None
    for p in range(8):
        arrived = rgin[plan[6, p]].astype(F32)
        total = arrived if total is None else arrived + plan[7, p].astype(F32) * total
        pref[40 + p] = total.astype(BF16)

    @pl.loop(0, NT)
    def _(t):
        value = spread_of(16, 8 + t).astype(BF16).astype(F32)
        value = value + plan[9, t].astype(F32) * pref[40 + plan[8, t]].astype(F32)
        g2f[t] = value
        pool4[t] = value.astype(BF16)

    job_stage(0, 1)
    gradient(768, [(hid, 0, NT)], [(pool4, 0)])
    job_stage(1, 0)

    @pl.loop(0, NT // GROUP)
    def _(g):
        back = dot_nt(rows_of(pool4, g * GROUP), wo[...]) * rows_of(usl, g * GROUP).astype(F32)
        slope = back.astype(BF16)
        put_rows(pool0, g * GROUP, slope)
        put_rows(g2f, g * GROUP, rows_of(g2f, g * GROUP) + dot_nt(slope, wu[...]))
        put_rows(pool1, g * GROUP, dot_nt(slope, wa[...]).astype(BF16))

    gradient(1280, [(nv, 0, NT)], [(pool0, 0)])
    job_stage(2, 0)
    job_stage(1, 1)
    gradient(1792, [(agg, 0, NT)], [(pool0, 0)])
    job_stage(3, 0)
    job_stage(0, 2)
    outer_edges = NT * (K - 1)
    spread(0, 0, outer_edges // 2, adjw, pool1)
    job_stage(2, 1)
    job_stage(3, 1)
    spread(0, outer_edges // 2, outer_edges, adjw, pool1)

    def message_slope(e):
        key = lax.rem(e + NT, NE)
        mbuf[e] = (spread_of(0, key) * msl[e].astype(F32)).astype(BF16)

    back_to = (north, south, west, east)
    back_has = (has_north, has_south, None, None)
    back_from = (has_south, has_north, None, None)

    def back_copy(d):
        dst = (backns.at[pl.ds(0, 4)], backns.at[pl.ds(4, 4)], redge.at[pl.ds(0, 4)], redge.at[pl.ds(4, 4)])[d]
        return send(usl.at[pl.ds(d * 4, 4)], dst, hg_s.at[d], hg_r.at[d], back_to[d])

    for d in range(4):

        @pl.loop(0, 4)
        def _(b, d=d):
            message_slope(NT + d * 4 + b)

        put_rows(usl, d * 4, dot_nt(rows_of(mbuf, NT + d * 4), wm[...]).astype(BF16))
        when(back_has[d], lambda d=d: back_copy(d).start())

    spread(0, outer_edges, ADJ_EDGES, adjw, pool1)

    @pl.loop(0, NT)
    def _(e):
        message_slope(e)

    left, right = [(nv, 0, NT), (halo, 0, NT)], [(mbuf, 0), (mbuf, NT)]
    gradient(LAST, left, right)
    last_stage(0)
    job_stage(0, 3)
    job_stage(1, 2)
    last_stage(1)
    job_stage(2, 2)
    job_stage(3, 2)

    @pl.loop(0, NT // GROUP)
    def _(g):
        put_rows(g2f, g * GROUP, rows_of(g2f, g * GROUP) + dot_nt(rows_of(mbuf, g * GROUP), wm[...]))

    job_stage(1, 3)
    job_stage(0, 4)
    last_stage(2)
    job_stage(2, 3)
    job_stage(3, 3)
    job_stage(1, 4)
    job_stage(0, 5)
    last_stage(3)
    job_stage(2, 4)
    job_stage(3, 4)
    job_stage(1, 5)
    job_stage(0, 6)
    job_stage(2, 5)
    job_stage(3, 5)
    job_stage(1, 6)
    last_stage(4)
    job_stage(2, 6)
    job_stage(3, 6)
    for d in range(4):
        when(back_from[d], lambda d=d: back_copy(d).wait_recv())
    for e in range(8):
        pref[e] = backns[e]
        pref[8 + e] = redge[e]
    total = None
    for p in range(16):
        arrived = pref[plan[11, p]].astype(F32)
        total = arrived if total is None else arrived + plan[12, p].astype(F32) * total
        pref[16 + p] = total.astype(BF16)

    @pl.loop(0, NT)
    def _(t):
        value = g2f[t] + plan[14, t].astype(F32) * pref[16 + plan[13, t]].astype(F32)
        agg[t] = value.astype(BF16)

    lat_out = pltpu.make_async_copy(agg, lat_hbm, out_sem.at[0])
    lat_out.start()
    for j in range(len(JOBS)):
        job_stage(j, 7)
    last_stage(5)
    lat_out.wait()
    for d in range(4):
        when(back_has[d], lambda d=d: back_copy(d).wait_send())


SQUARES = (2304, 1280, 1792, 768, 0)
LAT_PARTS = 4


def finish(lat_hbm, grads_hbm, latent_hbm, msg_hbm, upd_hbm, agg_hbm, out_hbm, dec_hbm, head_hbm,
           lat, grads, latent, squares, head, in_sems, out_sems):
    per = NT // LAT_PARTS
    parts = [pl.ds(i * per, per) for i in range(LAT_PARTS)]
    loads = [pltpu.make_async_copy(lat_hbm.at[part], lat.at[part], in_sems.at[i]) for i, part in enumerate(parts)]
    for i, (at, rows) in enumerate([(at, D) for at in SQUARES] + [(D, HALF)]):
        part = pl.ds(at, rows)
        loads.append(pltpu.make_async_copy(grads_hbm.at[:, part], grads.at[:, part], in_sems.at[LAT_PARTS + i]))
    for load in loads:
        load.start()
    stores = []

    def store(src, dst):
        stores.append(pltpu.make_async_copy(src, dst, out_sems.at[len(stores)]))
        stores[-1].start()

    for i, part in enumerate(parts):
        loads[i].wait()
        latent[part] = lat[part].astype(F32)
        store(latent.at[part], latent_hbm.at[part])
    for i, (at, dst) in enumerate(zip(SQUARES, (msg_hbm, upd_hbm, agg_hbm, out_hbm, dec_hbm))):
        loads[LAT_PARTS + i].wait()
        for half in range(2):
            squares[i, :, half * HALF : (half + 1) * HALF] = grads[half, at : at + D].astype(F32)
        store(squares.at[i], dst)
    loads[-1].wait()
    for half in range(2):
        head[:, half * HALF : (half + 1) * HALF] = grads[half, D : D + HALF].astype(F32)[:OUTC]
    store(head, head_hbm)
    for item in stores:
        item.wait()


def on_device(
    sizes, nodes, send_list, adj_index, adj_weight, dec_send, dec_index, dec_weight, hidden_mask, target,
    w_msg, w_update, w_aggregate, w_output, w_decode, w_head,
):
    n = sizes["n"]
    tiles = lambda count, dtype=BF16: pltpu.VMEM((count, TILE, D), dtype)
    any_spec = pl.BlockSpec(memory_space=pl.ANY)
    smem = pl.BlockSpec(memory_space=pltpu.SMEM)
    scratch = [
        tiles(NT), tiles(NT),
        pltpu.VMEM((NT * K, TILE, TILE), BF16), pltpu.VMEM((NT * KD, TILE, TILE), BF16),
        pltpu.VMEM((NT, OUTC, TILE), BF16),
        *[pltpu.VMEM((D, D), BF16)] * 5, pltpu.VMEM((OUTC, D), BF16),
        tiles(2 * NE), tiles(NE), tiles(NT, F32),
        tiles(NT), tiles(NT), tiles(NT),
        tiles(8), tiles(8), pltpu.VMEM((OUTC, SLOTS * TILE), BF16),
        tiles(NT), tiles(NT), tiles(NE), tiles(NT),
        pltpu.VMEM((TILE, D), F32),
        pltpu.VMEM((GRAD_F32, D), F32),
        pltpu.VMEM((GRAD_ROWS, HALF), BF16), pltpu.VMEM((GRAD_ROWS, HALF), BF16),
        pltpu.VMEM((n - 1, LAST // n, HALF), BF16), pltpu.VMEM((LAST // n, HALF), BF16),
        pltpu.VMEM((n - 1, LAST // n**2, HALF), BF16), pltpu.VMEM((n, GRAD_ROWS // n**2, HALF), BF16),
        pltpu.VMEM((n * n - 1, LAST_ROWS // n**2, HALF), BF16),
        tiles(8),
        pltpu.VMEM((24, 128), jnp.int32), pltpu.SMEM((24, 128), jnp.int32),
        pltpu.SemaphoreType.DMA((9 + NT,)), pltpu.SemaphoreType.DMA((2,)), pltpu.SemaphoreType.DMA((1,)),
        *[pltpu.SemaphoreType.DMA((4,))] * 2,
        *[pltpu.SemaphoreType.DMA((2,))] * 4,
        *[pltpu.SemaphoreType.DMA((4,))] * 2,
        *[pltpu.SemaphoreType.DMA((len(JOBS), JOB_SEMS))] * 2,
        pltpu.SemaphoreType.DMA((len(JOBS) + 1,)),
        *[pltpu.SemaphoreType.DMA((2 * n * n + n,))] * 2,
    ]
    lat, grads = pl.pallas_call(
        functools.partial(kernel, sizes),
        out_shape=(
            jax.ShapeDtypeStruct((NT, TILE, D), BF16),
            jax.ShapeDtypeStruct((CORES, GRAD_ROWS, HALF), BF16),
        ),
        in_specs=[smem] * 5 + [any_spec] * 10,
        out_specs=(any_spec,) * 2,
        scratch_shapes=scratch,
        compiler_params=pltpu.CompilerParams(
            collective_id=0, has_side_effects=True, vmem_limit_bytes=62 * 1024 * 1024
        ),
        name="mesh_step",
    )(
        send_list, adj_index.transpose(0, 2, 1), dec_send, dec_index.transpose(2, 0, 1), hidden_mask,
        nodes.reshape(NT, TILE, D),
        adj_weight.reshape(NT * K, TILE, TILE),
        dec_weight.reshape(NT * KD, TILE, TILE),
        target.T,
        w_msg, w_update, w_aggregate, w_output, w_decode, w_head.T,
    )
    f32 = lambda *shape: jax.ShapeDtypeStruct(shape, F32)
    outs = pl.pallas_call(
        finish,
        out_shape=(f32(NT, TILE, D), *[f32(D, D)] * 5, f32(OUTC, D)),
        in_specs=[any_spec] * 2,
        out_specs=(any_spec,) * 7,
        scratch_shapes=[
            tiles(NT), pltpu.VMEM((CORES, GRAD_ROWS, HALF), BF16),
            tiles(NT, F32), pltpu.VMEM((5, D, D), F32), pltpu.VMEM((OUTC, D), F32),
            pltpu.SemaphoreType.DMA((LAT_PARTS + 6,)), pltpu.SemaphoreType.DMA((LAT_PARTS + 6,)),
        ],
        compiler_params=pltpu.CompilerParams(vmem_limit_bytes=60 * 1024 * 1024),
        name="finish",
    )(lat, grads)
    latent, msg, upd, agg, out, dec, head = outs
    return latent.reshape(NT * TILE, D), msg, upd, agg, out, dec, head.T


def solution(mesh):
    rows, cols = mesh.shape["row"], mesh.shape["col"]
    sizes = dict(axes_of(rows, cols), rows=rows, cols=cols)
    both = ("row", "col")
    return jax.shard_map(
        functools.partial(on_device, sizes),
        mesh=mesh,
        in_specs=(
            P(both, None),
            P(both, None, None),
            P(both, None, None),
            P(both, None, None, None),
            P(both, None, None),
            P(both, None, None),
            P(both, None, None, None),
            P(both, None),
            P(both, None),
            *[P()] * 6,
        ),
        out_specs=(P(both, None), *[P()] * 6),
        check_vma=False,
    )
```

```python
import functools

import jax
import jax.numpy as jnp
from jax import lax
from jax.experimental import pallas as pl
from jax.experimental.pallas import tpu as pltpu
from jax.sharding import PartitionSpec as P

MESH = pl.DeviceIdType.MESH
F32 = jnp.float32
BF16 = jnp.bfloat16

D = 512
OUTC = 227
TILE = 128
NT = 16
NE = 32
NR = 24
K = 4
KD = 3
SLOTS = 12
DEC_EDGES = SLOTS * KD
ADJ_EDGES = NT * K
GROUP = 4
ROWS = GROUP * TILE
CORES = 2

JOBS = (
    (0, 768, ("x", "y"), "z"),
    (768, 1536, ("y", "z"), "x"),
    (2304, 512, ("x", "y"), "z"),
)
GRAD_ROWS = 2816
GRAD_F32 = 2304
HALF = D // 2


def axes_of(rows, cols):
    if (rows, cols) == (8, 16):
        return dict(zh=2, x=4, zl=2, y=4, n=4)
    return dict(zh=1, x=2, zl=2, y=2, n=2)


def dot(a, b):
    return lax.dot_general(a, b, (((1,), (0,)), ((), ())), preferred_element_type=F32)


def dot_nt(a, b):
    return lax.dot_general(a, b, (((1,), (1,)), ((), ())), preferred_element_type=F32)


def dot_tn(a, b):
    return lax.dot_general(a, b, (((0,), (0,)), ((), ())), preferred_element_type=F32)


def sigmoid(v):
    return 0.5 * jnp.tanh(0.5 * v) + 0.5


def rows_of(ref, start, count=GROUP):
    block = ref[pl.ds(start, count)]
    return block.reshape(count * TILE, block.shape[-1])


def put_rows(ref, start, value, count=GROUP):
    ref[pl.ds(start, count)] = value.reshape(count, TILE, value.shape[-1])


def outer_first(value, inner, outer):
    return jnp.where(value >= inner, value - inner, value + outer)


def sort_plan(values, blocks=None, per=1):
    count = len(values)
    depth = -(-count // 8) * 8
    down = lax.broadcasted_iota(jnp.int32, (depth, 128), 0)
    across = lax.broadcasted_iota(jnp.int32, (depth, 128), 1)
    mine = jnp.full((depth, 128), 1000, jnp.int32)
    other = jnp.full((depth, 128), 1000, jnp.int32)
    for q, value in enumerate(values):
        mine = jnp.where(down == q, value, mine)
        other = jnp.where(across == q, value, other)
    same_before = jnp.where((other == mine) & (across < down), 1, 0)
    before = jnp.where(other < mine, 1, 0) + same_before
    rank = jnp.sum(before, axis=1, keepdims=True)
    continues = jnp.minimum(jnp.sum(same_before, axis=1, keepdims=True), 1)
    hit = jnp.where((rank == across) & (down < count), 1, 0)
    order = jnp.sum(hit * down, axis=0, keepdims=True)
    follows = jnp.sum(hit * continues, axis=0, keepdims=True)
    upto = jnp.sum(jnp.where(mine <= across, 1, 0), axis=0, keepdims=True)
    present = jnp.minimum(jnp.sum(jnp.where(mine == across, 1, 0), axis=0, keepdims=True), 1)
    group = {1: down, 3: (down * 43) >> 7, 4: down >> 2}[per]
    group_row = jnp.sum(hit * group, axis=0, keepdims=True)
    named = down
    if blocks is not None:
        for q, value in enumerate(blocks):
            named = jnp.where(down == q, value, named)
    named_row = jnp.sum(hit * named, axis=0, keepdims=True)
    return order, follows, jnp.maximum(upto - 1, 0), present, group_row, named_row


def kernel(
    sizes,
    send_ref, adj_ref, dsend_ref, didx_ref, mask_ref,
    nodes_hbm, adjw_hbm, decw_hbm, target_hbm,
    wm_hbm, wu_hbm, wa_hbm, wo_hbm, wd_hbm, wh_hbm,
    lat_hbm, grads_hbm,
    nv, halo, adjw, decw, target, wm, wu, wa, wo, wd, wh,
    pref, msl, g2f, agg, hid, usl, redge, rgin, err, pool0, pool1, mbuf, pool4, acc,
    gbuf, cs, cr, r1, x4,
    backns, plan_v, plan,
    in_sems, plan_sem, out_sem, halo_s, halo_r, edge_s, edge_r, rg_s, rg_r, hg_s, hg_r, job_s, job_r, job_l,
):
    nrow, ncol, nx, ny, nzl = sizes["rows"], sizes["cols"], sizes["x"], sizes["y"], sizes["zl"]
    nzh, n = sizes["zh"], sizes["n"]
    r = lax.axis_index("row")
    c = lax.axis_index("col")
    zh, x = lax.div(r, nx), lax.rem(r, nx)
    zl = lax.div(c, ny * CORES)
    y = lax.rem(lax.div(c, CORES), ny)
    core = lax.rem(c, CORES)
    z = zh * nzl + zl
    place = {"x": x, "y": y, "z": z}

    def device_at(**moved):
        at = {**place, **moved}
        zhi, zlo = lax.div(at["z"], nzl), lax.rem(at["z"], nzl)
        return (zhi * nx + at["x"], (zlo * ny + at["y"]) * CORES + core)

    def line_peer(axis, step):
        return device_at(**{axis: lax.rem(place[axis] + step, n)})

    def plane_peer(axes, step):
        a, b = axes
        there = lax.rem(place[a] * n + place[b] + step, n * n)
        return device_at(**{a: lax.div(there, n), b: lax.rem(there, n)}), there

    mate = (r, c + 1 - 2 * core)
    west = (r, lax.rem(c + ncol - 1, ncol))
    east = (r, lax.rem(c + 1, ncol))
    north = (r - 1, c)
    south = (r + 1, c)
    has_north = r > 0
    has_south = r < nrow - 1

    loads = [
        pltpu.make_async_copy(src, dst, in_sems.at[i])
        for i, (src, dst) in enumerate(
            (
                (nodes_hbm, nv), (wm_hbm, wm), (wu_hbm, wu), (adjw_hbm, adjw), (wa_hbm, wa), (wo_hbm, wo),
                (decw_hbm, decw), (wd_hbm, wd), (wh_hbm, wh),
                *((target_hbm.at[:, pl.ds(g * TILE, TILE)], target.at[g]) for g in range(NT)),
            )
        )
    ]
    for load in loads[:3]:
        load.start()

    barrier = pltpu.get_barrier_semaphore()

    def greet(device):
        pl.semaphore_signal(barrier, inc=1, device_id=device, device_id_type=MESH)

    greet(west)
    greet(east)
    planes = (("x", "y"), ("y", "z"))
    for axes in planes:
        for step in range(1, n * n):
            greet(plane_peer(axes, step)[0])
    greeted = 2 + len(planes) * (n * n - 1)

    @pl.when(has_north)
    def _():
        greet(north)

    @pl.when(has_south)
    def _():
        greet(south)

    extra = jnp.where(has_north, 1, 0) + jnp.where(has_south, 1, 0)

    def send(src, dst, ssem, rsem, device):
        return pltpu.make_async_remote_copy(
            src_ref=src, dst_ref=dst, send_sem=ssem, recv_sem=rsem, device_id=device, device_id_type=MESH
        )

    loads[0].wait()
    for d in range(4):
        for b in range(4):
            pool1[d * 4 + b] = nv[send_ref[0, d, b]]
    pl.semaphore_wait(barrier, greeted + extra)

    halo_to = (south, north, east, west)
    halo_has = (has_south, has_north, None, None)
    from_has = (has_north, has_south, None, None)
    no_from = (jnp.logical_not(has_north), jnp.logical_not(has_south))

    def when(condition, body):
        if condition is None:
            body()
        else:
            pl.when(condition)(body)

    def halo_copy(d):
        part = pl.ds(d * 4, 4)
        return send(pool1.at[part], halo.at[part], halo_s.at[d], halo_r.at[d], halo_to[d])

    for d in range(4):
        when(halo_has[d], lambda d=d: halo_copy(d).start())
    for load in loads[3:]:
        load.start()

    for d in range(2):

        @pl.when(no_from[d])
        def _(d=d):
            halo[pl.ds(d * 4, 4)] = jnp.zeros((4, TILE, D), BF16)
            backns[pl.ds(4 - d * 4, 4)] = jnp.zeros((4, TILE, D), BF16)

    def messages(xs, at):
        pre = dot(xs, wm[...])
        s = sigmoid(pre)
        put_rows(pref, NE + at, (pre * s).astype(BF16))
        put_rows(msl, at, (s * (1.0 + pre * (1.0 - s))).astype(BF16))

    loads[1].wait()
    loads[2].wait()

    @pl.loop(0, NT // GROUP)
    def _(g):
        xs = rows_of(nv, g * GROUP)
        messages(xs, g * GROUP)
        put_rows(g2f, g * GROUP, dot(xs, wu[...]))

    def write_plan(at, rows):
        for i, row in enumerate(rows):
            plan_v[at + i : at + i + 1, :] = row

    write_plan(0, sort_plan([outer_first(adj_ref[0, k, t], NT, NT) for t in range(NT) for k in range(K)], per=K))
    write_plan(6, sort_plan([dsend_ref[0, d, s] for d in range(2) for s in range(4)])[:4])
    write_plan(10, sort_plan([1 - mask_ref[0, g] for g in range(NT)])[:1])
    write_plan(11, sort_plan([send_ref[0, d, b] for d in range(4) for b in range(4)])[:4])
    first = pltpu.make_async_copy(plan_v.at[pl.ds(0, 16)], plan.at[pl.ds(0, 16)], plan_sem.at[0])
    first.start()
    first.wait()
    hidden = [plan[10, s] for s in range(SLOTS)]
    edge_list = [(hidden[s], k) for s in range(SLOTS) for k in range(KD)]
    write_plan(16, sort_plan([outer_first(didx_ref[k, 0, g], NT, 8) for g, k in edge_list], [g * KD + k for g, k in edge_list], KD))
    second = pltpu.make_async_copy(plan_v.at[pl.ds(16, 8)], plan.at[pl.ds(16, 8)], plan_sem.at[1])
    second.start()
    second.wait()

    for d in (3, 2, 0, 1):
        when(from_has[d], lambda d=d: halo_copy(d).wait_recv())
        messages(rows_of(halo, d * 4), NT + d * 4)

    for i in (3, 4, 5):
        loads[i].wait()

    @pl.loop(0, NT // GROUP)
    def _(g):
        for i in range(GROUP):
            t = g * GROUP + i
            weights = jnp.concatenate([adjw[t * K + k] for k in range(K)], axis=1)
            picked = jnp.concatenate(
                [pref[NE + t], pref[NE + NT + t], pref[NE + adj_ref[0, 2, t]], pref[NE + adj_ref[0, 3, t]]], axis=0
            )
            agg[t] = dot(weights, picked).astype(BF16)
        upre = rows_of(g2f, g * GROUP) + dot(rows_of(agg, g * GROUP), wa[...])
        s = sigmoid(upre)
        hidden_rows = (upre * s).astype(BF16)
        put_rows(hid, g * GROUP, hidden_rows)
        put_rows(usl, g * GROUP, (s * (1.0 + upre * (1.0 - s))).astype(BF16))
        v2 = rows_of(nv, g * GROUP).astype(F32) + dot(hidden_rows, wo[...])
        put_rows(pref, g * GROUP, v2.astype(BF16))

    for d in range(4):
        when(halo_has[d], lambda d=d: halo_copy(d).wait_send())
    for d in range(2):
        for s in range(4):
            pref[NE + d * 4 + s] = pref[dsend_ref[0, d, s]]
    edges = [
        send(pref.at[pl.ds(NE, 4)], redge.at[pl.ds(4, 4)], edge_s.at[0], edge_r.at[0], west),
        send(pref.at[pl.ds(NE + 4, 4)], redge.at[pl.ds(0, 4)], edge_s.at[1], edge_r.at[1], east),
    ]
    for edge in edges:
        edge.start()
    for load in loads[6:]:
        load.wait()
    for edge in edges:
        edge.wait()
    for e in range(8):
        pref[NT + e] = redge[e]

    @pl.loop(0, SLOTS // GROUP)
    def _(g):
        goals, marks = [], []
        for i in range(GROUP):
            s = g * GROUP + i
            block = plan[10, s]
            weights = jnp.concatenate([decw[block * KD + k] for k in range(KD)], axis=1)
            picked = jnp.concatenate([pref[didx_ref[k, 0, block]] for k in range(KD)], axis=0)
            pool0[s] = dot(weights, picked).astype(BF16)
            goals.append(target[block].astype(F32))
            marks.append(jnp.full((1, TILE), mask_ref[0, block].astype(F32), F32))
        dpre = dot(rows_of(pool0, g * GROUP), wd[...])
        s = sigmoid(dpre)
        q = (dpre * s).astype(BF16)
        put_rows(pool1, g * GROUP, q)
        slope = s * (1.0 + dpre * (1.0 - s))
        residual = dot_nt(wh[...], q) - jnp.concatenate(goals, axis=1)
        residual = (jnp.concatenate(marks, axis=1) * residual).astype(BF16)
        err[:, pl.ds(pl.multiple_of(g * ROWS, ROWS), ROWS)] = residual
        dslope = (dot_tn(residual, wh[...]) * slope).astype(BF16)
        put_rows(mbuf, g * GROUP, dslope)
        put_rows(pool4, g * GROUP, dot_nt(dslope, wd[...]).astype(BF16))

    def spread(at, first_edge, last_edge, weight, source):
        if first_edge == 0:
            acc[...] = jnp.zeros((TILE, D), F32)

        @pl.loop(first_edge // GROUP, last_edge // GROUP)
        def _(h):
            total = acc[...]
            for i in range(GROUP):
                p = h * GROUP + i
                total = dot_tn(weight[plan[at + 5, p]], source[plan[at + 4, p]]) + plan[at + 1, p].astype(F32) * total
                pref[p] = total.astype(BF16)
            acc[...] = total

    def spread_of(at, tile):
        return plan[at + 3, tile].astype(F32) * pref[plan[at + 2, tile]].astype(F32)

    spread(16, 0, SLOTS * (KD - 1), decw, pool4)
    for e in range(8):
        pref[48 + e] = spread_of(16, e).astype(BF16)
    returns = [
        send(pref.at[pl.ds(48, 4)], rgin.at[pl.ds(4, 4)], rg_s.at[0], rg_r.at[0], west),
        send(pref.at[pl.ds(52, 4)], rgin.at[pl.ds(0, 4)], rg_s.at[1], rg_r.at[1], east),
    ]
    for item in returns:
        item.start()
    spread(16, SLOTS * (KD - 1), DEC_EDGES, decw, pool4)

    def job_copy(j, sem, src, dst, device):
        return send(src, dst, job_s.at[j, sem], job_r.at[j, sem], device)

    def core_out(j):
        at, rows = JOBS[j][:2]
        return job_copy(j, 0, cs.at[pl.ds(at, rows)], cr.at[pl.ds(at, rows)], mate)

    def scatter(j):
        at, rows, axes, _ = JOBS[j]
        chunk = rows // (n * n)
        out = []
        for step in range(1, n * n):
            device, there = plane_peer(axes, step)
            src = cs.at[pl.ds(pl.multiple_of(at + there * chunk, 16), chunk)]
            out.append(job_copy(j, step, src, r1.at[step - 1, pl.ds(at // (n * n), chunk)], device))
        return out

    def exchange(j):
        at, rows, _, axis = JOBS[j]
        mine = x4.at[place[axis], pl.ds(at // (n * n), rows // (n * n))]
        return [job_copy(j, n * n + step, mine, mine, line_peer(axis, step)) for step in range(1, n)]

    def own_chunk(j):
        at, rows, (a, b), _ = JOBS[j]
        chunk = rows // (n * n)
        return pl.ds(pl.multiple_of(at + (place[a] * n + place[b]) * chunk, 16), chunk)

    def gather(j):
        part = cr.at[own_chunk(j)]
        return [
            job_copy(j, n * n + n + step, part, part, plane_peer(JOBS[j][2], step)[0]) for step in range(1, n * n)
        ]

    def core_back(j):
        at, rows = JOBS[j][:2]
        part = pl.ds(at, rows)
        return (
            job_copy(j, n * n, cr.at[part], grads_hbm.at[core, part], mate),
            pltpu.make_async_copy(cr.at[part], grads_hbm.at[core, part], job_l.at[j]),
        )

    def job_stage(j, stage_number):
        at, rows, _, axis = JOBS[j]
        whole, own = pl.ds(at, rows), pl.ds(at % GRAD_F32, rows)
        small = pl.ds(at // (n * n), rows // (n * n))
        if stage_number == 0:
            low, high = gbuf[own, :HALF], gbuf[own, HALF:]
            cs[whole] = jnp.where(core == 0, high, low).astype(BF16)
            core_out(j).start()
        elif stage_number == 1:
            core_out(j).wait()
            low, high = gbuf[own, :HALF], gbuf[own, HALF:]
            cs[whole] = (jnp.where(core == 0, low, high) + cr[whole].astype(F32)).astype(BF16)
            for item in scatter(j):
                item.start()
        elif stage_number == 2:
            for item in scatter(j):
                item.wait()
            total = cs[own_chunk(j)].astype(F32)
            for step in range(n * n - 1):
                total = total + r1[step, small].astype(F32)
            x4[place[axis], small] = total.astype(BF16)
            for item in exchange(j):
                item.start()
        elif stage_number == 3:
            for item in exchange(j):
                item.wait()
            total = x4[0, small].astype(F32)
            for other in range(1, n):
                total = total + x4[other, small].astype(F32)
            cr[own_chunk(j)] = (total * (1.0 / (nrow * ncol))).astype(BF16)
            for item in gather(j):
                item.start()
        elif stage_number == 4:
            for item in gather(j):
                item.wait()
            for item in core_back(j):
                item.start()
        else:
            for item in core_back(j):
                item.wait()

    def gradient(at, left, right, halves=(0, 1)):
        for half in halves:
            lanes = slice(half * HALF, (half + 1) * HALF)
            total = None
            for (lref, lat, count), (rref, rat) in zip(left, right):
                lhs = lref[pl.ds(lat, count), :, lanes].reshape(count * TILE, HALF)
                term = dot_tn(lhs, rows_of(rref, rat, count))
                total = term if total is None else total + term
            gbuf[pl.ds(at % GRAD_F32 + half * HALF, HALF)] = total

    gradient(0, [(pool0, 0, SLOTS)], [(mbuf, 0)])
    q_rows = pool1[pl.ds(0, SLOTS)].reshape(SLOTS * TILE, D)
    gbuf[512:768, :] = jnp.zeros((256, D), F32)
    gbuf[512 : 512 + OUTC, :] = dot(err[...], q_rows)
    job_stage(0, 0)

    for item in returns:
        item.wait()
    total = None
    for p in range(8):
        arrived = rgin[plan[6, p]].astype(F32)
        total = arrived if total is None else arrived + plan[7, p].astype(F32) * total
        pref[40 + p] = total.astype(BF16)

    @pl.loop(0, NT)
    def _(t):
        value = spread_of(16, 8 + t).astype(BF16).astype(F32)
        value = value + plan[9, t].astype(F32) * pref[40 + plan[8, t]].astype(F32)
        g2f[t] = value
        pool4[t] = value.astype(BF16)

    job_stage(0, 1)
    gradient(768, [(hid, 0, NT)], [(pool4, 0)])

    @pl.loop(0, NT // GROUP)
    def _(g):
        back = dot_nt(rows_of(pool4, g * GROUP), wo[...]) * rows_of(usl, g * GROUP).astype(F32)
        slope = back.astype(BF16)
        put_rows(pool0, g * GROUP, slope)
        put_rows(g2f, g * GROUP, rows_of(g2f, g * GROUP) + dot_nt(slope, wu[...]))
        put_rows(pool1, g * GROUP, dot_nt(slope, wa[...]).astype(BF16))

    gradient(1280, [(nv, 0, NT)], [(pool0, 0)])
    gradient(1792, [(agg, 0, NT)], [(pool0, 0)])
    job_stage(1, 0)
    job_stage(0, 2)
    outer_edges = NT * (K - 1)
    spread(0, 0, outer_edges // 2, adjw, pool1)
    job_stage(1, 1)
    job_stage(0, 3)
    spread(0, outer_edges // 2, outer_edges, adjw, pool1)

    def message_slope(e):
        key = lax.rem(e + NT, NE)
        mbuf[e] = (spread_of(0, key) * msl[e].astype(F32)).astype(BF16)

    back_to = (north, south, west, east)
    back_has = (has_north, has_south, None, None)
    back_from = (has_south, has_north, None, None)

    def back_copy(d):
        dst = (backns.at[pl.ds(0, 4)], backns.at[pl.ds(4, 4)], redge.at[pl.ds(0, 4)], redge.at[pl.ds(4, 4)])[d]
        return send(usl.at[pl.ds(d * 4, 4)], dst, hg_s.at[d], hg_r.at[d], back_to[d])

    for d in range(4):

        @pl.loop(0, 4)
        def _(b, d=d):
            message_slope(NT + d * 4 + b)

        put_rows(usl, d * 4, dot_nt(rows_of(mbuf, NT + d * 4), wm[...]).astype(BF16))
        when(back_has[d], lambda d=d: back_copy(d).start())

    spread(0, outer_edges, ADJ_EDGES, adjw, pool1)

    @pl.loop(0, NT)
    def _(e):
        message_slope(e)

    left, right = [(nv, 0, NT), (halo, 0, NT)], [(mbuf, 0), (mbuf, NT)]
    gradient(2304, left, right)
    job_stage(2, 0)
    job_stage(1, 2)
    job_stage(2, 1)

    @pl.loop(0, NT // GROUP)
    def _(g):
        put_rows(g2f, g * GROUP, rows_of(g2f, g * GROUP) + dot_nt(rows_of(mbuf, g * GROUP), wm[...]))

    job_stage(0, 4)
    job_stage(1, 3)
    job_stage(2, 2)
    job_stage(2, 3)
    for d in range(4):
        when(back_from[d], lambda d=d: back_copy(d).wait_recv())
    for e in range(8):
        pref[e] = backns[e]
        pref[8 + e] = redge[e]
    total = None
    for p in range(16):
        arrived = pref[plan[11, p]].astype(F32)
        total = arrived if total is None else arrived + plan[12, p].astype(F32) * total
        pref[16 + p] = total.astype(BF16)

    @pl.loop(0, NT)
    def _(t):
        value = g2f[t] + plan[14, t].astype(F32) * pref[16 + plan[13, t]].astype(F32)
        agg[t] = value.astype(BF16)

    lat_out = pltpu.make_async_copy(agg, lat_hbm, out_sem.at[0])
    lat_out.start()
    job_stage(1, 4)
    job_stage(2, 4)
    for j in range(len(JOBS)):
        job_stage(j, 5)
    lat_out.wait()
    for d in range(4):
        when(back_has[d], lambda d=d: back_copy(d).wait_send())


SQUARES = (2304, 1280, 1792, 768, 0)
LAT_PARTS = 4


def finish(lat_hbm, grads_hbm, latent_hbm, msg_hbm, upd_hbm, agg_hbm, out_hbm, dec_hbm, head_hbm,
           lat, grads, latent, squares, head, in_sems, out_sems):
    per = NT // LAT_PARTS
    parts = [pl.ds(i * per, per) for i in range(LAT_PARTS)]
    loads = [pltpu.make_async_copy(lat_hbm.at[part], lat.at[part], in_sems.at[i]) for i, part in enumerate(parts)]
    for i, (at, rows) in enumerate([(at, D) for at in SQUARES] + [(D, HALF)]):
        part = pl.ds(at, rows)
        loads.append(pltpu.make_async_copy(grads_hbm.at[:, part], grads.at[:, part], in_sems.at[LAT_PARTS + i]))
    for load in loads:
        load.start()
    stores = []

    def store(src, dst):
        stores.append(pltpu.make_async_copy(src, dst, out_sems.at[len(stores)]))
        stores[-1].start()

    for i, part in enumerate(parts):
        loads[i].wait()
        latent[part] = lat[part].astype(F32)
        store(latent.at[part], latent_hbm.at[part])
    for i, (at, dst) in enumerate(zip(SQUARES, (msg_hbm, upd_hbm, agg_hbm, out_hbm, dec_hbm))):
        loads[LAT_PARTS + i].wait()
        for half in range(2):
            squares[i, :, half * HALF : (half + 1) * HALF] = grads[half, at : at + D].astype(F32)
        store(squares.at[i], dst)
    loads[-1].wait()
    for half in range(2):
        head[:, half * HALF : (half + 1) * HALF] = grads[half, D : D + HALF].astype(F32)[:OUTC]
    store(head, head_hbm)
    for item in stores:
        item.wait()


def on_device(
    sizes, nodes, send_list, adj_index, adj_weight, dec_send, dec_index, dec_weight, hidden_mask, target,
    w_msg, w_update, w_aggregate, w_output, w_decode, w_head,
):
    n = sizes["n"]
    tiles = lambda count, dtype=BF16: pltpu.VMEM((count, TILE, D), dtype)
    any_spec = pl.BlockSpec(memory_space=pl.ANY)
    smem = pl.BlockSpec(memory_space=pltpu.SMEM)
    scratch = [
        tiles(NT), tiles(NT),
        pltpu.VMEM((NT * K, TILE, TILE), BF16), pltpu.VMEM((NT * KD, TILE, TILE), BF16),
        pltpu.VMEM((NT, OUTC, TILE), BF16),
        *[pltpu.VMEM((D, D), BF16)] * 5, pltpu.VMEM((OUTC, D), BF16),
        tiles(2 * NE), tiles(NE), tiles(NT, F32),
        tiles(NT), tiles(NT), tiles(NT),
        tiles(8), tiles(8), pltpu.VMEM((OUTC, SLOTS * TILE), BF16),
        tiles(NT), tiles(NT), tiles(NE), tiles(NT),
        pltpu.VMEM((TILE, D), F32),
        pltpu.VMEM((GRAD_F32, D), F32),
        pltpu.VMEM((GRAD_ROWS, HALF), BF16), pltpu.VMEM((GRAD_ROWS, HALF), BF16),
        pltpu.VMEM((n * n - 1, GRAD_ROWS // n**2, HALF), BF16), pltpu.VMEM((n, GRAD_ROWS // n**2, HALF), BF16),
        tiles(8),
        pltpu.VMEM((24, 128), jnp.int32), pltpu.SMEM((24, 128), jnp.int32),
        pltpu.SemaphoreType.DMA((9 + NT,)), pltpu.SemaphoreType.DMA((2,)), pltpu.SemaphoreType.DMA((1,)),
        *[pltpu.SemaphoreType.DMA((4,))] * 2,
        *[pltpu.SemaphoreType.DMA((2,))] * 4,
        *[pltpu.SemaphoreType.DMA((4,))] * 2,
        *[pltpu.SemaphoreType.DMA((len(JOBS), 2 * n * n + n))] * 2,
        pltpu.SemaphoreType.DMA((len(JOBS),)),
    ]
    lat, grads = pl.pallas_call(
        functools.partial(kernel, sizes),
        out_shape=(
            jax.ShapeDtypeStruct((NT, TILE, D), BF16),
            jax.ShapeDtypeStruct((CORES, GRAD_ROWS, HALF), BF16),
        ),
        in_specs=[smem] * 5 + [any_spec] * 10,
        out_specs=(any_spec,) * 2,
        scratch_shapes=scratch,
        compiler_params=pltpu.CompilerParams(
            collective_id=0, has_side_effects=True, vmem_limit_bytes=62 * 1024 * 1024
        ),
        name="mesh_step",
    )(
        send_list, adj_index.transpose(0, 2, 1), dec_send, dec_index.transpose(2, 0, 1), hidden_mask,
        nodes.reshape(NT, TILE, D),
        adj_weight.reshape(NT * K, TILE, TILE),
        dec_weight.reshape(NT * KD, TILE, TILE),
        target.T,
        w_msg, w_update, w_aggregate, w_output, w_decode, w_head.T,
    )
    f32 = lambda *shape: jax.ShapeDtypeStruct(shape, F32)
    outs = pl.pallas_call(
        finish,
        out_shape=(f32(NT, TILE, D), *[f32(D, D)] * 5, f32(OUTC, D)),
        in_specs=[any_spec] * 2,
        out_specs=(any_spec,) * 7,
        scratch_shapes=[
            tiles(NT), pltpu.VMEM((CORES, GRAD_ROWS, HALF), BF16),
            tiles(NT, F32), pltpu.VMEM((5, D, D), F32), pltpu.VMEM((OUTC, D), F32),
            pltpu.SemaphoreType.DMA((LAT_PARTS + 6,)), pltpu.SemaphoreType.DMA((LAT_PARTS + 6,)),
        ],
        compiler_params=pltpu.CompilerParams(vmem_limit_bytes=60 * 1024 * 1024),
        name="finish",
    )(lat, grads)
    latent, msg, upd, agg, out, dec, head = outs
    return latent.reshape(NT * TILE, D), msg, upd, agg, out, dec, head.T


def solution(mesh):
    rows, cols = mesh.shape["row"], mesh.shape["col"]
    sizes = dict(axes_of(rows, cols), rows=rows, cols=cols)
    both = ("row", "col")
    return jax.shard_map(
        functools.partial(on_device, sizes),
        mesh=mesh,
        in_specs=(
            P(both, None),
            P(both, None, None),
            P(both, None, None),
            P(both, None, None, None),
            P(both, None, None),
            P(both, None, None),
            P(both, None, None, None),
            P(both, None),
            P(both, None),
            *[P()] * 6,
        ),
        out_specs=(P(both, None), *[P()] * 6),
        check_vma=False,
    )
```

```python
import functools

import jax
import jax.numpy as jnp
from jax import lax
from jax.experimental import pallas as pl
from jax.experimental.pallas import tpu as pltpu
from jax.sharding import PartitionSpec as P

MESH = pl.DeviceIdType.MESH
F32 = jnp.float32
BF16 = jnp.bfloat16

D = 512
OUTC = 227
TILE = 128
NT = 16
NE = 32
NR = 24
K = 4
KD = 3
SLOTS = 12
DEC_EDGES = SLOTS * KD
ADJ_EDGES = NT * K
GROUP = 4
ROWS = GROUP * TILE
CORES = 2

JOBS = (
    (0, 768, ("z", "y", "x")),
    (768, 512, ("z", "x", "y")),
    (1280, 512, ("x", "y", "z")),
    (1792, 512, ("y", "z", "x")),
)
LAST, LAST_ROWS = 2304, 512
GRAD_ROWS = 2816
GRAD_F32 = 2304
HALF = D // 2
JOB_SEMS = 17


def axes_of(rows, cols):
    if (rows, cols) == (8, 16):
        return dict(zh=2, x=4, zl=2, y=4, n=4)
    return dict(zh=1, x=2, zl=2, y=2, n=2)


def dot(a, b):
    return lax.dot_general(a, b, (((1,), (0,)), ((), ())), preferred_element_type=F32)


def dot_nt(a, b):
    return lax.dot_general(a, b, (((1,), (1,)), ((), ())), preferred_element_type=F32)


def dot_tn(a, b):
    return lax.dot_general(a, b, (((0,), (0,)), ((), ())), preferred_element_type=F32)


def sigmoid(v):
    return 0.5 * jnp.tanh(0.5 * v) + 0.5


def rows_of(ref, start, count=GROUP):
    block = ref[pl.ds(start, count)]
    return block.reshape(count * TILE, block.shape[-1])


def put_rows(ref, start, value, count=GROUP):
    ref[pl.ds(start, count)] = value.reshape(count, TILE, value.shape[-1])


def outer_first(value, inner, outer):
    return jnp.where(value >= inner, value - inner, value + outer)


def sort_plan(values, blocks=None, per=1):
    count = len(values)
    depth = -(-count // 8) * 8
    down = lax.broadcasted_iota(jnp.int32, (depth, 128), 0)
    across = lax.broadcasted_iota(jnp.int32, (depth, 128), 1)
    mine = jnp.full((depth, 128), 1000, jnp.int32)
    other = jnp.full((depth, 128), 1000, jnp.int32)
    for q, value in enumerate(values):
        mine = jnp.where(down == q, value, mine)
        other = jnp.where(across == q, value, other)
    same_before = jnp.where((other == mine) & (across < down), 1, 0)
    before = jnp.where(other < mine, 1, 0) + same_before
    rank = jnp.sum(before, axis=1, keepdims=True)
    continues = jnp.minimum(jnp.sum(same_before, axis=1, keepdims=True), 1)
    hit = jnp.where((rank == across) & (down < count), 1, 0)
    order = jnp.sum(hit * down, axis=0, keepdims=True)
    follows = jnp.sum(hit * continues, axis=0, keepdims=True)
    upto = jnp.sum(jnp.where(mine <= across, 1, 0), axis=0, keepdims=True)
    present = jnp.minimum(jnp.sum(jnp.where(mine == across, 1, 0), axis=0, keepdims=True), 1)
    group = {1: down, 3: (down * 43) >> 7, 4: down >> 2}[per]
    group_row = jnp.sum(hit * group, axis=0, keepdims=True)
    named = down
    if blocks is not None:
        for q, value in enumerate(blocks):
            named = jnp.where(down == q, value, named)
    named_row = jnp.sum(hit * named, axis=0, keepdims=True)
    return order, follows, jnp.maximum(upto - 1, 0), present, group_row, named_row


def kernel(
    sizes,
    send_ref, adj_ref, dsend_ref, didx_ref, mask_ref,
    nodes_hbm, adjw_hbm, decw_hbm, target_hbm,
    wm_hbm, wu_hbm, wa_hbm, wo_hbm, wd_hbm, wh_hbm,
    lat_hbm, grads_hbm,
    nv, halo, adjw, decw, target, wm, wu, wa, wo, wd, wh,
    pref, msl, g2f, agg, hid, usl, redge, rgin, err, pool0, pool1, mbuf, pool4, acc,
    gbuf, cs, cr, r1, s2, r2, x4, rl,
    backns, plan_v, plan,
    in_sems, plan_sem, out_sem, halo_s, halo_r, edge_s, edge_r, rg_s, rg_r, hg_s, hg_r, job_s, job_r, job_l, last_s, last_r,
):
    nrow, ncol, nx, ny, nzl = sizes["rows"], sizes["cols"], sizes["x"], sizes["y"], sizes["zl"]
    nzh, n = sizes["zh"], sizes["n"]
    r = lax.axis_index("row")
    c = lax.axis_index("col")
    zh, x = lax.div(r, nx), lax.rem(r, nx)
    zl = lax.div(c, ny * CORES)
    y = lax.rem(lax.div(c, CORES), ny)
    core = lax.rem(c, CORES)
    z = zh * nzl + zl
    place = {"x": x, "y": y, "z": z}

    def peer(axis, step):
        there = lax.rem(place[axis] + step, n)
        if axis == "x":
            return (zh * nx + there, c), there
        if axis == "y":
            return (r, (zl * ny + there) * CORES + core), there
        return (lax.div(there, nzl) * nx + x, (lax.rem(there, nzl) * ny + y) * CORES + core), there

    def plane_peer(step):
        there = lax.rem(x * n + y + step, n * n)
        return (zh * nx + lax.div(there, n), (zl * ny + lax.rem(there, n)) * CORES + core), there

    mate = (r, c + 1 - 2 * core)
    west = (r, lax.rem(c + ncol - 1, ncol))
    east = (r, lax.rem(c + 1, ncol))
    north = (r - 1, c)
    south = (r + 1, c)
    has_north = r > 0
    has_south = r < nrow - 1

    loads = [
        pltpu.make_async_copy(src, dst, in_sems.at[i])
        for i, (src, dst) in enumerate(
            (
                (nodes_hbm, nv), (wm_hbm, wm), (wu_hbm, wu), (adjw_hbm, adjw), (wa_hbm, wa), (wo_hbm, wo),
                (decw_hbm, decw), (wd_hbm, wd), (wh_hbm, wh),
                *((target_hbm.at[:, pl.ds(g * TILE, TILE)], target.at[g]) for g in range(NT)),
            )
        )
    ]
    for load in loads[:3]:
        load.start()

    barrier = pltpu.get_barrier_semaphore()

    def greet(device):
        pl.semaphore_signal(barrier, inc=1, device_id=device, device_id_type=MESH)

    greet(west)
    greet(east)
    for step in range(1, n):
        greet(peer("z", step)[0])
    for step in range(1, n * n):
        greet(plane_peer(step)[0])
    greeted = 2 + (n - 1) + (n * n - 1)

    @pl.when(has_north)
    def _():
        greet(north)

    @pl.when(has_south)
    def _():
        greet(south)

    extra = jnp.where(has_north, 1, 0) + jnp.where(has_south, 1, 0)

    def send(src, dst, ssem, rsem, device):
        return pltpu.make_async_remote_copy(
            src_ref=src, dst_ref=dst, send_sem=ssem, recv_sem=rsem, device_id=device, device_id_type=MESH
        )

    loads[0].wait()
    for d in range(4):
        for b in range(4):
            pool1[d * 4 + b] = nv[send_ref[0, d, b]]
    pl.semaphore_wait(barrier, greeted + extra)

    halo_to = (south, north, east, west)
    halo_has = (has_south, has_north, None, None)
    from_has = (has_north, has_south, None, None)
    no_from = (jnp.logical_not(has_north), jnp.logical_not(has_south))

    def when(condition, body):
        if condition is None:
            body()
        else:
            pl.when(condition)(body)

    def halo_copy(d):
        part = pl.ds(d * 4, 4)
        return send(pool1.at[part], halo.at[part], halo_s.at[d], halo_r.at[d], halo_to[d])

    for d in range(4):
        when(halo_has[d], lambda d=d: halo_copy(d).start())
    for load in loads[3:]:
        load.start()

    for d in range(2):

        @pl.when(no_from[d])
        def _(d=d):
            halo[pl.ds(d * 4, 4)] = jnp.zeros((4, TILE, D), BF16)
            backns[pl.ds(4 - d * 4, 4)] = jnp.zeros((4, TILE, D), BF16)

    def messages(xs, at):
        pre = dot(xs, wm[...])
        s = sigmoid(pre)
        put_rows(pref, NE + at, (pre * s).astype(BF16))
        put_rows(msl, at, (s * (1.0 + pre * (1.0 - s))).astype(BF16))

    loads[1].wait()
    loads[2].wait()

    @pl.loop(0, NT // GROUP)
    def _(g):
        xs = rows_of(nv, g * GROUP)
        messages(xs, g * GROUP)
        put_rows(g2f, g * GROUP, dot(xs, wu[...]))

    def write_plan(at, rows):
        for i, row in enumerate(rows):
            plan_v[at + i : at + i + 1, :] = row

    write_plan(0, sort_plan([outer_first(adj_ref[0, k, t], NT, NT) for t in range(NT) for k in range(K)], per=K))
    write_plan(6, sort_plan([dsend_ref[0, d, s] for d in range(2) for s in range(4)])[:4])
    write_plan(10, sort_plan([1 - mask_ref[0, g] for g in range(NT)])[:1])
    write_plan(11, sort_plan([send_ref[0, d, b] for d in range(4) for b in range(4)])[:4])
    first = pltpu.make_async_copy(plan_v.at[pl.ds(0, 16)], plan.at[pl.ds(0, 16)], plan_sem.at[0])
    first.start()
    first.wait()
    hidden = [plan[10, s] for s in range(SLOTS)]
    edge_list = [(hidden[s], k) for s in range(SLOTS) for k in range(KD)]
    write_plan(16, sort_plan([outer_first(didx_ref[k, 0, g], NT, 8) for g, k in edge_list], [g * KD + k for g, k in edge_list], KD))
    second = pltpu.make_async_copy(plan_v.at[pl.ds(16, 8)], plan.at[pl.ds(16, 8)], plan_sem.at[1])
    second.start()
    second.wait()

    for d in (3, 2, 0, 1):
        when(from_has[d], lambda d=d: halo_copy(d).wait_recv())
        messages(rows_of(halo, d * 4), NT + d * 4)

    for i in (3, 4, 5):
        loads[i].wait()

    @pl.loop(0, NT // GROUP)
    def _(g):
        for i in range(GROUP):
            t = g * GROUP + i
            weights = jnp.concatenate([adjw[t * K + k] for k in range(K)], axis=1)
            picked = jnp.concatenate(
                [pref[NE + t], pref[NE + NT + t], pref[NE + adj_ref[0, 2, t]], pref[NE + adj_ref[0, 3, t]]], axis=0
            )
            agg[t] = dot(weights, picked).astype(BF16)
        upre = rows_of(g2f, g * GROUP) + dot(rows_of(agg, g * GROUP), wa[...])
        s = sigmoid(upre)
        hidden_rows = (upre * s).astype(BF16)
        put_rows(hid, g * GROUP, hidden_rows)
        put_rows(usl, g * GROUP, (s * (1.0 + upre * (1.0 - s))).astype(BF16))
        v2 = rows_of(nv, g * GROUP).astype(F32) + dot(hidden_rows, wo[...])
        put_rows(pref, g * GROUP, v2.astype(BF16))

    for d in range(4):
        when(halo_has[d], lambda d=d: halo_copy(d).wait_send())
    for d in range(2):
        for s in range(4):
            pref[NE + d * 4 + s] = pref[dsend_ref[0, d, s]]
    edges = [
        send(pref.at[pl.ds(NE, 4)], redge.at[pl.ds(4, 4)], edge_s.at[0], edge_r.at[0], west),
        send(pref.at[pl.ds(NE + 4, 4)], redge.at[pl.ds(0, 4)], edge_s.at[1], edge_r.at[1], east),
    ]
    for edge in edges:
        edge.start()
    for load in loads[6:]:
        load.wait()
    for edge in edges:
        edge.wait()
    for e in range(8):
        pref[NT + e] = redge[e]

    @pl.loop(0, SLOTS // GROUP)
    def _(g):
        goals, marks = [], []
        for i in range(GROUP):
            s = g * GROUP + i
            block = plan[10, s]
            weights = jnp.concatenate([decw[block * KD + k] for k in range(KD)], axis=1)
            picked = jnp.concatenate([pref[didx_ref[k, 0, block]] for k in range(KD)], axis=0)
            pool0[s] = dot(weights, picked).astype(BF16)
            goals.append(target[block].astype(F32))
            marks.append(jnp.full((1, TILE), mask_ref[0, block].astype(F32), F32))
        dpre = dot(rows_of(pool0, g * GROUP), wd[...])
        s = sigmoid(dpre)
        q = (dpre * s).astype(BF16)
        put_rows(pool1, g * GROUP, q)
        slope = s * (1.0 + dpre * (1.0 - s))
        residual = dot_nt(wh[...], q) - jnp.concatenate(goals, axis=1)
        residual = (jnp.concatenate(marks, axis=1) * residual).astype(BF16)
        err[:, pl.ds(pl.multiple_of(g * ROWS, ROWS), ROWS)] = residual
        dslope = (dot_tn(residual, wh[...]) * slope).astype(BF16)
        put_rows(mbuf, g * GROUP, dslope)
        put_rows(pool4, g * GROUP, dot_nt(dslope, wd[...]).astype(BF16))

    def spread(at, first_edge, last_edge, weight, source):
        if first_edge == 0:
            acc[...] = jnp.zeros((TILE, D), F32)

        @pl.loop(first_edge // GROUP, last_edge // GROUP)
        def _(h):
            total = acc[...]
            for i in range(GROUP):
                p = h * GROUP + i
                total = dot_tn(weight[plan[at + 5, p]], source[plan[at + 4, p]]) + plan[at + 1, p].astype(F32) * total
                pref[p] = total.astype(BF16)
            acc[...] = total

    def spread_of(at, tile):
        return plan[at + 3, tile].astype(F32) * pref[plan[at + 2, tile]].astype(F32)

    spread(16, 0, SLOTS * (KD - 1), decw, pool4)
    for e in range(8):
        pref[48 + e] = spread_of(16, e).astype(BF16)
    returns = [
        send(pref.at[pl.ds(48, 4)], rgin.at[pl.ds(4, 4)], rg_s.at[0], rg_r.at[0], west),
        send(pref.at[pl.ds(52, 4)], rgin.at[pl.ds(0, 4)], rg_s.at[1], rg_r.at[1], east),
    ]
    for item in returns:
        item.start()
    spread(16, SLOTS * (KD - 1), DEC_EDGES, decw, pool4)

    def job_copy(j, sem, src, dst, device):
        return send(src, dst, job_s.at[j, sem], job_r.at[j, sem], device)

    def c_copy(j):
        at, rows, _ = JOBS[j]
        return job_copy(j, 0, cs.at[pl.ds(at, rows)], cr.at[pl.ds(at, rows)], mate)

    def first_copies(j):
        at, rows, order = JOBS[j]
        quarter = rows // n
        out = []
        for step in range(1, n):
            device, there = peer(order[0], step)
            src = cs.at[pl.ds(pl.multiple_of(at + there * quarter, 16), quarter)]
            out.append(job_copy(j, step, src, r1.at[step - 1, pl.ds(at // n, quarter)], device))
        return out

    def second_copies(j):
        at, rows, order = JOBS[j]
        small = rows // (n * n)
        out = []
        for step in range(1, n):
            device, there = peer(order[1], step)
            src = s2.at[pl.ds(pl.multiple_of(at // n + there * small, 16), small)]
            out.append(job_copy(j, 3 + step, src, r2.at[step - 1, pl.ds(at // (n * n), small)], device))
        return out

    def third_copies(j):
        at, rows, order = JOBS[j]
        small = rows // (n * n)
        out = []
        for step in range(1, n):
            device, _ = peer(order[2], step)
            mine = x4.at[place[order[2]], pl.ds(at // (n * n), small)]
            out.append(job_copy(j, 6 + step, mine, mine, device))
        return out

    def small_at(j):
        at, rows, order = JOBS[j]
        quarter, small = rows // n, rows // (n * n)
        return pl.multiple_of(at + place[order[0]] * quarter + place[order[1]] * small, 16)

    def back_small(j):
        at, rows, order = JOBS[j]
        part = cr.at[pl.ds(small_at(j), rows // (n * n))]
        return [
            job_copy(j, 9 + step, part, part, peer(order[1], step)[0]) for step in range(1, n)
        ]

    def back_quarter(j):
        at, rows, order = JOBS[j]
        quarter = rows // n
        part = cr.at[pl.ds(pl.multiple_of(at + place[order[0]] * quarter, 16), quarter)]
        return [
            job_copy(j, 12 + step, part, part, peer(order[0], step)[0]) for step in range(1, n)
        ]

    def back_core(j):
        at, rows, _ = JOBS[j]
        part = pl.ds(at, rows)
        return (
            job_copy(j, 16, cr.at[part], grads_hbm.at[core, part], mate),
            pltpu.make_async_copy(cr.at[part], grads_hbm.at[core, part], job_l.at[j]),
        )

    def job_stage(j, stage_number):
        at, rows, order = JOBS[j]
        quarter, small = rows // n, rows // (n * n)
        whole = pl.ds(at, rows)
        own = pl.ds(at % GRAD_F32, rows)
        if stage_number == 0:
            low, high = gbuf[own, :HALF], gbuf[own, HALF:]
            cs[whole] = jnp.where(core == 0, high, low).astype(BF16)
            c_copy(j).start()
        elif stage_number == 1:
            c_copy(j).wait()
            low, high = gbuf[own, :HALF], gbuf[own, HALF:]
            cs[whole] = (jnp.where(core == 0, low, high) + cr[whole].astype(F32)).astype(BF16)
            for item in first_copies(j):
                item.start()
        elif stage_number == 2:
            mine = pl.ds(pl.multiple_of(at + place[order[0]] * quarter, 16), quarter)
            for item in first_copies(j):
                item.wait()
            total = cs[mine].astype(F32)
            for step in range(n - 1):
                total = total + r1[step, pl.ds(at // n, quarter)].astype(F32)
            s2[pl.ds(at // n, quarter)] = total.astype(BF16)
            for item in second_copies(j):
                item.start()
        elif stage_number == 3:
            mine = pl.ds(pl.multiple_of(at // n + place[order[1]] * small, 16), small)
            for item in second_copies(j):
                item.wait()
            total = s2[mine].astype(F32)
            for step in range(n - 1):
                total = total + r2[step, pl.ds(at // (n * n), small)].astype(F32)
            x4[place[order[2]], pl.ds(at // (n * n), small)] = total.astype(BF16)
            for item in third_copies(j):
                item.start()
        elif stage_number == 4:
            for item in third_copies(j):
                item.wait()
            total = x4[0, pl.ds(at // (n * n), small)].astype(F32)
            for other in range(1, n):
                total = total + x4[other, pl.ds(at // (n * n), small)].astype(F32)
            cr[pl.ds(small_at(j), small)] = (total * (1.0 / (nrow * ncol))).astype(BF16)
            for item in back_small(j):
                item.start()
        elif stage_number == 5:
            for item in back_small(j):
                item.wait()
            for item in back_quarter(j):
                item.start()
        elif stage_number == 6:
            for item in back_quarter(j):
                item.wait()
            for item in back_core(j):
                item.start()
        else:
            for item in back_core(j):
                item.wait()

    chunk = LAST_ROWS // (n * n)
    last_mine = pl.ds(pl.multiple_of(LAST + (x * n + y) * chunk, 16), chunk)
    last_place = pl.ds(LAST // (n * n), chunk)

    def last_copy(sem, src, dst, device):
        return send(src, dst, last_s.at[sem], last_r.at[sem], device)

    def last_core():
        return last_copy(0, cs.at[pl.ds(LAST, LAST_ROWS)], cr.at[pl.ds(LAST, LAST_ROWS)], mate)

    def last_scatter():
        out = []
        for step in range(1, n * n):
            device, there = plane_peer(step)
            src = cs.at[pl.ds(pl.multiple_of(LAST + there * chunk, 16), chunk)]
            out.append(last_copy(step, src, rl.at[step - 1], device))
        return out

    def last_exchange():
        mine = x4.at[z, last_place]
        return [last_copy(n * n + step, mine, mine, peer("z", step)[0]) for step in range(1, n)]

    def last_gather():
        part = cr.at[last_mine]
        return [last_copy(n * n + n + step, part, part, plane_peer(step)[0]) for step in range(1, n * n)]

    def last_back():
        part = pl.ds(LAST, LAST_ROWS)
        return (
            last_copy(n * n, cr.at[part], grads_hbm.at[core, part], mate),
            pltpu.make_async_copy(cr.at[part], grads_hbm.at[core, part], job_l.at[len(JOBS)]),
        )

    def last_stage(stage_number):
        whole = pl.ds(LAST, LAST_ROWS)
        if stage_number == 0:
            low, high = gbuf[:LAST_ROWS, :HALF], gbuf[:LAST_ROWS, HALF:]
            cs[whole] = jnp.where(core == 0, high, low).astype(BF16)
            last_core().start()
        elif stage_number == 1:
            last_core().wait()
            low, high = gbuf[:LAST_ROWS, :HALF], gbuf[:LAST_ROWS, HALF:]
            cs[whole] = (jnp.where(core == 0, low, high) + cr[whole].astype(F32)).astype(BF16)
            for item in last_scatter():
                item.start()
        elif stage_number == 2:
            for item in last_scatter():
                item.wait()
            total = cs[last_mine].astype(F32)
            for step in range(n * n - 1):
                total = total + rl[step].astype(F32)
            x4[z, last_place] = total.astype(BF16)
            for item in last_exchange():
                item.start()
        elif stage_number == 3:
            for item in last_exchange():
                item.wait()
            total = x4[0, last_place].astype(F32)
            for other in range(1, n):
                total = total + x4[other, last_place].astype(F32)
            cr[last_mine] = (total * (1.0 / (nrow * ncol))).astype(BF16)
            for item in last_gather():
                item.start()
        elif stage_number == 4:
            for item in last_gather():
                item.wait()
            for item in last_back():
                item.start()
        else:
            for item in last_back():
                item.wait()

    def gradient(at, left, right, halves=(0, 1)):
        for half in halves:
            lanes = slice(half * HALF, (half + 1) * HALF)
            total = None
            for (lref, lat, count), (rref, rat) in zip(left, right):
                lhs = lref[pl.ds(lat, count), :, lanes].reshape(count * TILE, HALF)
                term = dot_tn(lhs, rows_of(rref, rat, count))
                total = term if total is None else total + term
            gbuf[pl.ds(at % GRAD_F32 + half * HALF, HALF)] = total

    gradient(0, [(pool0, 0, SLOTS)], [(mbuf, 0)])
    q_rows = pool1[pl.ds(0, SLOTS)].reshape(SLOTS * TILE, D)
    gbuf[512:768, :] = jnp.zeros((256, D), F32)
    gbuf[512 : 512 + OUTC, :] = dot(err[...], q_rows)
    job_stage(0, 0)

    for item in returns:
        item.wait()
    total = None
    for p in range(8):
        arrived = rgin[plan[6, p]].astype(F32)
        total = arrived if total is None else arrived + plan[7, p].astype(F32) * total
        pref[40 + p] = total.astype(BF16)

    @pl.loop(0, NT)
    def _(t):
        value = spread_of(16, 8 + t).astype(BF16).astype(F32)
        value = value + plan[9, t].astype(F32) * pref[40 + plan[8, t]].astype(F32)
        g2f[t] = value
        pool4[t] = value.astype(BF16)

    job_stage(0, 1)
    gradient(768, [(hid, 0, NT)], [(pool4, 0)])
    job_stage(1, 0)

    @pl.loop(0, NT // GROUP)
    def _(g):
        back = dot_nt(rows_of(pool4, g * GROUP), wo[...]) * rows_of(usl, g * GROUP).astype(F32)
        slope = back.astype(BF16)
        put_rows(pool0, g * GROUP, slope)
        put_rows(g2f, g * GROUP, rows_of(g2f, g * GROUP) + dot_nt(slope, wu[...]))
        put_rows(pool1, g * GROUP, dot_nt(slope, wa[...]).astype(BF16))

    gradient(1280, [(nv, 0, NT)], [(pool0, 0)])
    job_stage(2, 0)
    job_stage(1, 1)
    gradient(1792, [(agg, 0, NT)], [(pool0, 0)])
    job_stage(3, 0)
    job_stage(0, 2)
    outer_edges = NT * (K - 1)
    spread(0, 0, outer_edges // 2, adjw, pool1)
    job_stage(2, 1)
    job_stage(3, 1)
    spread(0, outer_edges // 2, outer_edges, adjw, pool1)

    def message_slope(e):
        key = lax.rem(e + NT, NE)
        mbuf[e] = (spread_of(0, key) * msl[e].astype(F32)).astype(BF16)

    back_to = (north, south, west, east)
    back_has = (has_north, has_south, None, None)
    back_from = (has_south, has_north, None, None)

    def back_copy(d):
        dst = (backns.at[pl.ds(0, 4)], backns.at[pl.ds(4, 4)], redge.at[pl.ds(0, 4)], redge.at[pl.ds(4, 4)])[d]
        return send(usl.at[pl.ds(d * 4, 4)], dst, hg_s.at[d], hg_r.at[d], back_to[d])

    for d in range(4):

        @pl.loop(0, 4)
        def _(b, d=d):
            message_slope(NT + d * 4 + b)

        put_rows(usl, d * 4, dot_nt(rows_of(mbuf, NT + d * 4), wm[...]).astype(BF16))
        when(back_has[d], lambda d=d: back_copy(d).start())

    job_stage(0, 3)
    job_stage(1, 2)
    spread(0, outer_edges, ADJ_EDGES, adjw, pool1)
    job_stage(2, 2)
    job_stage(3, 2)

    @pl.loop(0, NT)
    def _(e):
        message_slope(e)

    left, right = [(nv, 0, NT), (halo, 0, NT)], [(mbuf, 0), (mbuf, NT)]
    gradient(LAST, left, right)
    last_stage(0)
    job_stage(1, 3)
    job_stage(0, 4)
    last_stage(1)
    job_stage(2, 3)
    job_stage(3, 3)

    @pl.loop(0, NT // GROUP)
    def _(g):
        put_rows(g2f, g * GROUP, rows_of(g2f, g * GROUP) + dot_nt(rows_of(mbuf, g * GROUP), wm[...]))

    job_stage(1, 4)
    job_stage(0, 5)
    job_stage(2, 4)
    job_stage(3, 4)
    last_stage(2)
    job_stage(1, 5)
    job_stage(2, 5)
    job_stage(3, 5)
    job_stage(0, 6)
    last_stage(3)
    job_stage(1, 6)
    job_stage(2, 6)
    job_stage(3, 6)
    for d in range(4):
        when(back_from[d], lambda d=d: back_copy(d).wait_recv())
    for e in range(8):
        pref[e] = backns[e]
        pref[8 + e] = redge[e]
    total = None
    for p in range(16):
        arrived = pref[plan[11, p]].astype(F32)
        total = arrived if total is None else arrived + plan[12, p].astype(F32) * total
        pref[16 + p] = total.astype(BF16)

    @pl.loop(0, NT)
    def _(t):
        value = g2f[t] + plan[14, t].astype(F32) * pref[16 + plan[13, t]].astype(F32)
        agg[t] = value.astype(BF16)

    lat_out = pltpu.make_async_copy(agg, lat_hbm, out_sem.at[0])
    lat_out.start()
    last_stage(4)
    for j in range(len(JOBS)):
        job_stage(j, 7)
    last_stage(5)
    lat_out.wait()
    for d in range(4):
        when(back_has[d], lambda d=d: back_copy(d).wait_send())


SQUARES = (2304, 1280, 1792, 768, 0)
LAT_PARTS = 4


def finish(lat_hbm, grads_hbm, latent_hbm, msg_hbm, upd_hbm, agg_hbm, out_hbm, dec_hbm, head_hbm,
           lat, grads, latent, squares, head, in_sems, out_sems):
    per = NT // LAT_PARTS
    parts = [pl.ds(i * per, per) for i in range(LAT_PARTS)]
    loads = [pltpu.make_async_copy(lat_hbm.at[part], lat.at[part], in_sems.at[i]) for i, part in enumerate(parts)]
    for i, (at, rows) in enumerate([(at, D) for at in SQUARES] + [(D, HALF)]):
        part = pl.ds(at, rows)
        loads.append(pltpu.make_async_copy(grads_hbm.at[:, part], grads.at[:, part], in_sems.at[LAT_PARTS + i]))
    for load in loads:
        load.start()
    stores = []

    def store(src, dst):
        stores.append(pltpu.make_async_copy(src, dst, out_sems.at[len(stores)]))
        stores[-1].start()

    for i, part in enumerate(parts):
        loads[i].wait()
        latent[part] = lat[part].astype(F32)
        store(latent.at[part], latent_hbm.at[part])
    for i, (at, dst) in enumerate(zip(SQUARES, (msg_hbm, upd_hbm, agg_hbm, out_hbm, dec_hbm))):
        loads[LAT_PARTS + i].wait()
        for half in range(2):
            squares[i, :, half * HALF : (half + 1) * HALF] = grads[half, at : at + D].astype(F32)
        store(squares.at[i], dst)
    loads[-1].wait()
    for half in range(2):
        head[:, half * HALF : (half + 1) * HALF] = grads[half, D : D + HALF].astype(F32)[:OUTC]
    store(head, head_hbm)
    for item in stores:
        item.wait()


def on_device(
    sizes, nodes, send_list, adj_index, adj_weight, dec_send, dec_index, dec_weight, hidden_mask, target,
    w_msg, w_update, w_aggregate, w_output, w_decode, w_head,
):
    n = sizes["n"]
    tiles = lambda count, dtype=BF16: pltpu.VMEM((count, TILE, D), dtype)
    any_spec = pl.BlockSpec(memory_space=pl.ANY)
    smem = pl.BlockSpec(memory_space=pltpu.SMEM)
    scratch = [
        tiles(NT), tiles(NT),
        pltpu.VMEM((NT * K, TILE, TILE), BF16), pltpu.VMEM((NT * KD, TILE, TILE), BF16),
        pltpu.VMEM((NT, OUTC, TILE), BF16),
        *[pltpu.VMEM((D, D), BF16)] * 5, pltpu.VMEM((OUTC, D), BF16),
        tiles(2 * NE), tiles(NE), tiles(NT, F32),
        tiles(NT), tiles(NT), tiles(NT),
        tiles(8), tiles(8), pltpu.VMEM((OUTC, SLOTS * TILE), BF16),
        tiles(NT), tiles(NT), tiles(NE), tiles(NT),
        pltpu.VMEM((TILE, D), F32),
        pltpu.VMEM((GRAD_F32, D), F32),
        pltpu.VMEM((GRAD_ROWS, HALF), BF16), pltpu.VMEM((GRAD_ROWS, HALF), BF16),
        pltpu.VMEM((n - 1, LAST // n, HALF), BF16), pltpu.VMEM((LAST // n, HALF), BF16),
        pltpu.VMEM((n - 1, LAST // n**2, HALF), BF16), pltpu.VMEM((n, GRAD_ROWS // n**2, HALF), BF16),
        pltpu.VMEM((n * n - 1, LAST_ROWS // n**2, HALF), BF16),
        tiles(8),
        pltpu.VMEM((24, 128), jnp.int32), pltpu.SMEM((24, 128), jnp.int32),
        pltpu.SemaphoreType.DMA((9 + NT,)), pltpu.SemaphoreType.DMA((2,)), pltpu.SemaphoreType.DMA((1,)),
        *[pltpu.SemaphoreType.DMA((4,))] * 2,
        *[pltpu.SemaphoreType.DMA((2,))] * 4,
        *[pltpu.SemaphoreType.DMA((4,))] * 2,
        *[pltpu.SemaphoreType.DMA((len(JOBS), JOB_SEMS))] * 2,
        pltpu.SemaphoreType.DMA((len(JOBS) + 1,)),
        *[pltpu.SemaphoreType.DMA((2 * n * n + n,))] * 2,
    ]
    lat, grads = pl.pallas_call(
        functools.partial(kernel, sizes),
        out_shape=(
            jax.ShapeDtypeStruct((NT, TILE, D), BF16),
            jax.ShapeDtypeStruct((CORES, GRAD_ROWS, HALF), BF16),
        ),
        in_specs=[smem] * 5 + [any_spec] * 10,
        out_specs=(any_spec,) * 2,
        scratch_shapes=scratch,
        compiler_params=pltpu.CompilerParams(
            collective_id=0, has_side_effects=True, vmem_limit_bytes=62 * 1024 * 1024
        ),
        name="mesh_step",
    )(
        send_list, adj_index.transpose(0, 2, 1), dec_send, dec_index.transpose(2, 0, 1), hidden_mask,
        nodes.reshape(NT, TILE, D),
        adj_weight.reshape(NT * K, TILE, TILE),
        dec_weight.reshape(NT * KD, TILE, TILE),
        target.T,
        w_msg, w_update, w_aggregate, w_output, w_decode, w_head.T,
    )
    f32 = lambda *shape: jax.ShapeDtypeStruct(shape, F32)
    outs = pl.pallas_call(
        finish,
        out_shape=(f32(NT, TILE, D), *[f32(D, D)] * 5, f32(OUTC, D)),
        in_specs=[any_spec] * 2,
        out_specs=(any_spec,) * 7,
        scratch_shapes=[
            tiles(NT), pltpu.VMEM((CORES, GRAD_ROWS, HALF), BF16),
            tiles(NT, F32), pltpu.VMEM((5, D, D), F32), pltpu.VMEM((OUTC, D), F32),
            pltpu.SemaphoreType.DMA((LAT_PARTS + 6,)), pltpu.SemaphoreType.DMA((LAT_PARTS + 6,)),
        ],
        compiler_params=pltpu.CompilerParams(vmem_limit_bytes=60 * 1024 * 1024),
        name="finish",
    )(lat, grads)
    latent, msg, upd, agg, out, dec, head = outs
    return latent.reshape(NT * TILE, D), msg, upd, agg, out, dec, head.T


def solution(mesh):
    rows, cols = mesh.shape["row"], mesh.shape["col"]
    sizes = dict(axes_of(rows, cols), rows=rows, cols=cols)
    both = ("row", "col")
    return jax.shard_map(
        functools.partial(on_device, sizes),
        mesh=mesh,
        in_specs=(
            P(both, None),
            P(both, None, None),
            P(both, None, None),
            P(both, None, None, None),
            P(both, None, None),
            P(both, None, None),
            P(both, None, None, None),
            P(both, None),
            P(both, None),
            *[P()] * 6,
        ),
        out_specs=(P(both, None), *[P()] * 6),
        check_vma=False,
    )
```

```python
import functools

import jax
import jax.numpy as jnp
from jax import lax
from jax.experimental import pallas as pl
from jax.experimental.pallas import tpu as pltpu
from jax.sharding import PartitionSpec as P

MESH = pl.DeviceIdType.MESH
F32 = jnp.float32
BF16 = jnp.bfloat16

D = 512
OUTC = 227
TILE = 128
NT = 16
NE = 32
NR = 24
K = 4
KD = 3
SLOTS = 12
DEC_EDGES = SLOTS * KD
ADJ_EDGES = NT * K
GROUP = 4
ROWS = GROUP * TILE
CORES = 2

JOBS = (
    (0, 768, ("z", "y", "x")),
    (768, 512, ("z", "x", "y")),
    (1280, 512, ("x", "y", "z")),
    (1792, 512, ("y", "z", "x")),
)
LAST, LAST_ROWS = 2304, 512
GRAD_ROWS = 2816
GRAD_F32 = 2304
HALF = D // 2
JOB_SEMS = 17


def axes_of(rows, cols):
    if (rows, cols) == (8, 16):
        return dict(zh=2, x=4, zl=2, y=4, n=4)
    return dict(zh=1, x=2, zl=2, y=2, n=2)


def dot(a, b):
    return lax.dot_general(a, b, (((1,), (0,)), ((), ())), preferred_element_type=F32)


def dot_nt(a, b):
    return lax.dot_general(a, b, (((1,), (1,)), ((), ())), preferred_element_type=F32)


def dot_tn(a, b):
    return lax.dot_general(a, b, (((0,), (0,)), ((), ())), preferred_element_type=F32)


def sigmoid(v):
    return 0.5 * jnp.tanh(0.5 * v) + 0.5


def rows_of(ref, start, count=GROUP):
    block = ref[pl.ds(start, count)]
    return block.reshape(count * TILE, block.shape[-1])


def put_rows(ref, start, value, count=GROUP):
    ref[pl.ds(start, count)] = value.reshape(count, TILE, value.shape[-1])


def outer_first(value, inner, outer):
    return jnp.where(value >= inner, value - inner, value + outer)


def sort_plan(values, blocks=None, per=1):
    count = len(values)
    depth = -(-count // 8) * 8
    down = lax.broadcasted_iota(jnp.int32, (depth, 128), 0)
    across = lax.broadcasted_iota(jnp.int32, (depth, 128), 1)
    mine = jnp.full((depth, 128), 1000, jnp.int32)
    other = jnp.full((depth, 128), 1000, jnp.int32)
    for q, value in enumerate(values):
        mine = jnp.where(down == q, value, mine)
        other = jnp.where(across == q, value, other)
    same_before = jnp.where((other == mine) & (across < down), 1, 0)
    before = jnp.where(other < mine, 1, 0) + same_before
    rank = jnp.sum(before, axis=1, keepdims=True)
    continues = jnp.minimum(jnp.sum(same_before, axis=1, keepdims=True), 1)
    hit = jnp.where((rank == across) & (down < count), 1, 0)
    order = jnp.sum(hit * down, axis=0, keepdims=True)
    follows = jnp.sum(hit * continues, axis=0, keepdims=True)
    upto = jnp.sum(jnp.where(mine <= across, 1, 0), axis=0, keepdims=True)
    present = jnp.minimum(jnp.sum(jnp.where(mine == across, 1, 0), axis=0, keepdims=True), 1)
    group = {1: down, 3: (down * 43) >> 7, 4: down >> 2}[per]
    group_row = jnp.sum(hit * group, axis=0, keepdims=True)
    named = down
    if blocks is not None:
        for q, value in enumerate(blocks):
            named = jnp.where(down == q, value, named)
    named_row = jnp.sum(hit * named, axis=0, keepdims=True)
    return order, follows, jnp.maximum(upto - 1, 0), present, group_row, named_row


def kernel(
    sizes,
    send_ref, adj_ref, dsend_ref, didx_ref, mask_ref,
    nodes_hbm, adjw_hbm, decw_hbm, target_hbm,
    wm_hbm, wu_hbm, wa_hbm, wo_hbm, wd_hbm, wh_hbm,
    lat_hbm, grads_hbm,
    nv, halo, adjw, decw, target, wm, wu, wa, wo, wd, wh,
    pref, msl, g2f, agg, hid, usl, redge, rgin, err, pool0, pool1, mbuf, pool4, acc,
    gbuf, cs, cr, r1, s2, r2, x4, rl,
    backns, plan_v, plan,
    in_sems, plan_sem, out_sem, halo_s, halo_r, edge_s, edge_r, rg_s, rg_r, hg_s, hg_r, job_s, job_r, job_l, last_s, last_r,
):
    nrow, ncol, nx, ny, nzl = sizes["rows"], sizes["cols"], sizes["x"], sizes["y"], sizes["zl"]
    nzh, n = sizes["zh"], sizes["n"]
    r = lax.axis_index("row")
    c = lax.axis_index("col")
    zh, x = lax.div(r, nx), lax.rem(r, nx)
    zl = lax.div(c, ny * CORES)
    y = lax.rem(lax.div(c, CORES), ny)
    core = lax.rem(c, CORES)
    z = zh * nzl + zl
    place = {"x": x, "y": y, "z": z}

    def peer(axis, step):
        there = lax.rem(place[axis] + step, n)
        if axis == "x":
            return (zh * nx + there, c), there
        if axis == "y":
            return (r, (zl * ny + there) * CORES + core), there
        return (lax.div(there, nzl) * nx + x, (lax.rem(there, nzl) * ny + y) * CORES + core), there

    def plane_peer(step):
        there = lax.rem(x * n + y + step, n * n)
        return (zh * nx + lax.div(there, n), (zl * ny + lax.rem(there, n)) * CORES + core), there

    mate = (r, c + 1 - 2 * core)
    west = (r, lax.rem(c + ncol - 1, ncol))
    east = (r, lax.rem(c + 1, ncol))
    north = (r - 1, c)
    south = (r + 1, c)
    has_north = r > 0
    has_south = r < nrow - 1

    loads = [
        pltpu.make_async_copy(src, dst, in_sems.at[i])
        for i, (src, dst) in enumerate(
            (
                (nodes_hbm, nv), (wm_hbm, wm), (wu_hbm, wu), (adjw_hbm, adjw), (wa_hbm, wa), (wo_hbm, wo),
                (decw_hbm, decw), (wd_hbm, wd), (wh_hbm, wh),
                *((target_hbm.at[:, pl.ds(g * TILE, TILE)], target.at[g]) for g in range(NT)),
            )
        )
    ]
    for load in loads[:3]:
        load.start()

    barrier = pltpu.get_barrier_semaphore()

    def greet(device):
        pl.semaphore_signal(barrier, inc=1, device_id=device, device_id_type=MESH)

    greet(west)
    greet(east)
    for step in range(1, n):
        greet(peer("z", step)[0])
    for step in range(1, n * n):
        greet(plane_peer(step)[0])
    greeted = 2 + (n - 1) + (n * n - 1)

    @pl.when(has_north)
    def _():
        greet(north)

    @pl.when(has_south)
    def _():
        greet(south)

    extra = jnp.where(has_north, 1, 0) + jnp.where(has_south, 1, 0)

    def send(src, dst, ssem, rsem, device):
        return pltpu.make_async_remote_copy(
            src_ref=src, dst_ref=dst, send_sem=ssem, recv_sem=rsem, device_id=device, device_id_type=MESH
        )

    loads[0].wait()
    for d in range(4):
        for b in range(4):
            pool1[d * 4 + b] = nv[send_ref[0, d, b]]
    pl.semaphore_wait(barrier, greeted + extra)

    halo_to = (south, north, east, west)
    halo_has = (has_south, has_north, None, None)
    from_has = (has_north, has_south, None, None)
    no_from = (jnp.logical_not(has_north), jnp.logical_not(has_south))

    def when(condition, body):
        if condition is None:
            body()
        else:
            pl.when(condition)(body)

    def halo_copy(d):
        part = pl.ds(d * 4, 4)
        return send(pool1.at[part], halo.at[part], halo_s.at[d], halo_r.at[d], halo_to[d])

    for d in range(4):
        when(halo_has[d], lambda d=d: halo_copy(d).start())
    for load in loads[3:]:
        load.start()

    for d in range(2):

        @pl.when(no_from[d])
        def _(d=d):
            halo[pl.ds(d * 4, 4)] = jnp.zeros((4, TILE, D), BF16)
            backns[pl.ds(4 - d * 4, 4)] = jnp.zeros((4, TILE, D), BF16)

    def messages(xs, at):
        pre = dot(xs, wm[...])
        s = sigmoid(pre)
        put_rows(pref, NE + at, (pre * s).astype(BF16))
        put_rows(msl, at, (s * (1.0 + pre * (1.0 - s))).astype(BF16))

    loads[1].wait()
    loads[2].wait()

    @pl.loop(0, NT // GROUP)
    def _(g):
        xs = rows_of(nv, g * GROUP)
        messages(xs, g * GROUP)
        put_rows(g2f, g * GROUP, dot(xs, wu[...]))

    def write_plan(at, rows):
        for i, row in enumerate(rows):
            plan_v[at + i : at + i + 1, :] = row

    write_plan(0, sort_plan([outer_first(adj_ref[0, k, t], NT, NT) for t in range(NT) for k in range(K)], per=K))
    write_plan(6, sort_plan([dsend_ref[0, d, s] for d in range(2) for s in range(4)])[:4])
    write_plan(10, sort_plan([1 - mask_ref[0, g] for g in range(NT)])[:1])
    write_plan(11, sort_plan([send_ref[0, d, b] for d in range(4) for b in range(4)])[:4])
    first = pltpu.make_async_copy(plan_v.at[pl.ds(0, 16)], plan.at[pl.ds(0, 16)], plan_sem.at[0])
    first.start()
    first.wait()
    hidden = [plan[10, s] for s in range(SLOTS)]
    edge_list = [(hidden[s], k) for s in range(SLOTS) for k in range(KD)]
    write_plan(16, sort_plan([outer_first(didx_ref[k, 0, g], NT, 8) for g, k in edge_list], [g * KD + k for g, k in edge_list], KD))
    second = pltpu.make_async_copy(plan_v.at[pl.ds(16, 8)], plan.at[pl.ds(16, 8)], plan_sem.at[1])
    second.start()
    second.wait()

    for d in (3, 2, 0, 1):
        when(from_has[d], lambda d=d: halo_copy(d).wait_recv())
        messages(rows_of(halo, d * 4), NT + d * 4)

    for i in (3, 4, 5):
        loads[i].wait()

    @pl.loop(0, NT // GROUP)
    def _(g):
        for i in range(GROUP):
            t = g * GROUP + i
            weights = jnp.concatenate([adjw[t * K + k] for k in range(K)], axis=1)
            picked = jnp.concatenate(
                [pref[NE + t], pref[NE + NT + t], pref[NE + adj_ref[0, 2, t]], pref[NE + adj_ref[0, 3, t]]], axis=0
            )
            agg[t] = dot(weights, picked).astype(BF16)
        upre = rows_of(g2f, g * GROUP) + dot(rows_of(agg, g * GROUP), wa[...])
        s = sigmoid(upre)
        hidden_rows = (upre * s).astype(BF16)
        put_rows(hid, g * GROUP, hidden_rows)
        put_rows(usl, g * GROUP, (s * (1.0 + upre * (1.0 - s))).astype(BF16))
        v2 = rows_of(nv, g * GROUP).astype(F32) + dot(hidden_rows, wo[...])
        put_rows(pref, g * GROUP, v2.astype(BF16))

    for d in range(4):
        when(halo_has[d], lambda d=d: halo_copy(d).wait_send())
    for d in range(2):
        for s in range(4):
            pref[NE + d * 4 + s] = pref[dsend_ref[0, d, s]]
    edges = [
        send(pref.at[pl.ds(NE, 4)], redge.at[pl.ds(4, 4)], edge_s.at[0], edge_r.at[0], west),
        send(pref.at[pl.ds(NE + 4, 4)], redge.at[pl.ds(0, 4)], edge_s.at[1], edge_r.at[1], east),
    ]
    for edge in edges:
        edge.start()
    for load in loads[6:]:
        load.wait()
    for edge in edges:
        edge.wait()
    for e in range(8):
        pref[NT + e] = redge[e]

    @pl.loop(0, SLOTS // GROUP)
    def _(g):
        goals, marks = [], []
        for i in range(GROUP):
            s = g * GROUP + i
            block = plan[10, s]
            weights = jnp.concatenate([decw[block * KD + k] for k in range(KD)], axis=1)
            picked = jnp.concatenate([pref[didx_ref[k, 0, block]] for k in range(KD)], axis=0)
            pool0[s] = dot(weights, picked).astype(BF16)
            goals.append(target[block].astype(F32))
            marks.append(jnp.full((1, TILE), mask_ref[0, block].astype(F32), F32))
        dpre = dot(rows_of(pool0, g * GROUP), wd[...])
        s = sigmoid(dpre)
        q = (dpre * s).astype(BF16)
        put_rows(pool1, g * GROUP, q)
        slope = s * (1.0 + dpre * (1.0 - s))
        residual = dot_nt(wh[...], q) - jnp.concatenate(goals, axis=1)
        residual = (jnp.concatenate(marks, axis=1) * residual).astype(BF16)
        err[:, pl.ds(pl.multiple_of(g * ROWS, ROWS), ROWS)] = residual
        dslope = (dot_tn(residual, wh[...]) * slope).astype(BF16)
        put_rows(mbuf, g * GROUP, dslope)
        put_rows(pool4, g * GROUP, dot_nt(dslope, wd[...]).astype(BF16))

    def spread(at, first_edge, last_edge, weight, source):
        if first_edge == 0:
            acc[...] = jnp.zeros((TILE, D), F32)

        @pl.loop(first_edge // GROUP, last_edge // GROUP)
        def _(h):
            total = acc[...]
            for i in range(GROUP):
                p = h * GROUP + i
                total = dot_tn(weight[plan[at + 5, p]], source[plan[at + 4, p]]) + plan[at + 1, p].astype(F32) * total
                pref[p] = total.astype(BF16)
            acc[...] = total

    def spread_of(at, tile):
        return plan[at + 3, tile].astype(F32) * pref[plan[at + 2, tile]].astype(F32)

    spread(16, 0, SLOTS * (KD - 1), decw, pool4)
    for e in range(8):
        pref[48 + e] = spread_of(16, e).astype(BF16)
    returns = [
        send(pref.at[pl.ds(48, 4)], rgin.at[pl.ds(4, 4)], rg_s.at[0], rg_r.at[0], west),
        send(pref.at[pl.ds(52, 4)], rgin.at[pl.ds(0, 4)], rg_s.at[1], rg_r.at[1], east),
    ]
    for item in returns:
        item.start()
    spread(16, SLOTS * (KD - 1), DEC_EDGES, decw, pool4)

    def job_copy(j, sem, src, dst, device):
        return send(src, dst, job_s.at[j, sem], job_r.at[j, sem], device)

    def c_copy(j):
        at, rows, _ = JOBS[j]
        return job_copy(j, 0, cs.at[pl.ds(at, rows)], cr.at[pl.ds(at, rows)], mate)

    def first_copies(j):
        at, rows, order = JOBS[j]
        quarter = rows // n
        out = []
        for step in range(1, n):
            device, there = peer(order[0], step)
            src = cs.at[pl.ds(pl.multiple_of(at + there * quarter, 16), quarter)]
            out.append(job_copy(j, step, src, r1.at[step - 1, pl.ds(at // n, quarter)], device))
        return out

    def second_copies(j):
        at, rows, order = JOBS[j]
        small = rows // (n * n)
        out = []
        for step in range(1, n):
            device, there = peer(order[1], step)
            src = s2.at[pl.ds(pl.multiple_of(at // n + there * small, 16), small)]
            out.append(job_copy(j, 3 + step, src, r2.at[step - 1, pl.ds(at // (n * n), small)], device))
        return out

    def third_copies(j):
        at, rows, order = JOBS[j]
        small = rows // (n * n)
        out = []
        for step in range(1, n):
            device, _ = peer(order[2], step)
            mine = x4.at[place[order[2]], pl.ds(at // (n * n), small)]
            out.append(job_copy(j, 6 + step, mine, mine, device))
        return out

    def small_at(j):
        at, rows, order = JOBS[j]
        quarter, small = rows // n, rows // (n * n)
        return pl.multiple_of(at + place[order[0]] * quarter + place[order[1]] * small, 16)

    def back_small(j):
        at, rows, order = JOBS[j]
        part = cr.at[pl.ds(small_at(j), rows // (n * n))]
        return [
            job_copy(j, 9 + step, part, part, peer(order[1], step)[0]) for step in range(1, n)
        ]

    def back_quarter(j):
        at, rows, order = JOBS[j]
        quarter = rows // n
        part = cr.at[pl.ds(pl.multiple_of(at + place[order[0]] * quarter, 16), quarter)]
        return [
            job_copy(j, 12 + step, part, part, peer(order[0], step)[0]) for step in range(1, n)
        ]

    def back_core(j):
        at, rows, _ = JOBS[j]
        part = pl.ds(at, rows)
        return (
            job_copy(j, 16, cr.at[part], grads_hbm.at[core, part], mate),
            pltpu.make_async_copy(cr.at[part], grads_hbm.at[core, part], job_l.at[j]),
        )

    def job_stage(j, stage_number):
        at, rows, order = JOBS[j]
        quarter, small = rows // n, rows // (n * n)
        whole = pl.ds(at, rows)
        own = pl.ds(at % GRAD_F32, rows)
        if stage_number == 0:
            low, high = gbuf[own, :HALF], gbuf[own, HALF:]
            cs[whole] = jnp.where(core == 0, high, low).astype(BF16)
            c_copy(j).start()
        elif stage_number == 1:
            c_copy(j).wait()
            low, high = gbuf[own, :HALF], gbuf[own, HALF:]
            cs[whole] = (jnp.where(core == 0, low, high) + cr[whole].astype(F32)).astype(BF16)
            for item in first_copies(j):
                item.start()
        elif stage_number == 2:
            mine = pl.ds(pl.multiple_of(at + place[order[0]] * quarter, 16), quarter)
            for item in first_copies(j):
                item.wait()
            total = cs[mine].astype(F32)
            for step in range(n - 1):
                total = total + r1[step, pl.ds(at // n, quarter)].astype(F32)
            s2[pl.ds(at // n, quarter)] = total.astype(BF16)
            for item in second_copies(j):
                item.start()
        elif stage_number == 3:
            mine = pl.ds(pl.multiple_of(at // n + place[order[1]] * small, 16), small)
            for item in second_copies(j):
                item.wait()
            total = s2[mine].astype(F32)
            for step in range(n - 1):
                total = total + r2[step, pl.ds(at // (n * n), small)].astype(F32)
            x4[place[order[2]], pl.ds(at // (n * n), small)] = total.astype(BF16)
            for item in third_copies(j):
                item.start()
        elif stage_number == 4:
            for item in third_copies(j):
                item.wait()
            total = x4[0, pl.ds(at // (n * n), small)].astype(F32)
            for other in range(1, n):
                total = total + x4[other, pl.ds(at // (n * n), small)].astype(F32)
            cr[pl.ds(small_at(j), small)] = (total * (1.0 / (nrow * ncol))).astype(BF16)
            for item in back_small(j):
                item.start()
        elif stage_number == 5:
            for item in back_small(j):
                item.wait()
            for item in back_quarter(j):
                item.start()
        elif stage_number == 6:
            for item in back_quarter(j):
                item.wait()
            for item in back_core(j):
                item.start()
        else:
            for item in back_core(j):
                item.wait()

    chunk = LAST_ROWS // (n * n)
    last_mine = pl.ds(pl.multiple_of(LAST + (x * n + y) * chunk, 16), chunk)
    last_place = pl.ds(LAST // (n * n), chunk)

    def last_copy(sem, src, dst, device):
        return send(src, dst, last_s.at[sem], last_r.at[sem], device)

    def last_core():
        return last_copy(0, cs.at[pl.ds(LAST, LAST_ROWS)], cr.at[pl.ds(LAST, LAST_ROWS)], mate)

    def last_scatter():
        out = []
        for step in range(1, n * n):
            device, there = plane_peer(step)
            src = cs.at[pl.ds(pl.multiple_of(LAST + there * chunk, 16), chunk)]
            out.append(last_copy(step, src, rl.at[step - 1], device))
        return out

    def last_exchange():
        mine = x4.at[z, last_place]
        return [last_copy(n * n + step, mine, mine, peer("z", step)[0]) for step in range(1, n)]

    def last_gather():
        part = cr.at[last_mine]
        return [last_copy(n * n + n + step, part, part, plane_peer(step)[0]) for step in range(1, n * n)]

    def last_back():
        part = pl.ds(LAST, LAST_ROWS)
        return (
            last_copy(n * n, cr.at[part], grads_hbm.at[core, part], mate),
            pltpu.make_async_copy(cr.at[part], grads_hbm.at[core, part], job_l.at[len(JOBS)]),
        )

    def last_stage(stage_number):
        whole = pl.ds(LAST, LAST_ROWS)
        if stage_number == 0:
            low, high = gbuf[:LAST_ROWS, :HALF], gbuf[:LAST_ROWS, HALF:]
            cs[whole] = jnp.where(core == 0, high, low).astype(BF16)
            last_core().start()
        elif stage_number == 1:
            last_core().wait()
            low, high = gbuf[:LAST_ROWS, :HALF], gbuf[:LAST_ROWS, HALF:]
            cs[whole] = (jnp.where(core == 0, low, high) + cr[whole].astype(F32)).astype(BF16)
            for item in last_scatter():
                item.start()
        elif stage_number == 2:
            for item in last_scatter():
                item.wait()
            total = cs[last_mine].astype(F32)
            for step in range(n * n - 1):
                total = total + rl[step].astype(F32)
            x4[z, last_place] = total.astype(BF16)
            for item in last_exchange():
                item.start()
        elif stage_number == 3:
            for item in last_exchange():
                item.wait()
            total = x4[0, last_place].astype(F32)
            for other in range(1, n):
                total = total + x4[other, last_place].astype(F32)
            cr[last_mine] = (total * (1.0 / (nrow * ncol))).astype(BF16)
            for item in last_gather():
                item.start()
        elif stage_number == 4:
            for item in last_gather():
                item.wait()
            for item in last_back():
                item.start()
        else:
            for item in last_back():
                item.wait()

    def gradient(at, left, right, halves=(0, 1)):
        for half in halves:
            lanes = slice(half * HALF, (half + 1) * HALF)
            total = None
            for (lref, lat, count), (rref, rat) in zip(left, right):
                lhs = lref[pl.ds(lat, count), :, lanes].reshape(count * TILE, HALF)
                term = dot_tn(lhs, rows_of(rref, rat, count))
                total = term if total is None else total + term
            gbuf[pl.ds(at % GRAD_F32 + half * HALF, HALF)] = total

    gradient(0, [(pool0, 0, SLOTS)], [(mbuf, 0)])
    q_rows = pool1[pl.ds(0, SLOTS)].reshape(SLOTS * TILE, D)
    gbuf[512:768, :] = jnp.zeros((256, D), F32)
    gbuf[512 : 512 + OUTC, :] = dot(err[...], q_rows)
    job_stage(0, 0)

    for item in returns:
        item.wait()
    total = None
    for p in range(8):
        arrived = rgin[plan[6, p]].astype(F32)
        total = arrived if total is None else arrived + plan[7, p].astype(F32) * total
        pref[40 + p] = total.astype(BF16)

    @pl.loop(0, NT)
    def _(t):
        value = spread_of(16, 8 + t).astype(BF16).astype(F32)
        value = value + plan[9, t].astype(F32) * pref[40 + plan[8, t]].astype(F32)
        g2f[t] = value
        pool4[t] = value.astype(BF16)

    job_stage(0, 1)
    gradient(768, [(hid, 0, NT)], [(pool4, 0)])
    job_stage(1, 0)

    @pl.loop(0, NT // GROUP)
    def _(g):
        back = dot_nt(rows_of(pool4, g * GROUP), wo[...]) * rows_of(usl, g * GROUP).astype(F32)
        slope = back.astype(BF16)
        put_rows(pool0, g * GROUP, slope)
        put_rows(g2f, g * GROUP, rows_of(g2f, g * GROUP) + dot_nt(slope, wu[...]))
        put_rows(pool1, g * GROUP, dot_nt(slope, wa[...]).astype(BF16))

    gradient(1280, [(nv, 0, NT)], [(pool0, 0)])
    job_stage(2, 0)
    job_stage(1, 1)
    gradient(1792, [(agg, 0, NT)], [(pool0, 0)])
    job_stage(3, 0)
    job_stage(0, 2)
    outer_edges = NT * (K - 1)
    spread(0, 0, outer_edges // 2, adjw, pool1)
    job_stage(2, 1)
    job_stage(3, 1)
    spread(0, outer_edges // 2, outer_edges, adjw, pool1)

    def message_slope(e):
        key = lax.rem(e + NT, NE)
        mbuf[e] = (spread_of(0, key) * msl[e].astype(F32)).astype(BF16)

    back_to = (north, south, west, east)
    back_has = (has_north, has_south, None, None)
    back_from = (has_south, has_north, None, None)

    def back_copy(d):
        dst = (backns.at[pl.ds(0, 4)], backns.at[pl.ds(4, 4)], redge.at[pl.ds(0, 4)], redge.at[pl.ds(4, 4)])[d]
        return send(usl.at[pl.ds(d * 4, 4)], dst, hg_s.at[d], hg_r.at[d], back_to[d])

    for d in range(4):

        @pl.loop(0, 4)
        def _(b, d=d):
            message_slope(NT + d * 4 + b)

        put_rows(usl, d * 4, dot_nt(rows_of(mbuf, NT + d * 4), wm[...]).astype(BF16))
        when(back_has[d], lambda d=d: back_copy(d).start())

    spread(0, outer_edges, ADJ_EDGES, adjw, pool1)

    @pl.loop(0, NT)
    def _(e):
        message_slope(e)

    left, right = [(nv, 0, NT), (halo, 0, NT)], [(mbuf, 0), (mbuf, NT)]
    gradient(LAST, left, right)
    last_stage(0)
    job_stage(2, 2)
    job_stage(3, 2)
    last_stage(1)
    job_stage(1, 2)
    job_stage(0, 3)

    @pl.loop(0, NT // GROUP)
    def _(g):
        put_rows(g2f, g * GROUP, rows_of(g2f, g * GROUP) + dot_nt(rows_of(mbuf, g * GROUP), wm[...]))

    job_stage(2, 3)
    job_stage(3, 3)
    last_stage(2)
    job_stage(1, 3)
    job_stage(0, 4)
    job_stage(2, 4)
    job_stage(3, 4)
    last_stage(3)
    job_stage(1, 4)
    job_stage(0, 5)
    job_stage(2, 5)
    job_stage(3, 5)
    job_stage(1, 5)
    job_stage(0, 6)
    last_stage(4)
    job_stage(2, 6)
    job_stage(3, 6)
    job_stage(1, 6)
    for d in range(4):
        when(back_from[d], lambda d=d: back_copy(d).wait_recv())
    for e in range(8):
        pref[e] = backns[e]
        pref[8 + e] = redge[e]
    total = None
    for p in range(16):
        arrived = pref[plan[11, p]].astype(F32)
        total = arrived if total is None else arrived + plan[12, p].astype(F32) * total
        pref[16 + p] = total.astype(BF16)

    @pl.loop(0, NT)
    def _(t):
        value = g2f[t] + plan[14, t].astype(F32) * pref[16 + plan[13, t]].astype(F32)
        agg[t] = value.astype(BF16)

    lat_out = pltpu.make_async_copy(agg, lat_hbm, out_sem.at[0])
    lat_out.start()
    for j in range(len(JOBS)):
        job_stage(j, 7)
    last_stage(5)
    lat_out.wait()
    for d in range(4):
        when(back_has[d], lambda d=d: back_copy(d).wait_send())


SQUARES = (2304, 1280, 1792, 768, 0)
LAT_PARTS = 4


def finish(lat_hbm, grads_hbm, latent_hbm, msg_hbm, upd_hbm, agg_hbm, out_hbm, dec_hbm, head_hbm,
           lat, grads, latent, squares, head, in_sems, out_sems):
    per = NT // LAT_PARTS
    parts = [pl.ds(i * per, per) for i in range(LAT_PARTS)]
    loads = [pltpu.make_async_copy(lat_hbm.at[part], lat.at[part], in_sems.at[i]) for i, part in enumerate(parts)]
    for i, (at, rows) in enumerate([(at, D) for at in SQUARES] + [(D, HALF)]):
        part = pl.ds(at, rows)
        loads.append(pltpu.make_async_copy(grads_hbm.at[:, part], grads.at[:, part], in_sems.at[LAT_PARTS + i]))
    for load in loads:
        load.start()
    stores = []

    def store(src, dst):
        stores.append(pltpu.make_async_copy(src, dst, out_sems.at[len(stores)]))
        stores[-1].start()

    for i, part in enumerate(parts):
        loads[i].wait()
        latent[part] = lat[part].astype(F32)
        store(latent.at[part], latent_hbm.at[part])
    for i, (at, dst) in enumerate(zip(SQUARES, (msg_hbm, upd_hbm, agg_hbm, out_hbm, dec_hbm))):
        loads[LAT_PARTS + i].wait()
        for half in range(2):
            squares[i, :, half * HALF : (half + 1) * HALF] = grads[half, at : at + D].astype(F32)
        store(squares.at[i], dst)
    loads[-1].wait()
    for half in range(2):
        head[:, half * HALF : (half + 1) * HALF] = grads[half, D : D + HALF].astype(F32)[:OUTC]
    store(head, head_hbm)
    for item in stores:
        item.wait()


def on_device(
    sizes, nodes, send_list, adj_index, adj_weight, dec_send, dec_index, dec_weight, hidden_mask, target,
    w_msg, w_update, w_aggregate, w_output, w_decode, w_head,
):
    n = sizes["n"]
    tiles = lambda count, dtype=BF16: pltpu.VMEM((count, TILE, D), dtype)
    any_spec = pl.BlockSpec(memory_space=pl.ANY)
    smem = pl.BlockSpec(memory_space=pltpu.SMEM)
    scratch = [
        tiles(NT), tiles(NT),
        pltpu.VMEM((NT * K, TILE, TILE), BF16), pltpu.VMEM((NT * KD, TILE, TILE), BF16),
        pltpu.VMEM((NT, OUTC, TILE), BF16),
        *[pltpu.VMEM((D, D), BF16)] * 5, pltpu.VMEM((OUTC, D), BF16),
        tiles(2 * NE), tiles(NE), tiles(NT, F32),
        tiles(NT), tiles(NT), tiles(NT),
        tiles(8), tiles(8), pltpu.VMEM((OUTC, SLOTS * TILE), BF16),
        tiles(NT), tiles(NT), tiles(NE), tiles(NT),
        pltpu.VMEM((TILE, D), F32),
        pltpu.VMEM((GRAD_F32, D), F32),
        pltpu.VMEM((GRAD_ROWS, HALF), BF16), pltpu.VMEM((GRAD_ROWS, HALF), BF16),
        pltpu.VMEM((n - 1, LAST // n, HALF), BF16), pltpu.VMEM((LAST // n, HALF), BF16),
        pltpu.VMEM((n - 1, LAST // n**2, HALF), BF16), pltpu.VMEM((n, GRAD_ROWS // n**2, HALF), BF16),
        pltpu.VMEM((n * n - 1, LAST_ROWS // n**2, HALF), BF16),
        tiles(8),
        pltpu.VMEM((24, 128), jnp.int32), pltpu.SMEM((24, 128), jnp.int32),
        pltpu.SemaphoreType.DMA((9 + NT,)), pltpu.SemaphoreType.DMA((2,)), pltpu.SemaphoreType.DMA((1,)),
        *[pltpu.SemaphoreType.DMA((4,))] * 2,
        *[pltpu.SemaphoreType.DMA((2,))] * 4,
        *[pltpu.SemaphoreType.DMA((4,))] * 2,
        *[pltpu.SemaphoreType.DMA((len(JOBS), JOB_SEMS))] * 2,
        pltpu.SemaphoreType.DMA((len(JOBS) + 1,)),
        *[pltpu.SemaphoreType.DMA((2 * n * n + n,))] * 2,
    ]
    lat, grads = pl.pallas_call(
        functools.partial(kernel, sizes),
        out_shape=(
            jax.ShapeDtypeStruct((NT, TILE, D), BF16),
            jax.ShapeDtypeStruct((CORES, GRAD_ROWS, HALF), BF16),
        ),
        in_specs=[smem] * 5 + [any_spec] * 10,
        out_specs=(any_spec,) * 2,
        scratch_shapes=scratch,
        compiler_params=pltpu.CompilerParams(
            collective_id=0, has_side_effects=True, vmem_limit_bytes=62 * 1024 * 1024
        ),
        name="mesh_step",
    )(
        send_list, adj_index.transpose(0, 2, 1), dec_send, dec_index.transpose(2, 0, 1), hidden_mask,
        nodes.reshape(NT, TILE, D),
        adj_weight.reshape(NT * K, TILE, TILE),
        dec_weight.reshape(NT * KD, TILE, TILE),
        target.T,
        w_msg, w_update, w_aggregate, w_output, w_decode, w_head.T,
    )
    f32 = lambda *shape: jax.ShapeDtypeStruct(shape, F32)
    outs = pl.pallas_call(
        finish,
        out_shape=(f32(NT, TILE, D), *[f32(D, D)] * 5, f32(OUTC, D)),
        in_specs=[any_spec] * 2,
        out_specs=(any_spec,) * 7,
        scratch_shapes=[
            tiles(NT), pltpu.VMEM((CORES, GRAD_ROWS, HALF), BF16),
            tiles(NT, F32), pltpu.VMEM((5, D, D), F32), pltpu.VMEM((OUTC, D), F32),
            pltpu.SemaphoreType.DMA((LAT_PARTS + 6,)), pltpu.SemaphoreType.DMA((LAT_PARTS + 6,)),
        ],
        compiler_params=pltpu.CompilerParams(vmem_limit_bytes=60 * 1024 * 1024),
        name="finish",
    )(lat, grads)
    latent, msg, upd, agg, out, dec, head = outs
    return latent.reshape(NT * TILE, D), msg, upd, agg, out, dec, head.T


def solution(mesh):
    rows, cols = mesh.shape["row"], mesh.shape["col"]
    sizes = dict(axes_of(rows, cols), rows=rows, cols=cols)
    both = ("row", "col")
    return jax.shard_map(
        functools.partial(on_device, sizes),
        mesh=mesh,
        in_specs=(
            P(both, None),
            P(both, None, None),
            P(both, None, None),
            P(both, None, None, None),
            P(both, None, None),
            P(both, None, None),
            P(both, None, None, None),
            P(both, None),
            P(both, None),
            *[P()] * 6,
        ),
        out_specs=(P(both, None), *[P()] * 6),
        check_vma=False,
    )
```
